32 devices in a mesh: segment: 2 (over y), slot: 16 (over z, x, core).
Axes of the slice: x: 2, y: 2, z: 4, core: 2. Of those that a mesh axis runs over, the one named last changes fastest.
Arguments:
- hidden_rows: bfloat16 [2, 4, 16, 8192], P('segment', None, None, 'slot'), may hold values from -6 to 6
- norm_gain: bfloat16 [2, 8192], P('segment', 'slot'), may hold values from 0.099609375 to 1.8984375
- qkv_weight: bfloat16 [2, 8192, 5120], P('segment', None, 'slot'), may hold values from -0.0625 to 0.0625
- out_weight: bfloat16 [2, 4096, 8192], P('segment', None, 'slot'), may hold values from -0.5 to 0.5
- cache_kv: bfloat16 [2, 2, 4, 16, 16, 1024], P('segment', None, None, 'slot'), may hold values from -86 to 86
- cache_len: int32 [2, 2, 4, 16], P('segment', None, None, 'slot'), may hold values from 1 to 16, as said below
- page_kv: bfloat16 [2, 16, 16, 8, 1024], P('segment', 'slot'), may hold values from -6 to 6
- page_dest: int32 [2, 16, 16], P('segment'), may hold values from 0 to 15, as said below
- page_row: int32 [2, 16, 16], P('segment'), may hold values from 0 to 7
- page_count: int32 [2, 16, 16], P('segment'), may hold values from 1 to 8, as said below
Outputs:
- final_rows: bfloat16 [2, 4, 16, 8192], P('segment', None, None, 'slot')
The draws below stay inside these ranges and needn't reach their ends.
Inputs may be any that keep to these rules, and one draw needn't show every extreme that they name: `cache_len`: positions of a row's cache from its length on are not part of it. `page_dest`: the 16 pages of one source device go to distinct slot indices, so every slot index receives one page from every source. `page_count`: tokens of a page from its count on are not part of it.
All inputs are finite; a program needn't handle non-finite values.
Results may differ from the reference program's by a relative error of at most 0.015.
Values may be sent and summed in bfloat16 or wider, within the bound.
No kernel may reach another device: no remote copies, remote signals or barrier semaphores. Data moves between devices by JAX's collectives and lax.ppermute only.
A program may use at most 64 MiB of HBM per device.

```python
import jax
import jax.numpy as jnp
from jax import lax

D = 8192
QUERY_HEADS = 32
KEY_VALUE_HEADS = 4
HEAD_SIZE = 128
CYCLE_STEPS = 2
SLOT_ROWS = 4
CACHE_POSITIONS = 16
PAGE_TOK = 8
QKV = 5120
KVW = 1024
PAGES = 16
N_SEGMENT = 2
N_SLOT = 16


def draw_cache_kv(key, part):
    complete_shape = (N_SEGMENT, CYCLE_STEPS, SLOT_ROWS, N_SLOT, CACHE_POSITIONS, 2 * KEY_VALUE_HEADS * HEAD_SIZE)
    values = jnp.clip(jax.random.normal(key, complete_shape, jnp.float32), -6.0, 6.0)
    return values.astype(jnp.bfloat16)


def draw_cache_len(key, part):
    key_vals, key_spot = jax.random.split(jax.random.fold_in(key, 11))
    complete_shape = (N_SEGMENT, CYCLE_STEPS, SLOT_ROWS, N_SLOT)
    values = jax.random.randint(key_vals, complete_shape, 1, CACHE_POSITIONS + 1, dtype=jnp.int32)
    flattened = values.reshape(-1)
    spot = jax.random.randint(key_spot, (), 0, flattened.shape[0], dtype=jnp.int32)
    flattened = flattened.at[spot].set(CACHE_POSITIONS)
    return flattened.reshape(complete_shape)


def draw_page_dest(key, part):
    key_common, key_perm, key_shuffle = jax.random.split(jax.random.fold_in(key, 23), 3)
    common_dest = jax.random.randint(key_common, (N_SEGMENT,), 0, N_SLOT, dtype=jnp.int32)
    perm_keys = jax.random.split(key_perm, N_SEGMENT * N_SLOT)
    orders = jax.vmap(lambda single: jax.random.permutation(single, N_SLOT))(perm_keys).astype(jnp.int32)
    orders = orders.reshape(N_SEGMENT, N_SLOT, N_SLOT)
    common_b = common_dest[:, None, None]
    where_common = jnp.argmax(orders == common_b, axis=2).astype(jnp.int32)
    leading = orders[..., 0]
    positions = jnp.arange(N_SLOT, dtype=jnp.int32)
    orders = jnp.where(positions[None, None, :] == where_common[..., None], leading[..., None], orders)
    orders = jnp.where(positions[None, None, :] == 0, common_b, orders)
    selected = orders[..., :PAGES]
    shuffle_keys = jax.random.split(key_shuffle, N_SEGMENT * N_SLOT)
    shuffle = jax.vmap(lambda single: jax.random.permutation(single, PAGES))(shuffle_keys).astype(jnp.int32)
    shuffle = shuffle.reshape(N_SEGMENT, N_SLOT, PAGES)
    return jnp.take_along_axis(selected, shuffle, axis=2).astype(jnp.int32)


def draw_page_count(key, part):
    key_vals, key_spot = jax.random.split(jax.random.fold_in(key, 37))
    complete_shape = (N_SEGMENT, N_SLOT, PAGES)
    values = jax.random.randint(key_vals, complete_shape, 1, PAGE_TOK + 1, dtype=jnp.int32)
    flattened = values.reshape(-1)
    spot = jax.random.randint(key_spot, (), 0, flattened.shape[0], dtype=jnp.int32)
    flattened = flattened.at[spot].set(PAGE_TOK)
    return flattened.reshape(complete_shape)


def touch_ends(result, key, least, top_value):
    shape = result.shape
    index_at = [jax.random.randint(jax.random.fold_in(key, axis), (), 0, shape[axis]) for axis in range(len(shape))]
    result = result.at[tuple(index_at)].set(least)
    longest = shape.index(max(shape))
    index_at[longest] = (index_at[longest] + 1) % shape[longest]
    return result.at[tuple(index_at)].set(top_value)


def block_levels(stream_key, dims, pieces, low, high):
    def one(axis_at, blocks):
        draws = jax.random.uniform(jax.random.fold_in(jax.random.fold_in(stream_key, 6), axis_at), (blocks,), jnp.float32, low / len(pieces), high / len(pieces))
        return jnp.repeat(jnp.exp(draws), dims[axis_at] // blocks).reshape((-1,) + (1,) * (len(dims) - axis_at - 1))

    gain = one(*pieces[0])
    for cut in pieces[1:]:
        gain = gain * one(*cut)
    return gain


def gaussian(rng, dims, deviation, bound, cuts=(), kind=jnp.bfloat16):
    values = deviation * jax.random.normal(rng, dims, jnp.float32)
    if cuts:
        values = values * block_levels(rng, dims, cuts, -0.22, 0.18)
    return jnp.clip(values, -bound, bound).astype(kind)


def setup_inputs(seed: int = 0) -> dict:
    streams_of = jax.random.split(jax.random.key(seed), 11)
    return {
        "hidden_rows": gaussian(streams_of[0], (N_SEGMENT, SLOT_ROWS, N_SLOT, D), 1.0, 6.0, ((0, 2), (3, 16))),
        "norm_gain": jnp.clip(1.0 + 0.18 * jax.random.normal(streams_of[1], (N_SEGMENT, D), jnp.float32), 0.099609375, 1.8984375).astype(jnp.bfloat16),
        "qkv_weight": gaussian(streams_of[2], (N_SEGMENT, D, QKV), D ** -0.5, 0.0625, ((0, 2), (2, 16))),
        "out_weight": gaussian(streams_of[3], (N_SEGMENT, QUERY_HEADS * HEAD_SIZE, D), HEAD_SIZE ** -0.5, 0.5, ((0, 2), (2, 16))),
        "cache_kv": draw_cache_kv(jax.random.fold_in(streams_of[10], 71), 0),
        "cache_len": draw_cache_len(jax.random.fold_in(streams_of[10], 71), 0),
        "page_kv": gaussian(streams_of[6], (N_SEGMENT, N_SLOT, PAGES, PAGE_TOK, KVW), 1.0, 6.0, ((0, 2), (1, 16))),
        "page_dest": draw_page_dest(jax.random.fold_in(streams_of[10], 71), 0),
        "page_row": touch_ends(jax.random.randint(streams_of[8], (N_SEGMENT, N_SLOT, PAGES), 0, CYCLE_STEPS * SLOT_ROWS), jax.random.fold_in(streams_of[8], 1), 0, (CYCLE_STEPS * SLOT_ROWS) - 1).astype(jnp.int32),
        "page_count": draw_page_count(jax.random.fold_in(streams_of[10], 71), 0),
    }


norm_eps = 1e-06

def segment_layer(visit_idx, current, gain_row, weight_in, weight_out, cache_now, length_now, page_vals, dest_now, row_now, count_now):
    width_of_keys = KEY_VALUE_HEADS * HEAD_SIZE
    query_group_width = QUERY_HEADS // KEY_VALUE_HEADS
    score_scale = HEAD_SIZE ** (-0.5)
    total_page_keys = N_SLOT * PAGE_TOK
    as_float = current.astype(jnp.float32)
    square_sum = lax.optimization_barrier(jnp.sum(as_float * as_float, axis=2))
    scaled = (as_float * gain_row.astype(jnp.float32)).astype(jnp.bfloat16)
    projected = jnp.dot(scaled.reshape(SLOT_ROWS * N_SLOT, D), weight_in, preferred_element_type=jnp.float32).reshape(SLOT_ROWS, N_SLOT, QKV)
    query_key_value_rows = (projected * lax.rsqrt(square_sum / D + norm_eps)[..., None]).astype(jnp.bfloat16).astype(jnp.float32)
    query_rows = query_key_value_rows[..., :QUERY_HEADS * HEAD_SIZE].reshape(SLOT_ROWS, N_SLOT, KEY_VALUE_HEADS, query_group_width, HEAD_SIZE)
    fresh_key = query_key_value_rows[..., QUERY_HEADS * HEAD_SIZE:QUERY_HEADS * HEAD_SIZE + width_of_keys].reshape(SLOT_ROWS, N_SLOT, KEY_VALUE_HEADS, HEAD_SIZE)
    fresh_value = query_key_value_rows[..., QUERY_HEADS * HEAD_SIZE + width_of_keys:].reshape(SLOT_ROWS, N_SLOT, KEY_VALUE_HEADS, HEAD_SIZE)
    slot_ids = jnp.arange(N_SLOT, dtype=jnp.int32)
    arriving = dest_now[None, :, :] == slot_ids[:, None, None]
    chosen = arriving.astype(jnp.float32)
    flat_pages = page_vals.reshape(N_SLOT, PAGES, PAGE_TOK * KVW).astype(jnp.float32)
    received_state = jnp.einsum('djp,jpk->djk', chosen, flat_pages, precision=lax.Precision.HIGHEST)
    received_state = received_state.reshape(N_SLOT, total_page_keys, KVW)
    present = jnp.any(arriving, axis=2)
    owner_row = lax.optimization_barrier(jnp.sum(jnp.where(arriving, row_now[None, :, :], 0), axis=2))
    live_count = lax.optimization_barrier(jnp.sum(jnp.where(arriving, count_now[None, :, :], 0), axis=2))
    token_ids = jnp.arange(PAGE_TOK, dtype=jnp.int32)
    page_live = present[:, :, None] & (token_ids[None, None, :] < live_count[:, :, None])
    row_ids = visit_idx * SLOT_ROWS + jnp.arange(SLOT_ROWS, dtype=jnp.int32)
    visible_pages = page_live[None] & (owner_row[None, :, :, None] == row_ids[:, None, None, None])
    visible_pages = visible_pages.reshape(SLOT_ROWS, N_SLOT, total_page_keys)
    cache_as_real = cache_now.astype(jnp.float32)
    resident_key_rows = cache_as_real[..., :width_of_keys].reshape(SLOT_ROWS, N_SLOT, CACHE_POSITIONS, KEY_VALUE_HEADS, HEAD_SIZE)
    resident_value_rows = cache_as_real[..., width_of_keys:].reshape(SLOT_ROWS, N_SLOT, CACHE_POSITIONS, KEY_VALUE_HEADS, HEAD_SIZE)
    cropped_page_keys = received_state[..., :width_of_keys].reshape(N_SLOT, total_page_keys, KEY_VALUE_HEADS, HEAD_SIZE)
    cropped_page_values = received_state[..., width_of_keys:].reshape(N_SLOT, total_page_keys, KEY_VALUE_HEADS, HEAD_SIZE)
    score_cache = jnp.einsum('bdhgx,bdchx->bdhgc', query_rows, resident_key_rows)
    score_pages = jnp.einsum('bdhgx,dphx->bdhgp', query_rows, cropped_page_keys)
    score_self = jnp.einsum('bdhgx,bdhx->bdhg', query_rows, fresh_key)[..., None]
    scores = jnp.concatenate([score_cache, score_pages, score_self], axis=-1) * score_scale
    cache_ids = jnp.arange(CACHE_POSITIONS, dtype=jnp.int32)
    visible_cache = cache_ids[None, None, :] < length_now[:, :, None]
    visible = jnp.concatenate([visible_cache, visible_pages, jnp.ones((SLOT_ROWS, N_SLOT, 1), dtype=bool)], axis=-1)
    scores = jnp.where(visible[:, :, None, None, :], scores, -1e+30)
    row_max = lax.optimization_barrier(jnp.max(scores, axis=-1, keepdims=True))
    expd = jnp.exp(scores - row_max)
    denominator = lax.optimization_barrier(jnp.sum(expd, axis=-1, keepdims=True))
    weights = (expd / denominator).astype(jnp.bfloat16).astype(jnp.float32)
    context = jnp.einsum('bdhgc,bdchx->bdhgx', weights[..., :CACHE_POSITIONS], resident_value_rows)
    context = context + jnp.einsum('bdhgp,dphx->bdhgx', weights[..., CACHE_POSITIONS:CACHE_POSITIONS + total_page_keys], cropped_page_values)
    context = context + weights[..., -1:] * fresh_value[:, :, :, None, :]
    context = context.astype(jnp.bfloat16).reshape(SLOT_ROWS * N_SLOT, QUERY_HEADS * HEAD_SIZE)
    output = jnp.dot(context, weight_out, preferred_element_type=jnp.float32).reshape(SLOT_ROWS, N_SLOT, D)
    return (as_float + output).astype(jnp.bfloat16)

def reference(hidden_rows, norm_gain, qkv_weight, out_weight, cache_kv, cache_len, page_kv, page_dest, page_row, page_count):
    current = hidden_rows
    for visit_idx in range(CYCLE_STEPS):

        def run_segment(stacked, visit_idx=visit_idx):
            return segment_layer(visit_idx, *stacked)
        updated = lax.map(run_segment, (current, norm_gain, qkv_weight, out_weight, cache_kv[:, visit_idx], cache_len[:, visit_idx], page_kv, page_dest, page_row, page_count))
        current = jnp.roll(updated, 1, axis=0)
    return current
```

```python
import functools

import jax
import jax.numpy as jnp
import numpy as np
from jax import lax
from jax.experimental import pallas as pl
from jax.experimental.pallas import tpu as pltpu
from jax.sharding import PartitionSpec as P

QUERY_HEADS = 32
KEY_VALUE_HEADS = 4
HEAD_SIZE = 128
CYCLE_STEPS = 2
GROUP = QUERY_HEADS // KEY_VALUE_HEADS
KEY_WIDTH = KEY_VALUE_HEADS * HEAD_SIZE
LANES = 128

norm_eps = 1e-06
VMEM_LIMIT = 24 * 1024 * 1024


def params(**kw):
    return pltpu.CompilerParams(vmem_limit_bytes=VMEM_LIMIT, **kw)


def iota(shape, dim):
    return lax.broadcasted_iota(jnp.int32, shape, dim)


def exchange(block, mask):
    n = lax.axis_size("slot")
    return lax.ppermute(block, "slot", [(i, i ^ mask) for i in range(n)])


def next_segment(block):
    n = lax.axis_size("segment")
    return lax.ppermute(block, "segment", [(i, (i + 1) % n) for i in range(n)])


def row_order(slots, batch, inverse):
    rows = slots * batch
    out, src = iota((rows, rows), 0), iota((rows, rows), 1)
    if inverse:
        want = lax.rem(out, slots) * batch + out // slots
    else:
        want = lax.rem(out, batch) * slots + out // batch
    return (src == want).astype(jnp.bfloat16)


def prep_kernel(own_ref, dest_sm, x_ref, gain_ref, pages_ref, dest_ref, row_ref, count_ref,
                x_out, scaled_out, send_ref, code_ref, *, slots, batch):
    rows, width = x_ref.shape
    order = row_order(slots, batch, False)
    x = jnp.dot(order, x_ref[...], preferred_element_type=jnp.float32)
    x_out[...] = x.astype(jnp.bfloat16)
    gain = gain_ref[...].astype(jnp.float32)
    scaled_out[0] = (x * gain).astype(jnp.bfloat16)
    column = jnp.sum(x * x, axis=1, keepdims=True)
    extra = jnp.zeros((8, LANES), jnp.float32)
    at = iota((8, LANES), 0)
    gain_rows = width // LANES
    for r in range(gain_rows):
        extra = jnp.where(at == r, gain[:, r * LANES:(r + 1) * LANES], extra)
    spans = -(-rows // LANES)
    ident_row, ident_lane = iota((rows, LANES), 0), iota((rows, LANES), 1)
    for r in range(spans):
        line = jnp.sum(jnp.where(ident_row == ident_lane + r * LANES, column, 0.0), axis=0,
                       keepdims=True)
        for part in range(3):
            piece = line.astype(jnp.bfloat16).astype(jnp.float32)
            extra = jnp.where(at == gain_rows + 3 * r + part, piece, extra)
            line = line - piece
    extra = extra.astype(jnp.bfloat16)
    kv_width = pages_ref.shape[2]
    own = own_ref[0]
    for p in range(pages_ref.shape[0]):
        send_ref[dest_sm[own, p], :, :kv_width] = pages_ref[p]
    for j in range(slots):
        send_ref[j, :, kv_width:] = extra
    tokens = code_ref.shape[1]
    page_tok = tokens // slots
    mine = dest_ref[...] == own
    spread = (iota((slots, tokens), 1) // page_tok == iota((slots, tokens), 0)).astype(jnp.float32)

    def to_tokens(values):
        kept = jnp.where(mine, values, 0).astype(jnp.float32)
        wide = lax.dot_general(kept, spread, (((0,), (0,)), ((), ())),
                               preferred_element_type=jnp.float32)
        return jnp.sum(wide, axis=0, keepdims=True)

    place = lax.rem(iota((1, tokens), 1), page_tok).astype(jnp.float32)
    live = place < to_tokens(count_ref[...])
    code = jnp.where(live, to_tokens(row_ref[...]), -1.0)
    code_ref[...] = jnp.broadcast_to(code, code_ref.shape).astype(jnp.int32)


def prepare(own, x, gain, pages, dest, row, count):
    batch, slots, width = x.shape
    rows = batch * slots
    total, page_tok, kv_width = pages.shape
    whole = pl.BlockSpec(memory_space=pltpu.VMEM)
    scalar = pl.BlockSpec(memory_space=pltpu.SMEM)
    return pl.pallas_call(
        functools.partial(prep_kernel, slots=slots, batch=batch),
        out_shape=[
            jax.ShapeDtypeStruct((rows, width), jnp.bfloat16),
            jax.ShapeDtypeStruct((1, rows, width), jnp.bfloat16),
            jax.ShapeDtypeStruct((slots, page_tok, kv_width + LANES), jnp.bfloat16),
            jax.ShapeDtypeStruct((8, slots * page_tok), jnp.int32),
        ],
        in_specs=[scalar, scalar] + [whole] * 6,
        out_specs=[whole] * 4,
        compiler_params=params(),
        name="prepare",
    )(own, dest, x.reshape(rows, width), gain, pages, dest, row, count)


def project_kernel(*refs, first, last, scale, rows_sum, slots, batch, model_width):
    order_ref, x_ref, w_ref = refs[:3]
    refs = list(refs[3:])
    extra_ref = refs.pop(0) if (scale or (last and not scale)) else None
    acc_in = None if first else refs.pop(0)
    sum_in = None if first or not scale else refs.pop(0)
    if last:
        out_ref = refs.pop(0)
        acc = refs.pop(0)
        square = refs.pop(0) if scale else None
    else:
        acc = refs.pop(0)
        square = refs.pop(0) if scale else None
    step = pl.program_id(0)

    @pl.when(step == 0)
    def _():
        acc[...] = jnp.zeros_like(acc) if first else acc_in[...]
        if scale:
            square[...] = jnp.zeros_like(square) if first else sum_in[...]

    x = x_ref[0]
    rows, width = x.shape
    if scale:
        parts = []
        total = square[...]
        for r in range(width // LANES):
            part = x[:, r * LANES:(r + 1) * LANES].astype(jnp.float32)
            total = total + part * part
            parts.append((part * extra_ref[0, r:r + 1, :].astype(jnp.float32)).astype(jnp.bfloat16))
        square[...] = total
        x = parts[0] if len(parts) == 1 else jnp.concatenate(parts, axis=1)
    acc[...] += jnp.dot(x, w_ref[...], preferred_element_type=jnp.float32)

    if last:
        @pl.when(step == pl.num_programs(0) - 1)
        def _():
            if scale:
                sums = jnp.sum(square[...], axis=1, keepdims=True)
            else:
                gain_rows = width // LANES
                lines = jnp.sum(extra_ref[...].astype(jnp.float32), axis=0)
                sums = jnp.zeros((rows, 1), jnp.float32)
                ident_row, ident_lane = iota((rows, LANES), 0), iota((rows, LANES), 1)
                for r in range(-(-rows // LANES)):
                    at = gain_rows + 3 * r
                    line = lines[at:at + 1] + lines[at + 1:at + 2] + lines[at + 2:at + 3]
                    sums = sums + jnp.sum(
                        jnp.where(ident_row == ident_lane + r * LANES, line, 0.0), axis=1,
                        keepdims=True)
            out = acc[...] * lax.rsqrt(sums / model_width + norm_eps)
            for j in range(slots):
                out_ref[j] = out[j * batch:(j + 1) * batch].astype(jnp.bfloat16)


def project(order, start, x, weight, extra, state, *, scale, last, slots, batch, kv_width):
    blocks, rows, width = x.shape
    columns = weight.shape[1]
    first = state is None
    page_tok = extra.shape[1]
    in_specs = [
        pl.BlockSpec((1, rows, width), lambda s, order: (s, 0, 0)),
        pl.BlockSpec((width, columns), lambda s, order: (order[start + s], 0)),
    ]
    operands = [x, weight]
    if scale:
        in_specs.append(pl.BlockSpec((1, page_tok, LANES),
                                     lambda s, order: (order[start + s], 0, kv_width // LANES)))
        operands.append(extra)
    elif last:
        in_specs.append(pl.BlockSpec((slots, page_tok, LANES),
                                     lambda s, order: (0, 0, kv_width // LANES)))
        operands.append(extra)
    acc_shape = jax.ShapeDtypeStruct((rows, columns), jnp.float32)
    sum_shape = jax.ShapeDtypeStruct((rows, LANES), jnp.float32)
    fixed = lambda shape: pl.BlockSpec(shape, lambda s, order: (0,) * len(shape))
    if not first:
        for value in state:
            in_specs.append(fixed(value.shape))
            operands.append(value)
    scratch = []
    if last:
        out_shape = jax.ShapeDtypeStruct((slots, batch, columns), jnp.bfloat16)
        out_specs = fixed(out_shape.shape)
        scratch = [pltpu.VMEM((rows, columns), jnp.float32)]
        if scale:
            scratch.append(pltpu.VMEM((rows, LANES), jnp.float32))
    else:
        out_shape = [acc_shape] + ([sum_shape] if scale else [])
        out_specs = [fixed(s.shape) for s in out_shape]
    return pl.pallas_call(
        functools.partial(project_kernel, first=first, last=last, scale=scale, rows_sum=None,
                          slots=slots, batch=batch, model_width=weight.shape[0]),
        out_shape=out_shape,
        grid_spec=pltpu.PrefetchScalarGridSpec(
            num_scalar_prefetch=1, grid=(blocks,), in_specs=in_specs, out_specs=out_specs,
            scratch_shapes=scratch),
        compiler_params=params(),
        cost_estimate=pl.CostEstimate(flops=8 * rows * width * columns * blocks,
                                      bytes_accessed=2 * width * columns * blocks,
                                      transcendentals=0),
        name="project",
    )(order, *operands)


def attend_kernel(len_ref, qkv_ref, cache_ref, pages_ref, code_ref, out_ref, *, visit):
    slots, batch, columns = qkv_ref.shape
    positions = cache_ref.shape[2]
    tokens = pages_ref.shape[0]
    full = jnp.concatenate([qkv_ref[j].astype(jnp.float32) for j in range(slots)], axis=1)
    group_rows = GROUP * batch
    near = batch * positions
    near_pad = -(-(near + 16) // LANES) * LANES
    rows = KEY_VALUE_HEADS * group_rows
    nt = (((1,), (1,)), ((), ()))
    far_scores, near_scores, near_values = [], [], []
    key_at = QUERY_HEADS * HEAD_SIZE
    value_at = key_at + KEY_WIDTH
    for h in range(KEY_VALUE_HEADS):
        query = jnp.concatenate(
            [full[:, (h * GROUP + g) * HEAD_SIZE:(h * GROUP + g + 1) * HEAD_SIZE]
             for g in range(GROUP)], axis=0).astype(jnp.bfloat16)
        lo, hi = h * HEAD_SIZE, (h + 1) * HEAD_SIZE

        def nearby(cache_lo, fresh_lo):
            fresh = full[:, fresh_lo:fresh_lo + HEAD_SIZE]
            fresh = jnp.concatenate(
                [fresh, jnp.zeros((near_pad - near - batch, HEAD_SIZE), jnp.float32)], axis=0)
            old = [cache_ref[0, b, :, cache_lo:cache_lo + HEAD_SIZE] for b in range(batch)]
            return jnp.concatenate(old + [fresh.astype(jnp.bfloat16)], axis=0)

        keys = nearby(lo, key_at + lo)
        near_values.append(nearby(KEY_WIDTH + lo, value_at + lo))
        far_scores.append(lax.dot_general(query, pages_ref[:, lo:hi], nt,
                                          preferred_element_type=jnp.float32))
        near_scores.append(lax.dot_general(query, keys, nt, preferred_element_type=jnp.float32))
    scale = HEAD_SIZE ** (-0.5)
    far = jnp.concatenate(far_scores, axis=0) * scale
    close = jnp.concatenate(near_scores, axis=0) * scale
    far_row = lax.rem(iota((rows, tokens), 0), batch)
    far = jnp.where(code_ref[0:1, :] == far_row + visit * batch, far, -1e30)
    row = lax.rem(iota((rows, near_pad), 0), batch)
    lane = iota((rows, near_pad), 1)
    lengths = jnp.zeros((rows, near_pad), jnp.int32)
    for b in range(batch):
        lengths = jnp.where(row == b, len_ref[visit, b], lengths)
    position = lane - row * positions
    seen = (position >= 0) & (position < lengths) | (lane == near + row)
    close = jnp.where(seen, close, -1e30)
    top = jnp.maximum(jnp.max(far, axis=1, keepdims=True), jnp.max(close, axis=1, keepdims=True))
    far = jnp.exp(far - top)
    close = jnp.exp(close - top)
    denominator = jnp.sum(far, axis=1, keepdims=True) + jnp.sum(close, axis=1, keepdims=True)
    far = (far / denominator).astype(jnp.bfloat16)
    close = (close / denominator).astype(jnp.bfloat16)
    for h in range(KEY_VALUE_HEADS):
        mine = slice(h * group_rows, (h + 1) * group_rows)
        lo = KEY_WIDTH + h * HEAD_SIZE
        context = jnp.dot(far[mine], pages_ref[:, lo:lo + HEAD_SIZE],
                          preferred_element_type=jnp.float32)
        context = context + jnp.dot(close[mine], near_values[h],
                                    preferred_element_type=jnp.float32)
        for g in range(GROUP):
            at = (h * GROUP + g) * HEAD_SIZE
            out_ref[0, :, at:at + HEAD_SIZE] = context[g * batch:(g + 1) * batch].astype(
                jnp.bfloat16)


def attend(lengths, qkv, cache, pages, code, visit):
    slots, batch, columns = qkv.shape
    _, _, positions, kv_width = cache.shape
    tokens = pages.shape[0]
    return pl.pallas_call(
        functools.partial(attend_kernel, visit=visit),
        out_shape=jax.ShapeDtypeStruct((1, batch, QUERY_HEADS * HEAD_SIZE), jnp.bfloat16),
        grid=(1,),
        in_specs=[
            pl.BlockSpec(memory_space=pltpu.SMEM),
            pl.BlockSpec((slots, batch, columns), lambda s: (0, 0, 0)),
            pl.BlockSpec((1, batch, positions, kv_width), lambda s: (visit, 0, 0, 0)),
            pl.BlockSpec((tokens, kv_width), lambda s: (0, 0)),
            pl.BlockSpec(code.shape, lambda s: (0, 0)),
        ],
        out_specs=pl.BlockSpec((1, batch, QUERY_HEADS * HEAD_SIZE), lambda s: (0, 0, 0)),
        compiler_params=params(),
        name="attend",
    )(lengths, qkv, cache, pages, code)


def output_kernel(place_ref, near_ref, far_ref, w_ref, now_ref, out_ref, left, acc, *, slots,
                  batch, final):
    step = pl.program_id(0)
    depth = w_ref.shape[0]
    half = near_ref.shape[0]

    @pl.when(step == 0)
    def _():
        acc[...] = jnp.zeros_like(acc)
        for j in range(slots):
            place = place_ref[j]
            spot = lax.rem(place, half)
            held = jnp.where(place < half, near_ref[spot], far_ref[spot])
            held = held.astype(jnp.float32)
            for k in range(left.shape[0]):
                left[k, j * batch:(j + 1) * batch, :] = held[:, k * depth:(k + 1) * depth]

    acc[...] += jnp.dot(left[step].astype(jnp.bfloat16), w_ref[...],
                        preferred_element_type=jnp.float32)

    @pl.when(step == pl.num_programs(0) - 1)
    def _():
        updated = (now_ref[...].astype(jnp.float32) + acc[...]).astype(jnp.bfloat16)
        if final:
            back = row_order(slots, batch, True)
            updated = jnp.dot(back, updated, preferred_element_type=jnp.float32).astype(
                jnp.bfloat16)
        out_ref[...] = updated


def output(place, near, far, weight, now, final):
    half, batch, features = near.shape
    slots = 2 * half
    rows, columns = now.shape
    steps = 4
    depth = features // steps
    fixed = lambda *shape: pl.BlockSpec(shape, lambda s, place: (0,) * len(shape))
    return pl.pallas_call(
        functools.partial(output_kernel, slots=slots, batch=batch, final=final),
        out_shape=jax.ShapeDtypeStruct((rows, columns), jnp.bfloat16),
        grid_spec=pltpu.PrefetchScalarGridSpec(
            num_scalar_prefetch=1, grid=(steps,),
            in_specs=[
                fixed(*near.shape), fixed(*far.shape),
                pl.BlockSpec((depth, columns), lambda s, place: (s, 0)),
                fixed(rows, columns),
            ],
            out_specs=fixed(rows, columns),
            scratch_shapes=[
                pltpu.VMEM((steps, rows, depth), jnp.float32),
                pltpu.VMEM((rows, columns), jnp.float32),
            ]),
        compiler_params=params(),
        name="output",
    )(place, near, far, weight, now)


def shards(hidden_rows, norm_gain, qkv_weight, out_weight, cache_kv, cache_len, page_kv,
           page_dest, page_row, page_count):
    slots = lax.axis_size("slot")
    batch = hidden_rows.shape[1]
    rows = batch * slots
    width = hidden_rows.shape[3]
    kv_width = cache_kv.shape[5]
    own = lax.axis_index("slot").astype(jnp.int32)
    masks = [slots >> (k + 1) for k in range(slots.bit_length() - 1)]
    offsets = [0]
    for mask in masks:
        offsets = offsets + [mask ^ o for o in offsets]
    order = own ^ jnp.asarray(np.array(offsets, np.int32))
    places = np.argsort(np.array(offsets)).astype(np.int32)
    place = jnp.asarray(places)[own ^ jnp.arange(slots, dtype=jnp.int32)]
    cache = cache_kv[0, :, :, 0]
    lengths = cache_len[0, :, :, 0]
    current, scaled, outgoing, code = prepare(
        own.reshape(1), hidden_rows[0], norm_gain, page_kv[0, 0], page_dest[0], page_row[0],
        page_count[0])
    incoming = lax.all_to_all(outgoing, "slot", split_axis=0, concat_axis=0, tiled=True)
    pages = incoming.reshape(-1, kv_width + LANES)
    for visit in range(CYCLE_STEPS):
        later = visit > 0
        block = current[None] if later else scaled
        for mask in masks[:-2]:
            block = jnp.concatenate([block, exchange(block, mask)], axis=0)
        quarter = block.shape[0]
        side = exchange(block, masks[-2])
        pair = exchange(block, masks[-1])
        corner = exchange(side, masks[-1])
        run = functools.partial(project, order, weight=qkv_weight[0], extra=incoming,
                                scale=later, slots=slots, batch=batch, kv_width=kv_width)
        state = run(start=0, x=block, state=None, last=False)
        state = run(start=2 * quarter, x=pair, state=state, last=False)
        state = run(start=quarter, x=side, state=state, last=False)
        qkv = run(start=3 * quarter, x=corner, state=state, last=True)
        qkv = lax.all_to_all(qkv, "slot", split_axis=0, concat_axis=0, tiled=True)
        context = attend(lengths, qkv, cache, pages, code, visit)
        for mask in masks[:-1]:
            context = jnp.concatenate([context, exchange(context, mask)], axis=0)
        other = exchange(context, masks[-1])
        updated = output(place, context, other, out_weight[0], current,
                         visit == CYCLE_STEPS - 1)
        current = next_segment(updated)
    return current.reshape(hidden_rows.shape)


def solution(mesh):
    return jax.shard_map(
        shards,
        mesh=mesh,
        in_specs=(
            P("segment", None, None, "slot"),
            P("segment", "slot"),
            P("segment", None, "slot"),
            P("segment", None, "slot"),
            P("segment", None, None, "slot", None, None),
            P("segment", None, None, "slot"),
            P("segment", "slot", None, None, None),
            P("segment", None, None),
            P("segment", None, None),
            P("segment", None, None),
        ),
        out_specs=P("segment", None, None, "slot"),
        check_vma=False,
    )
```

```python
import functools

import jax
import jax.numpy as jnp
import numpy as np
from jax import lax
from jax.experimental import pallas as pl
from jax.experimental.pallas import tpu as pltpu
from jax.sharding import PartitionSpec as P

QUERY_HEADS = 32
KEY_VALUE_HEADS = 4
HEAD_SIZE = 128
CYCLE_STEPS = 2
GROUP = QUERY_HEADS // KEY_VALUE_HEADS
KEY_WIDTH = KEY_VALUE_HEADS * HEAD_SIZE
LANES = 128

norm_eps = 1e-06
VMEM_LIMIT = 12 * 1024 * 1024


def params(**kw):
    return pltpu.CompilerParams(vmem_limit_bytes=VMEM_LIMIT, **kw)


def iota(shape, dim):
    return lax.broadcasted_iota(jnp.int32, shape, dim)


def exchange(block, mask):
    n = lax.axis_size("slot")
    return lax.ppermute(block, "slot", [(i, i ^ mask) for i in range(n)])


def next_segment(block):
    n = lax.axis_size("segment")
    return lax.ppermute(block, "segment", [(i, (i + 1) % n) for i in range(n)])


def split_rows(index, slots, batch, slot_first):
    if slot_first:
        return index // batch, lax.rem(index, batch)
    return lax.rem(index, slots), index // slots


def slot_rows_first(slots, batch):
    rows = slots * batch
    to_slot, to_row = split_rows(iota((rows, rows), 0), slots, batch, True)
    from_slot, from_row = split_rows(iota((rows, rows), 1), slots, batch, False)
    return ((to_slot == from_slot) & (to_row == from_row)).astype(jnp.bfloat16)


def arrival_rows(own, slots, batch):
    rows = slots * batch
    to_slot, to_row = split_rows(iota((rows, rows), 0), slots, batch, False)
    arrival, from_row = split_rows(iota((rows, rows), 1), slots, batch, True)
    away = to_slot ^ own
    bits = slots.bit_length() - 1
    place = jnp.zeros_like(away)
    for k in range(bits):
        place = place | (((away >> k) & 1) << (bits - 1 - k))
    return ((place == arrival) & (to_row == from_row)).astype(jnp.bfloat16)


def pack_kernel(own_ref, dest_sm, *refs):
    sources, (send_ref, code_ref), held, sem = refs[:6], refs[6:8], refs[8:14], refs[14]
    copies = [pltpu.make_async_copy(src, dst, sem.at[k])
              for k, (src, dst) in enumerate(zip(sources, held))]
    for copy in copies:
        copy.start()
    for copy in copies:
        copy.wait()
    x_ref, gain_ref, pages_ref, dest_ref, row_ref, count_ref = held
    slots, page_tok, wide = send_ref.shape
    kv_width = pages_ref.shape[2]
    own = own_ref[0]
    gain = gain_ref[...].astype(jnp.float32)
    at = iota((page_tok, LANES), 0)
    extra = jnp.zeros((page_tok, LANES), jnp.float32)
    gain_rows = gain.shape[1] // LANES
    for r in range(gain_rows):
        extra = jnp.where(at == r, gain[:, r * LANES:(r + 1) * LANES], extra)
    x = x_ref[...].astype(jnp.float32)
    rows = x.shape[0]
    column = jnp.sum(x * x, axis=1, keepdims=True)
    for r in range(-(-rows // LANES)):
        same = iota((rows, LANES), 0) == iota((rows, LANES), 1) + r * LANES
        line = jnp.sum(jnp.where(same, column, 0.0), axis=0, keepdims=True)
        for k in range(3):
            piece = line.astype(jnp.bfloat16).astype(jnp.float32)
            extra = jnp.where(at == gain_rows + 3 * r + k, piece, extra)
            line = line - piece
    extra = extra.astype(jnp.bfloat16)
    for p in range(pages_ref.shape[0]):
        send_ref[dest_sm[own, p], :, :kv_width] = pages_ref[p]
    for j in range(slots):
        send_ref[j, :, kv_width:] = extra
    tokens = code_ref.shape[1]
    mine = dest_ref[...] == own
    spread = (iota((slots, tokens), 1) // page_tok == iota((slots, tokens), 0)).astype(jnp.float32)

    def to_tokens(values):
        kept = jnp.where(mine, values, 0).astype(jnp.float32)
        by_token = lax.dot_general(kept, spread, (((0,), (0,)), ((), ())),
                                   preferred_element_type=jnp.float32)
        return jnp.sum(by_token, axis=0, keepdims=True)

    place = lax.rem(iota((1, tokens), 1), page_tok).astype(jnp.float32)
    live = place < to_tokens(count_ref[...])
    code = jnp.where(live, to_tokens(row_ref[...]), -1.0)
    code_ref[...] = jnp.broadcast_to(code, code_ref.shape).astype(jnp.int32)


def pack(own, x, gain, pages, dest, row, count):
    slots, total = dest.shape
    _, page_tok, kv_width = pages.shape
    fixed = lambda shape: pl.BlockSpec(shape, lambda s, own, dest: (0,) * len(shape))
    out_shape = [
        jax.ShapeDtypeStruct((slots, page_tok, kv_width + LANES), jnp.bfloat16),
        jax.ShapeDtypeStruct((8, slots * page_tok), jnp.int32),
    ]
    operands = [x, gain, pages, dest, row, count]
    return pl.pallas_call(
        pack_kernel,
        out_shape=out_shape,
        grid_spec=pltpu.PrefetchScalarGridSpec(
            num_scalar_prefetch=2, grid=(1,),
            in_specs=[pl.BlockSpec(memory_space=pltpu.HBM) for v in operands],
            out_specs=[fixed(v.shape) for v in out_shape],
            scratch_shapes=[pltpu.VMEM(v.shape, v.dtype) for v in operands] + [
                pltpu.SemaphoreType.DMA((len(operands),))]),
        compiler_params=params(),
        name="pack",
    )(own, dest, *operands)


def project_kernel(order_ref, x_ref, w_ref, *refs, scaled, first, last, slots, batch,
                   model_width):
    refs = list(refs)
    extra_ref = refs.pop(0) if last or not scaled else None
    states = 1 if scaled else 2
    before = [] if first else [refs.pop(0) for _ in range(states)]
    out_ref = refs.pop(0) if last else None
    acc = refs[0]
    step = pl.program_id(0)

    @pl.when(step == 0)
    def _():
        for k, ref in enumerate(refs):
            ref[...] = jnp.zeros_like(ref) if first else before[k][...]

    x = x_ref[0]
    rows, width = x.shape
    gain_rows = width // LANES
    if not scaled:
        parts = []
        total = refs[1][...]
        for r in range(gain_rows):
            part = x[:, r * LANES:(r + 1) * LANES].astype(jnp.float32)
            total = total + part * part
            gain = extra_ref[0, r:r + 1, :].astype(jnp.float32)
            parts.append((part * gain).astype(jnp.bfloat16))
        refs[1][...] = total
        x = parts[0] if len(parts) == 1 else jnp.concatenate(parts, axis=1)
    acc[...] += lax.dot_general(x, w_ref[...], (((1,), (1,)), ((), ())),
                                preferred_element_type=jnp.float32)

    if last:
        @pl.when(step == pl.num_programs(0) - 1)
        def _():
            if scaled:
                lines = jnp.sum(extra_ref[...].astype(jnp.float32), axis=0)
                sums = jnp.zeros((rows, 1), jnp.float32)
                for r in range(-(-rows // LANES)):
                    at = gain_rows + 3 * r
                    line = lines[at:at + 1] + lines[at + 1:at + 2] + lines[at + 2:at + 3]
                    same = iota((rows, LANES), 0) == iota((rows, LANES), 1) + r * LANES
                    sums = sums + jnp.sum(jnp.where(same, line, 0.0), axis=1, keepdims=True)
            else:
                sums = jnp.sum(refs[1][...], axis=1, keepdims=True)
            out = (acc[...] * lax.rsqrt(sums / model_width + norm_eps)).astype(jnp.bfloat16)
            out = jnp.dot(slot_rows_first(slots, batch), out, preferred_element_type=jnp.float32)
            for j in range(slots):
                out_ref[j] = out[j * batch:(j + 1) * batch].astype(jnp.bfloat16)


def project(order, start, x, weight, extra, state, *, scaled, last, slots, batch, kv_width):
    blocks, rows, width = x.shape
    columns, model_width = weight.shape
    first = state is None
    page_tok = extra.shape[1]
    fixed = lambda shape: pl.BlockSpec(shape, lambda s, order: (0,) * len(shape))
    in_specs = [
        pl.BlockSpec((1, rows, width), lambda s, order: (s, 0, 0)),
        pl.BlockSpec((columns, width), lambda s, order: (0, order[start + s])),
    ]
    operands = [x, weight]
    if not scaled:
        in_specs.append(pl.BlockSpec(
            (1, page_tok, LANES), lambda s, order: (order[start + s], 0, kv_width // LANES)))
        operands.append(extra)
    elif last:
        in_specs.append(pl.BlockSpec(
            (slots, page_tok, LANES), lambda s, order: (0, 0, kv_width // LANES)))
        operands.append(extra)
    if not first:
        in_specs += [fixed(v.shape) for v in state]
        operands += list(state)
    state_shape = [(rows, columns)] + ([] if scaled else [(rows, LANES)])
    if last:
        out_shape = jax.ShapeDtypeStruct((slots, batch, columns), jnp.bfloat16)
        out_specs = fixed(out_shape.shape)
        scratch = [pltpu.VMEM(shape, jnp.float32) for shape in state_shape]
    else:
        out_shape = [jax.ShapeDtypeStruct(shape, jnp.float32) for shape in state_shape]
        out_specs = [fixed(shape) for shape in state_shape]
        scratch = []
    return pl.pallas_call(
        functools.partial(project_kernel, scaled=scaled, first=first, last=last, slots=slots,
                          batch=batch, model_width=model_width),
        out_shape=out_shape,
        grid_spec=pltpu.PrefetchScalarGridSpec(
            num_scalar_prefetch=1, grid=(blocks,), in_specs=in_specs, out_specs=out_specs,
            scratch_shapes=scratch),
        compiler_params=params(),
        cost_estimate=pl.CostEstimate(flops=8 * rows * width * columns * blocks,
                                      bytes_accessed=2 * width * columns * blocks,
                                      transcendentals=0),
        name="project",
    )(order, *operands)


def attend_kernel(len_ref, qkv_ref, cache_ref, pages_ref, code_ref, out_ref, *, visit):
    slots, batch, columns = qkv_ref.shape
    positions = cache_ref.shape[2]
    tokens = pages_ref.shape[0]
    full = jnp.concatenate([qkv_ref[j].astype(jnp.float32) for j in range(slots)], axis=1)
    group_rows = GROUP * batch
    near = batch * positions
    near_pad = -(-(near + 16) // LANES) * LANES
    rows = KEY_VALUE_HEADS * group_rows
    nt = (((1,), (1,)), ((), ()))
    far_scores, near_scores, near_values = [], [], []
    key_at = QUERY_HEADS * HEAD_SIZE
    value_at = key_at + KEY_WIDTH
    for h in range(KEY_VALUE_HEADS):
        query = jnp.concatenate(
            [full[:, (h * GROUP + g) * HEAD_SIZE:(h * GROUP + g + 1) * HEAD_SIZE]
             for g in range(GROUP)], axis=0).astype(jnp.bfloat16)
        lo, hi = h * HEAD_SIZE, (h + 1) * HEAD_SIZE

        def nearby(cache_lo, fresh_lo):
            fresh = full[:, fresh_lo:fresh_lo + HEAD_SIZE]
            fresh = jnp.concatenate(
                [fresh, jnp.zeros((near_pad - near - batch, HEAD_SIZE), jnp.float32)], axis=0)
            old = [cache_ref[0, b, :, cache_lo:cache_lo + HEAD_SIZE] for b in range(batch)]
            return jnp.concatenate(old + [fresh.astype(jnp.bfloat16)], axis=0)

        keys = nearby(lo, key_at + lo)
        near_values.append(nearby(KEY_WIDTH + lo, value_at + lo))
        far_scores.append(lax.dot_general(query, pages_ref[:, lo:hi], nt,
                                          preferred_element_type=jnp.float32))
        near_scores.append(lax.dot_general(query, keys, nt, preferred_element_type=jnp.float32))
    scale = HEAD_SIZE ** (-0.5)
    far = jnp.concatenate(far_scores, axis=0) * scale
    close = jnp.concatenate(near_scores, axis=0) * scale
    far_row = lax.rem(iota((rows, tokens), 0), batch)
    far = jnp.where(code_ref[0:1, :] == far_row + visit * batch, far, -1e30)
    row = lax.rem(iota((rows, near_pad), 0), batch)
    lane = iota((rows, near_pad), 1)
    lengths = jnp.zeros((rows, near_pad), jnp.int32)
    for b in range(batch):
        lengths = jnp.where(row == b, len_ref[visit, b], lengths)
    position = lane - row * positions
    seen = (position >= 0) & (position < lengths) | (lane == near + row)
    close = jnp.where(seen, close, -1e30)
    top = jnp.maximum(jnp.max(far, axis=1, keepdims=True), jnp.max(close, axis=1, keepdims=True))
    far = jnp.exp(far - top)
    close = jnp.exp(close - top)
    denominator = jnp.sum(far, axis=1, keepdims=True) + jnp.sum(close, axis=1, keepdims=True)
    far = (far / denominator).astype(jnp.bfloat16)
    close = (close / denominator).astype(jnp.bfloat16)
    for h in range(KEY_VALUE_HEADS):
        mine = slice(h * group_rows, (h + 1) * group_rows)
        lo = KEY_WIDTH + h * HEAD_SIZE
        context = jnp.dot(far[mine], pages_ref[:, lo:lo + HEAD_SIZE],
                          preferred_element_type=jnp.float32)
        context = context + jnp.dot(close[mine], near_values[h],
                                    preferred_element_type=jnp.float32)
        for g in range(GROUP):
            at = (h * GROUP + g) * HEAD_SIZE
            out_ref[0, :, at:at + HEAD_SIZE] = context[g * batch:(g + 1) * batch].astype(
                jnp.bfloat16)


def attend(lengths, qkv, cache, pages, code, visit):
    slots, batch, columns = qkv.shape
    _, _, positions, kv_width = cache.shape
    tokens = pages.shape[0]
    return pl.pallas_call(
        functools.partial(attend_kernel, visit=visit),
        out_shape=jax.ShapeDtypeStruct((1, batch, QUERY_HEADS * HEAD_SIZE), jnp.bfloat16),
        grid=(1,),
        in_specs=[
            pl.BlockSpec(memory_space=pltpu.SMEM),
            pl.BlockSpec((slots, batch, columns), lambda s: (0, 0, 0)),
            pl.BlockSpec((1, batch, positions, kv_width), lambda s: (visit, 0, 0, 0)),
            pl.BlockSpec((tokens, kv_width), lambda s: (0, 0)),
            pl.BlockSpec(code.shape, lambda s: (0, 0)),
        ],
        out_specs=pl.BlockSpec((1, batch, QUERY_HEADS * HEAD_SIZE), lambda s: (0, 0, 0)),
        compiler_params=params(),
        name="attend",
    )(lengths, qkv, cache, pages, code)


def output_kernel(own_ref, *refs, slots, batch):
    pieces, (w_ref, now_ref, out_ref, acc) = refs[:4], refs[4:]
    step = pl.program_id(0)
    depth = w_ref.shape[0]

    @pl.when(step == 0)
    def _():
        acc[...] = jnp.zeros_like(acc)

    left = jnp.concatenate(
        [piece[i].astype(jnp.float32) for piece in pieces for i in range(piece.shape[0])], axis=0)
    acc[...] += jnp.dot(left.astype(jnp.bfloat16), w_ref[...], preferred_element_type=jnp.float32)

    @pl.when(step == pl.num_programs(0) - 1)
    def _():
        rest = acc[...]
        move = arrival_rows(own_ref[0], slots, batch)
        total = now_ref[...].astype(jnp.float32)
        moved = None
        for _ in range(3):
            part = rest.astype(jnp.bfloat16)
            rest = rest - part.astype(jnp.float32)
            part = jnp.dot(move, part, preferred_element_type=jnp.float32)
            moved = part if moved is None else moved + part
        out_ref[...] = (total + moved).astype(jnp.bfloat16)


def output(own, pieces, weight, now, slots):
    quarter, batch, features = pieces[0].shape
    rows, columns = now.shape
    steps = 4
    depth = features // steps
    fixed = lambda *shape: pl.BlockSpec(shape, lambda s, own: (0,) * len(shape))
    return pl.pallas_call(
        functools.partial(output_kernel, slots=slots, batch=batch),
        out_shape=jax.ShapeDtypeStruct((rows, columns), jnp.bfloat16),
        grid_spec=pltpu.PrefetchScalarGridSpec(
            num_scalar_prefetch=1, grid=(steps,),
            in_specs=[pl.BlockSpec((quarter, batch, depth), lambda s, own: (0, 0, s))] * 4 + [
                pl.BlockSpec((depth, columns), lambda s, own: (s, 0)),
                fixed(rows, columns),
            ],
            out_specs=fixed(rows, columns),
            scratch_shapes=[pltpu.VMEM((rows, columns), jnp.float32)]),
        compiler_params=params(),
        name="output",
    )(own, *pieces, weight, now)


def shards(hidden_rows, norm_gain, qkv_weight, out_weight, cache_kv, cache_len, page_kv,
           page_dest, page_row, page_count):
    slots = lax.axis_size("slot")
    batch = hidden_rows.shape[1]
    rows = batch * slots
    width = hidden_rows.shape[3]
    kv_width = cache_kv.shape[5]
    own = lax.axis_index("slot").astype(jnp.int32)
    masks = [slots >> (k + 1) for k in range(slots.bit_length() - 1)]
    offsets = [0]
    for mask in masks:
        offsets = offsets + [mask ^ o for o in offsets]
    order = own ^ jnp.asarray(np.array(offsets, np.int32))
    own = own.reshape(1)
    cache = cache_kv[0, :, :, 0]
    lengths = cache_len[0, :, :, 0]
    weight_in = qkv_weight[0].T
    current = hidden_rows.reshape(rows, width)
    scaled = (current.astype(jnp.float32) * norm_gain.astype(jnp.float32)).astype(jnp.bfloat16)
    outgoing, code = pack(own, current, norm_gain, page_kv[0, 0], page_dest[0], page_row[0], page_count[0])
    for visit in range(CYCLE_STEPS):
        block = (current if visit else scaled)[None]
        for mask in masks[:-2]:
            block = jnp.concatenate([block, exchange(block, mask)], axis=0)
            if mask == masks[0] and visit == 0:
                block, outgoing = lax.optimization_barrier((block, outgoing))
                incoming = lax.all_to_all(outgoing, "slot", split_axis=0, concat_axis=0,
                                          tiled=True)
                pages = incoming.reshape(-1, kv_width + LANES)
        quarter = block.shape[0]
        run = functools.partial(project, order, weight=weight_in, extra=incoming,
                                scaled=visit == 0, slots=slots, batch=batch, kv_width=kv_width)
        side = exchange(block, masks[-2])
        pair = exchange(block, masks[-1])
        state = run(start=0, x=block, state=None, last=False)
        state = run(start=2 * quarter, x=pair, state=state, last=False)
        side, state = lax.optimization_barrier((side, state))
        corner = exchange(side, masks[-1])
        state = run(start=quarter, x=side, state=state, last=False)
        qkv = run(start=3 * quarter, x=corner, state=state, last=True)
        qkv = lax.all_to_all(qkv, "slot", split_axis=0, concat_axis=0, tiled=True)
        context = attend(lengths, qkv, cache, pages, code, visit)
        for mask in masks[:-2]:
            context = jnp.concatenate([context, exchange(context, mask)], axis=0)
        side = exchange(context, masks[-2])
        pair = exchange(context, masks[-1])
        corner = exchange(side, masks[-1])
        updated = output(own, (context, side, pair, corner), out_weight[0], current, slots)
        current = next_segment(updated)
    return current.reshape(hidden_rows.shape)


def solution(mesh):
    return jax.shard_map(
        shards,
        mesh=mesh,
        in_specs=(
            P("segment", None, None, "slot"),
            P("segment", "slot"),
            P("segment", None, "slot"),
            P("segment", None, "slot"),
            P("segment", None, None, "slot", None, None),
            P("segment", None, None, "slot"),
            P("segment", "slot", None, None, None),
            P("segment", None, None),
            P("segment", None, None),
            P("segment", None, None),
        ),
        out_specs=P("segment", None, None, "slot"),
        check_vma=False,
    )
```

```python
import functools

import jax
import jax.numpy as jnp
import numpy as np
from jax import lax
from jax.experimental import pallas as pl
from jax.experimental.pallas import tpu as pltpu
from jax.sharding import PartitionSpec as P

QUERY_HEADS = 32
KEY_VALUE_HEADS = 4
HEAD_SIZE = 128
CYCLE_STEPS = 2
GROUP = QUERY_HEADS // KEY_VALUE_HEADS
KEY_WIDTH = KEY_VALUE_HEADS * HEAD_SIZE
LANES = 128

norm_eps = 1e-06
FIRST_LIMIT = 63 * 1024 * 1024
VMEM_LIMIT = 12 * 1024 * 1024


def params(**kw):
    return pltpu.CompilerParams(vmem_limit_bytes=VMEM_LIMIT, **kw)


def iota(shape, dim):
    return lax.broadcasted_iota(jnp.int32, shape, dim)


def exchange(block, mask):
    n = lax.axis_size("slot")
    return lax.ppermute(block, "slot", [(i, i ^ mask) for i in range(n)])


def next_segment(block):
    n = lax.axis_size("segment")
    return lax.ppermute(block, "segment", [(i, (i + 1) % n) for i in range(n)])


def split_rows(index, slots, batch, slot_first):
    if slot_first:
        return index // batch, lax.rem(index, batch)
    return lax.rem(index, slots), index // slots


def slot_rows_first(slots, batch):
    rows = slots * batch
    to_slot, to_row = split_rows(iota((rows, rows), 0), slots, batch, True)
    from_slot, from_row = split_rows(iota((rows, rows), 1), slots, batch, False)
    return ((to_slot == from_slot) & (to_row == from_row)).astype(jnp.bfloat16)


def arrival_rows(own, slots, batch):
    rows = slots * batch
    to_slot, to_row = split_rows(iota((rows, rows), 0), slots, batch, False)
    arrival, from_row = split_rows(iota((rows, rows), 1), slots, batch, True)
    away = to_slot ^ own
    bits = slots.bit_length() - 1
    place = jnp.zeros_like(away)
    for k in range(bits):
        place = place | (((away >> k) & 1) << (bits - 1 - k))
    return ((place == arrival) & (to_row == from_row)).astype(jnp.bfloat16)


def pack_kernel(own_ref, dest_ref, gain_hbm, pages_hbm, send_ref, gain_ref, pages_ref, sem):
    copies = [pltpu.make_async_copy(gain_hbm, gain_ref, sem.at[0]),
              pltpu.make_async_copy(pages_hbm, pages_ref, sem.at[1])]
    for copy in copies:
        copy.start()
    for copy in copies:
        copy.wait()
    slots, page_tok, wide = send_ref.shape
    kv_width = pages_ref.shape[2]
    gain = gain_ref[...].astype(jnp.float32)
    at = iota((page_tok, LANES), 0)
    extra = jnp.zeros((page_tok, LANES), jnp.float32)
    for r in range(gain.shape[1] // LANES):
        extra = jnp.where(at == r, gain[:, r * LANES:(r + 1) * LANES], extra)
    extra = extra.astype(jnp.bfloat16)
    for p in range(pages_ref.shape[0]):
        send_ref[dest_ref[own_ref[0], p], :, :kv_width] = pages_ref[p]
    for j in range(slots):
        send_ref[j, :, kv_width:] = extra


def pack(own, gain, pages, dest):
    _, page_tok, kv_width = pages.shape
    shape = (dest.shape[0], page_tok, kv_width + LANES)
    there = pl.BlockSpec(memory_space=pl.ANY)
    return pl.pallas_call(
        pack_kernel,
        out_shape=jax.ShapeDtypeStruct(shape, pages.dtype),
        grid_spec=pltpu.PrefetchScalarGridSpec(
            num_scalar_prefetch=2, grid=(1,), in_specs=[there, there],
            out_specs=pl.BlockSpec(shape, lambda s, own, dest: (0, 0, 0)),
            scratch_shapes=[pltpu.VMEM(gain.shape, gain.dtype), pltpu.VMEM(pages.shape, pages.dtype),
                            pltpu.SemaphoreType.DMA((2,))]),
        compiler_params=pltpu.CompilerParams(vmem_limit_bytes=FIRST_LIMIT),
        name="pack",
    )(own, dest, gain, pages)


def project_kernel(order_ref, x_ref, w_ref, extra_ref, *refs, start, first, last, batch, kv_width):
    acc_in, square_in = (None, None) if first else refs[:2]
    outs = refs if first else refs[2:]
    blocks, rows, width = x_ref.shape
    columns, model_width = w_ref.shape
    acc = jnp.zeros((rows, columns), jnp.float32) if first else acc_in[...]
    square = jnp.zeros((rows, LANES), jnp.float32) if first else square_in[...]
    for i in range(blocks):
        source = order_ref[start + i]
        x = x_ref[i]
        gain = extra_ref[source, :, kv_width:].astype(jnp.float32)
        parts = []
        for r in range(width // LANES):
            part = x[:, r * LANES:(r + 1) * LANES].astype(jnp.float32)
            square = square + part * part
            parts.append((part * gain[r:r + 1]).astype(jnp.bfloat16))
        x = parts[0] if len(parts) == 1 else jnp.concatenate(parts, axis=1)
        here = pl.ds(pl.multiple_of(source * width, width), width)
        acc = acc + lax.dot_general(x, w_ref[:, here], (((1,), (1,)), ((), ())),
                                    preferred_element_type=jnp.float32)
    if not last:
        outs[0][...] = acc
        outs[1][...] = square
        return
    sums = jnp.sum(square, axis=1, keepdims=True)
    out = (acc * lax.rsqrt(sums / model_width + norm_eps)).astype(jnp.bfloat16)
    slots = rows // batch
    out = jnp.dot(slot_rows_first(slots, batch), out, preferred_element_type=jnp.float32)
    for j in range(slots):
        outs[0][j] = out[j * batch:(j + 1) * batch].astype(jnp.bfloat16)


def project(order, start, x, weight, extra, state, *, last, batch, kv_width):
    blocks, rows, width = x.shape
    columns = weight.shape[0]
    first = state is None
    operands = [x, weight, extra] + ([] if first else list(state))
    if last:
        out_shape = jax.ShapeDtypeStruct((rows // batch, batch, columns), jnp.bfloat16)
    else:
        out_shape = [jax.ShapeDtypeStruct((rows, columns), jnp.float32),
                     jax.ShapeDtypeStruct((rows, LANES), jnp.float32)]
    whole = pl.BlockSpec(memory_space=pltpu.VMEM)
    return pl.pallas_call(
        functools.partial(project_kernel, start=start, first=first, last=last, batch=batch,
                          kv_width=kv_width),
        out_shape=out_shape,
        in_specs=[pl.BlockSpec(memory_space=pltpu.SMEM)] + [whole] * len(operands),
        out_specs=whole if last else [whole] * len(out_shape),
        compiler_params=params(),
        cost_estimate=pl.CostEstimate(flops=8 * rows * width * columns * blocks,
                                      bytes_accessed=2 * width * columns * blocks,
                                      transcendentals=0),
        name="project",
    )(order, *operands)


def token_rows(own, dest_ref, row_ref, count_ref, page_tok):
    slots = dest_ref.shape[0]
    tokens = slots * page_tok
    mine = dest_ref[...] == own
    spread = (iota((slots, tokens), 1) // page_tok == iota((slots, tokens), 0)).astype(jnp.float32)

    def to_tokens(values):
        kept = jnp.where(mine, values, 0).astype(jnp.float32)
        by_token = lax.dot_general(kept, spread, (((0,), (0,)), ((), ())),
                                   preferred_element_type=jnp.float32)
        return jnp.sum(by_token, axis=0, keepdims=True)

    place = lax.rem(iota((1, tokens), 1), page_tok).astype(jnp.float32)
    live = place < to_tokens(count_ref[...])
    return jnp.where(live, to_tokens(row_ref[...]), -1.0).astype(jnp.int32)


def attend_kernel(own_ref, len_ref, qkv_ref, cache_ref, pages_ref, dest_ref, page_row_ref, count_ref,
                  out_ref, *, visit):
    slots, batch, columns = qkv_ref.shape
    positions = cache_ref.shape[2]
    tokens = pages_ref.shape[0]
    full = jnp.concatenate([qkv_ref[j].astype(jnp.float32) for j in range(slots)], axis=1)
    group_rows = GROUP * batch
    near = batch * positions
    near_pad = -(-(near + 16) // LANES) * LANES
    rows = KEY_VALUE_HEADS * group_rows
    nt = (((1,), (1,)), ((), ()))
    far_scores, near_scores, near_values = [], [], []
    key_at = QUERY_HEADS * HEAD_SIZE
    value_at = key_at + KEY_WIDTH
    for h in range(KEY_VALUE_HEADS):
        query = jnp.concatenate(
            [full[:, (h * GROUP + g) * HEAD_SIZE:(h * GROUP + g + 1) * HEAD_SIZE]
             for g in range(GROUP)], axis=0).astype(jnp.bfloat16)
        lo, hi = h * HEAD_SIZE, (h + 1) * HEAD_SIZE

        def nearby(cache_lo, fresh_lo):
            fresh = full[:, fresh_lo:fresh_lo + HEAD_SIZE]
            fresh = jnp.concatenate(
                [fresh, jnp.zeros((near_pad - near - batch, HEAD_SIZE), jnp.float32)], axis=0)
            old = [cache_ref[0, b, :, cache_lo:cache_lo + HEAD_SIZE] for b in range(batch)]
            return jnp.concatenate(old + [fresh.astype(jnp.bfloat16)], axis=0)

        keys = nearby(lo, key_at + lo)
        near_values.append(nearby(KEY_WIDTH + lo, value_at + lo))
        far_scores.append(lax.dot_general(query, pages_ref[:, lo:hi], nt,
                                          preferred_element_type=jnp.float32))
        near_scores.append(lax.dot_general(query, keys, nt, preferred_element_type=jnp.float32))
    scale = HEAD_SIZE ** (-0.5)
    far = jnp.concatenate(far_scores, axis=0) * scale
    close = jnp.concatenate(near_scores, axis=0) * scale
    far_row = lax.rem(iota((rows, tokens), 0), batch)
    code = token_rows(own_ref[0], dest_ref, page_row_ref, count_ref, tokens // slots)
    far = jnp.where(code == far_row + visit * batch, far, -1e30)
    row = lax.rem(iota((rows, near_pad), 0), batch)
    lane = iota((rows, near_pad), 1)
    lengths = jnp.zeros((rows, near_pad), jnp.int32)
    for b in range(batch):
        lengths = jnp.where(row == b, len_ref[visit, b], lengths)
    position = lane - row * positions
    seen = (position >= 0) & (position < lengths) | (lane == near + row)
    close = jnp.where(seen, close, -1e30)
    top = jnp.maximum(jnp.max(far, axis=1, keepdims=True), jnp.max(close, axis=1, keepdims=True))
    far = jnp.exp(far - top)
    close = jnp.exp(close - top)
    denominator = jnp.sum(far, axis=1, keepdims=True) + jnp.sum(close, axis=1, keepdims=True)
    far = (far / denominator).astype(jnp.bfloat16)
    close = (close / denominator).astype(jnp.bfloat16)
    for h in range(KEY_VALUE_HEADS):
        mine = slice(h * group_rows, (h + 1) * group_rows)
        lo = KEY_WIDTH + h * HEAD_SIZE
        context = jnp.dot(far[mine], pages_ref[:, lo:lo + HEAD_SIZE],
                          preferred_element_type=jnp.float32)
        context = context + jnp.dot(close[mine], near_values[h],
                                    preferred_element_type=jnp.float32)
        for g in range(GROUP):
            at = (h * GROUP + g) * HEAD_SIZE
            out_ref[0, :, at:at + HEAD_SIZE] = context[g * batch:(g + 1) * batch].astype(
                jnp.bfloat16)


def attend(own, lengths, qkv, cache, pages, arrivals, visit):
    slots, batch, columns = qkv.shape
    _, _, positions, kv_width = cache.shape
    tokens = pages.shape[0]
    scalars = pl.BlockSpec(memory_space=pltpu.SMEM)
    fixed = lambda *shape: pl.BlockSpec(shape, lambda s: (0,) * len(shape))
    return pl.pallas_call(
        functools.partial(attend_kernel, visit=visit),
        out_shape=jax.ShapeDtypeStruct((1, batch, QUERY_HEADS * HEAD_SIZE), jnp.bfloat16),
        grid=(1,),
        in_specs=[
            scalars, scalars, fixed(slots, batch, columns),
            pl.BlockSpec((1, batch, positions, kv_width), lambda s: (visit, 0, 0, 0)),
            fixed(tokens, kv_width)] + [fixed(*v.shape) for v in arrivals],
        out_specs=fixed(1, batch, QUERY_HEADS * HEAD_SIZE),
        compiler_params=params(),
        name="attend",
    )(own, lengths, qkv, cache, pages, *arrivals)


def output_kernel(own_ref, *refs, slots, batch):
    pieces, (w_ref, now_ref, out_ref) = refs[:4], refs[4:]
    features = w_ref.shape[0]
    depth = features // 4
    acc = jnp.zeros(out_ref.shape, jnp.float32)
    for k in range(0, features, depth):
        left = jnp.concatenate(
            [piece[i, :, k:k + depth].astype(jnp.float32)
             for piece in pieces for i in range(piece.shape[0])], axis=0)
        acc = acc + jnp.dot(left.astype(jnp.bfloat16), w_ref[k:k + depth],
                            preferred_element_type=jnp.float32)
    move = arrival_rows(own_ref[0], slots, batch)
    moved = None
    for _ in range(3):
        part = acc.astype(jnp.bfloat16)
        acc = acc - part.astype(jnp.float32)
        part = jnp.dot(move, part, preferred_element_type=jnp.float32)
        moved = part if moved is None else moved + part
    out_ref[...] = (now_ref[...].astype(jnp.float32) + moved).astype(jnp.bfloat16)


def output(own, pieces, weight, now, slots):
    batch = pieces[0].shape[1]
    whole = pl.BlockSpec(memory_space=pltpu.VMEM)
    return pl.pallas_call(
        functools.partial(output_kernel, slots=slots, batch=batch),
        out_shape=jax.ShapeDtypeStruct(now.shape, jnp.bfloat16),
        in_specs=[pl.BlockSpec(memory_space=pltpu.SMEM)] + [whole] * 6,
        out_specs=whole,
        compiler_params=params(),
        name="output",
    )(own, *pieces, weight, now)


def shards(hidden_rows, norm_gain, qkv_weight, out_weight, cache_kv, cache_len, page_kv,
           page_dest, page_row, page_count):
    slots = lax.axis_size("slot")
    batch = hidden_rows.shape[1]
    rows = batch * slots
    width = hidden_rows.shape[3]
    kv_width = cache_kv.shape[5]
    own = lax.axis_index("slot").astype(jnp.int32)
    masks = [slots >> (k + 1) for k in range(slots.bit_length() - 1)]
    offsets = [0]
    for mask in masks:
        offsets = offsets + [mask ^ o for o in offsets]
    order = own ^ jnp.asarray(np.array(offsets, np.int32))
    cache = cache_kv[0, :, :, 0]
    lengths = cache_len[0, :, :, 0]
    weight_in = qkv_weight[0].T
    weight_out = out_weight[0]
    own = own.reshape(1)
    current = hidden_rows.reshape(rows, width)
    outgoing = pack(own, norm_gain, page_kv[0, 0], page_dest[0])
    current, outgoing = lax.optimization_barrier((current, outgoing))
    incoming = lax.all_to_all(outgoing, "slot", split_axis=0, concat_axis=0, tiled=True)
    arrivals = (page_dest[0], page_row[0], page_count[0])
    for visit in range(CYCLE_STEPS):
        block = current[None]
        for mask in masks[:-2]:
            block = jnp.concatenate([block, exchange(block, mask)], axis=0)
        quarter = block.shape[0]
        run = functools.partial(project, order, weight=weight_in,
                                batch=batch, kv_width=kv_width)
        side = exchange(block, masks[-2])
        pair = exchange(block, masks[-1])
        held, incoming = lax.optimization_barrier((block, incoming))
        state = run(start=0, x=held, extra=incoming, state=None, last=False)
        state = run(start=2 * quarter, x=pair, extra=incoming, state=state, last=False)
        side, state = lax.optimization_barrier((side, state))
        corner = exchange(side, masks[-1])
        state = run(start=quarter, x=side, extra=incoming, state=state, last=False)
        qkv = run(start=3 * quarter, x=corner, extra=incoming, state=state, last=True)
        qkv = lax.all_to_all(qkv, "slot", split_axis=0, concat_axis=0, tiled=True)
        pages = incoming.reshape(-1, kv_width + LANES)
        context = attend(own, lengths, qkv, cache, pages, arrivals, visit)
        for mask in masks[:-2]:
            context = jnp.concatenate([context, exchange(context, mask)], axis=0)
        side = exchange(context, masks[-2])
        pair = exchange(context, masks[-1])
        corner = exchange(side, masks[-1])
        updated = output(own, (context, side, pair, corner), weight_out, current, slots)
        current = next_segment(updated)
    return current.reshape(hidden_rows.shape)


def solution(mesh):
    return jax.shard_map(
        shards,
        mesh=mesh,
        in_specs=(
            P("segment", None, None, "slot"),
            P("segment", "slot"),
            P("segment", None, "slot"),
            P("segment", None, "slot"),
            P("segment", None, None, "slot", None, None),
            P("segment", None, None, "slot"),
            P("segment", "slot", None, None, None),
            P("segment", None, None),
            P("segment", None, None),
            P("segment", None, None),
        ),
        out_specs=P("segment", None, None, "slot"),
        check_vma=False,
    )
```

```python
import functools

import jax
import jax.numpy as jnp
import numpy as np
from jax import lax
from jax.experimental import pallas as pl
from jax.experimental.pallas import tpu as pltpu
from jax.sharding import PartitionSpec as P

QUERY_HEADS = 32
KEY_VALUE_HEADS = 4
HEAD_SIZE = 128
CYCLE_STEPS = 2
GROUP = QUERY_HEADS // KEY_VALUE_HEADS
KEY_WIDTH = KEY_VALUE_HEADS * HEAD_SIZE
LANES = 128

norm_eps = 1e-06
VMEM_LIMIT = 12 * 1024 * 1024


def params(**kw):
    return pltpu.CompilerParams(vmem_limit_bytes=VMEM_LIMIT, **kw)


def iota(shape, dim):
    return lax.broadcasted_iota(jnp.int32, shape, dim)


def exchange(block, mask):
    n = lax.axis_size("slot")
    return lax.ppermute(block, "slot", [(i, i ^ mask) for i in range(n)])


def spread(block, masks):
    across, over, core = masks
    second = exchange(block, across)
    third = exchange(block, over)
    fourth = exchange(second, over)
    groups = [block, second, third, fourth]
    return groups + [exchange(group, core) for group in groups]


def next_segment(block, mask=0):
    n, slots = lax.axis_size("segment"), lax.axis_size("slot")
    route = [(s * slots + i, (s + 1) % n * slots + (i ^ mask)) for s in range(n)
             for i in range(slots)]
    return lax.ppermute(block, ("segment", "slot"), route)


def split_rows(index, slots, batch, slot_first):
    if slot_first:
        return index // batch, lax.rem(index, batch)
    return lax.rem(index, slots), index // slots


def slot_rows_first(slots, batch):
    rows = slots * batch
    to_slot, to_row = split_rows(iota((rows, rows), 0), slots, batch, True)
    from_slot, from_row = split_rows(iota((rows, rows), 1), slots, batch, False)
    return ((to_slot == from_slot) & (to_row == from_row)).astype(jnp.bfloat16)


def arrival_rows(own, slots, batch):
    rows = slots * batch
    to_slot, to_row = split_rows(iota((rows, rows), 0), slots, batch, False)
    arrival, from_row = split_rows(iota((rows, rows), 1), slots, batch, True)
    away = to_slot ^ own
    bits = slots.bit_length() - 1
    place = jnp.zeros_like(away)
    for k in range(bits):
        place = place | (((away >> k) & 1) << (bits - 1 - k))
    return ((place == arrival) & (to_row == from_row)).astype(jnp.bfloat16)


def room_for(columns):
    return -(-(columns // 2) // LANES) * LANES


def pack_kernel(own_ref, dest_ref, pages_ref, send_ref):
    slots, page_tok, wide = send_ref.shape
    kv_width = pages_ref.shape[2]
    for p in range(pages_ref.shape[0]):
        send_ref[dest_ref[own_ref[0], p], :, :kv_width] = pages_ref[p]
    for j in range(slots):
        send_ref[j, :, kv_width:] = jnp.zeros((page_tok, wide - kv_width), send_ref.dtype)


def pack(own, pages, dest, room):
    _, page_tok, kv_width = pages.shape
    whole = pl.BlockSpec(memory_space=pltpu.VMEM)
    scalars = pl.BlockSpec(memory_space=pltpu.SMEM)
    return pl.pallas_call(
        pack_kernel,
        out_shape=jax.ShapeDtypeStruct((dest.shape[0], page_tok, kv_width + room), pages.dtype),
        in_specs=[scalars, scalars, whole],
        out_specs=whole,
        compiler_params=params(),
        name="pack",
    )(own, dest, pages)


def project_kernel(order_ref, w_ref, *refs, starts, rows, carried, first, last, packed, batch):
    refs = list(refs)
    x_refs = [refs.pop(0) for _ in starts]
    kept = None if carried else refs.pop(0)
    acc_in, square_in = (None, None) if first else (refs.pop(0), refs.pop(0))
    if packed:
        refs.pop(0)
    if carried:
        kept = refs.pop(0)
    blocks, _, width = x_refs[0].shape
    columns, model_width = w_ref.shape
    acc = jnp.zeros((rows, columns), jnp.float32) if first else acc_in[...]
    square = jnp.zeros((rows, LANES), jnp.float32) if first else square_in[...]
    for g, start in enumerate(starts):
        for i in range(blocks):
            if carried:
                kept[g * blocks + i] = x_refs[g][i, rows:]
            x = x_refs[g][i, :rows]
            gain = kept[g * blocks + i].astype(jnp.float32)[:1]
            parts = []
            for r in range(0, width, LANES):
                part = x[:, r:r + LANES].astype(jnp.float32)
                square = square + part * part
                parts.append((part * gain[:, r:r + LANES]).astype(jnp.bfloat16))
            x = parts[0] if len(parts) == 1 else jnp.concatenate(parts, axis=1)
            here = pl.ds(pl.multiple_of(order_ref[start + i] * width, width), width)
            acc = acc + lax.dot_general(x, w_ref[:, here], (((1,), (1,)), ((), ())),
                                        preferred_element_type=jnp.float32)
    if not last:
        refs[0][...] = acc
        refs[1][...] = square
        return
    sums = jnp.sum(square, axis=1, keepdims=True)
    out = (acc * lax.rsqrt(sums / model_width + norm_eps)).astype(jnp.bfloat16)
    slots = rows // batch
    out = jnp.dot(slot_rows_first(slots, batch), out, preferred_element_type=jnp.float32)
    half = columns // 2
    for j in range(slots):
        mine = out[j * batch:(j + 1) * batch]
        if packed:
            at = refs[0].shape[2] - room_for(columns)
            mine = jnp.concatenate([mine[:, :half], mine[:, half:]], axis=0)
            refs[0][j, :, at:at + half] = mine.astype(jnp.bfloat16)
        else:
            refs[0][j] = mine.astype(jnp.bfloat16)


def project(order, rows, batch, weight, groups, gains, state, last=False, outgoing=None):
    blocks, held, width = groups[0][1].shape
    columns = weight.shape[0]
    carried, first, packed = gains is None, state is None, outgoing is not None
    operands = [weight] + [x for _, x in groups] + ([] if carried else [gains])
    operands += [] if first else list(state)
    aliases = {}
    out_shape = []
    if carried:
        out_shape.append(jax.ShapeDtypeStruct((len(groups) * blocks, held - rows, width),
                                              jnp.bfloat16))
    if packed:
        aliases = {len(operands) + 1: len(out_shape)}
        operands.append(outgoing)
        out_shape.append(jax.ShapeDtypeStruct(outgoing.shape, outgoing.dtype))
    elif last:
        out_shape.append(jax.ShapeDtypeStruct((rows // batch, batch, columns), jnp.bfloat16))
    else:
        out_shape += [jax.ShapeDtypeStruct((rows, columns), jnp.float32),
                      jax.ShapeDtypeStruct((rows, LANES), jnp.float32)]
    whole = pl.BlockSpec(memory_space=pltpu.VMEM)
    work = rows * width * columns * blocks * len(groups)
    out = pl.pallas_call(
        functools.partial(project_kernel, starts=[g * blocks for g, _ in groups], rows=rows,
                          carried=carried, first=first, last=last, packed=packed, batch=batch),
        out_shape=out_shape,
        in_specs=[pl.BlockSpec(memory_space=pltpu.SMEM)] + [whole] * len(operands),
        out_specs=[whole] * len(out_shape),
        input_output_aliases=aliases,
        compiler_params=params(),
        cost_estimate=pl.CostEstimate(flops=8 * work, bytes_accessed=2 * work // rows,
                                      transcendentals=0),
        name="project",
    )(order, *operands)
    if carried:
        gains, *out = out
    return gains, (out[0] if last else out)


def token_rows(own, dest_ref, row_ref, count_ref, page_tok):
    slots = dest_ref.shape[0]
    tokens = slots * page_tok
    mine = dest_ref[...] == own
    spread = (iota((slots, tokens), 1) // page_tok == iota((slots, tokens), 0)).astype(jnp.float32)

    def to_tokens(values):
        kept = jnp.where(mine, values, 0).astype(jnp.float32)
        by_token = lax.dot_general(kept, spread, (((0,), (0,)), ((), ())),
                                   preferred_element_type=jnp.float32)
        return jnp.sum(by_token, axis=0, keepdims=True)

    place = lax.rem(iota((1, tokens), 1), page_tok).astype(jnp.float32)
    live = place < to_tokens(count_ref[...])
    return jnp.where(live, to_tokens(row_ref[...]), -1.0).astype(jnp.int32)


def attend_kernel(own_ref, len_ref, qkv_ref, cache_ref, pages_ref, dest_ref, page_row_ref, count_ref,
                  out_ref, *, visit, columns, packed):
    slots = qkv_ref.shape[0]
    batch, positions = cache_ref.shape[1:3]
    tokens = pages_ref.shape[0]
    pieces = []
    for j in range(slots):
        piece = qkv_ref[j].astype(jnp.float32)
        if packed:
            half = columns // 2
            pieces += [piece[:batch, :half], piece[batch:2 * batch, :half]]
        else:
            pieces.append(piece)
    full = jnp.concatenate(pieces, axis=1)
    group_rows = GROUP * batch
    near = batch * positions
    near_pad = -(-(near + 16) // LANES) * LANES
    rows = KEY_VALUE_HEADS * group_rows
    nt = (((1,), (1,)), ((), ()))
    far_scores, near_scores, near_values = [], [], []
    key_at = QUERY_HEADS * HEAD_SIZE
    value_at = key_at + KEY_WIDTH
    for h in range(KEY_VALUE_HEADS):
        query = jnp.concatenate(
            [full[:, (h * GROUP + g) * HEAD_SIZE:(h * GROUP + g + 1) * HEAD_SIZE]
             for g in range(GROUP)], axis=0).astype(jnp.bfloat16)
        lo, hi = h * HEAD_SIZE, (h + 1) * HEAD_SIZE

        def nearby(cache_lo, fresh_lo):
            fresh = full[:, fresh_lo:fresh_lo + HEAD_SIZE]
            fresh = jnp.concatenate(
                [fresh, jnp.zeros((near_pad - near - batch, HEAD_SIZE), jnp.float32)], axis=0)
            old = [cache_ref[0, b, :, cache_lo:cache_lo + HEAD_SIZE] for b in range(batch)]
            return jnp.concatenate(old + [fresh.astype(jnp.bfloat16)], axis=0)

        keys = nearby(lo, key_at + lo)
        near_values.append(nearby(KEY_WIDTH + lo, value_at + lo))
        far_scores.append(lax.dot_general(query, pages_ref[:, lo:hi], nt,
                                          preferred_element_type=jnp.float32))
        near_scores.append(lax.dot_general(query, keys, nt, preferred_element_type=jnp.float32))
    scale = HEAD_SIZE ** (-0.5)
    far = jnp.concatenate(far_scores, axis=0) * scale
    close = jnp.concatenate(near_scores, axis=0) * scale
    far_row = lax.rem(iota((rows, tokens), 0), batch)
    code = token_rows(own_ref[0], dest_ref, page_row_ref, count_ref, tokens // slots)
    far = jnp.where(code == far_row + visit * batch, far, -1e30)
    row = lax.rem(iota((rows, near_pad), 0), batch)
    lane = iota((rows, near_pad), 1)
    lengths = jnp.zeros((rows, near_pad), jnp.int32)
    for b in range(batch):
        lengths = jnp.where(row == b, len_ref[visit, b], lengths)
    position = lane - row * positions
    seen = (position >= 0) & (position < lengths) | (lane == near + row)
    close = jnp.where(seen, close, -1e30)
    top = jnp.maximum(jnp.max(far, axis=1, keepdims=True), jnp.max(close, axis=1, keepdims=True))
    far = jnp.exp(far - top)
    close = jnp.exp(close - top)
    denominator = jnp.sum(far, axis=1, keepdims=True) + jnp.sum(close, axis=1, keepdims=True)
    far = (far / denominator).astype(jnp.bfloat16)
    close = (close / denominator).astype(jnp.bfloat16)
    for h in range(KEY_VALUE_HEADS):
        mine = slice(h * group_rows, (h + 1) * group_rows)
        lo = KEY_WIDTH + h * HEAD_SIZE
        context = jnp.dot(far[mine], pages_ref[:, lo:lo + HEAD_SIZE],
                          preferred_element_type=jnp.float32)
        context = context + jnp.dot(close[mine], near_values[h],
                                    preferred_element_type=jnp.float32)
        for g in range(GROUP):
            at = (h * GROUP + g) * HEAD_SIZE
            out_ref[0, :, at:at + HEAD_SIZE] = context[g * batch:(g + 1) * batch].astype(
                jnp.bfloat16)


def attend(own, lengths, qkv, columns, cache, pages, arrivals, visit):
    packed = qkv.ndim == 3 and qkv.shape[2] != columns
    slots = qkv.shape[0]
    _, batch, positions, kv_width = cache.shape
    tokens = pages.shape[0]
    scalars = pl.BlockSpec(memory_space=pltpu.SMEM)
    fixed = lambda *shape: pl.BlockSpec(shape, lambda s: (0,) * len(shape))
    return pl.pallas_call(
        functools.partial(attend_kernel, visit=visit, columns=columns, packed=packed),
        out_shape=jax.ShapeDtypeStruct((1, batch, QUERY_HEADS * HEAD_SIZE), jnp.bfloat16),
        grid=(1,),
        in_specs=[
            scalars, scalars,
            pl.BlockSpec((slots, qkv.shape[1], room_for(columns)),
                         lambda s: (0, 0, kv_width // room_for(columns))) if packed
            else fixed(*qkv.shape),
            pl.BlockSpec((1, batch, positions, kv_width), lambda s: (visit, 0, 0, 0)),
            fixed(tokens, kv_width)] + [fixed(*v.shape) for v in arrivals],
        out_specs=fixed(1, batch, QUERY_HEADS * HEAD_SIZE),
        compiler_params=params(),
        name="attend",
    )(own, lengths, qkv, cache, pages, *arrivals)


def output_kernel(own_ref, *refs, slots, batch):
    pieces, (w_ref, now_ref, out_ref) = refs[:-3], refs[-3:]
    features = w_ref.shape[0]
    depth = features // 4
    acc = jnp.zeros(out_ref.shape, jnp.float32)
    for k in range(0, features, depth):
        left = jnp.concatenate(
            [piece[i, :, k:k + depth].astype(jnp.float32)
             for piece in pieces for i in range(piece.shape[0])], axis=0)
        acc = acc + jnp.dot(left.astype(jnp.bfloat16), w_ref[k:k + depth],
                            preferred_element_type=jnp.float32)
    move = arrival_rows(own_ref[0], slots, batch)
    moved = None
    for _ in range(3):
        part = acc.astype(jnp.bfloat16)
        acc = acc - part.astype(jnp.float32)
        part = jnp.dot(move, part, preferred_element_type=jnp.float32)
        moved = part if moved is None else moved + part
    out_ref[...] = (now_ref[...].astype(jnp.float32) + moved).astype(jnp.bfloat16)


def output(own, pieces, weight, now, slots):
    batch = pieces[0].shape[1]
    whole = pl.BlockSpec(memory_space=pltpu.VMEM)
    return pl.pallas_call(
        functools.partial(output_kernel, slots=slots, batch=batch),
        out_shape=jax.ShapeDtypeStruct(now.shape, jnp.bfloat16),
        in_specs=[pl.BlockSpec(memory_space=pltpu.SMEM)] + [whole] * (len(pieces) + 2),
        out_specs=whole,
        compiler_params=params(),
        name="output",
    )(own, *pieces, weight, now)


def shards(hidden_rows, norm_gain, qkv_weight, out_weight, cache_kv, cache_len, page_kv,
           page_dest, page_row, page_count):
    slots = lax.axis_size("slot")
    batch = hidden_rows.shape[1]
    rows = batch * slots
    width = hidden_rows.shape[3]
    kv_width = cache_kv.shape[5]
    own = lax.axis_index("slot").astype(jnp.int32)
    masks = [slots >> (k + 1) for k in range(slots.bit_length() - 1)]
    offsets = [0]
    for mask in masks:
        offsets = offsets + [mask ^ o for o in offsets]
    order = own ^ jnp.asarray(np.array(offsets, np.int32))
    cache = cache_kv[0, :, :, 0]
    lengths = cache_len[0, :, :, 0]
    weight_in = qkv_weight[0].T
    weight_out = out_weight[0]
    own = own.reshape(1)
    current = hidden_rows.reshape(rows, width)
    columns = weight_in.shape[0]
    arrivals = (page_dest[0], page_row[0], page_count[0])
    gains = [None] * 5
    for visit in range(CYCLE_STEPS):
        if visit == 0:
            spare = jnp.zeros((15, width), norm_gain.dtype)
            block = jnp.concatenate([current, norm_gain, spare], axis=0)[None]
            block = jnp.concatenate([block, exchange(block, masks[0])], axis=0)
            outgoing = pack(own, page_kv[0, 0], page_dest[0], room_for(columns))
            block, outgoing = lax.optimization_barrier((block, outgoing))
        else:
            block = jnp.stack([current, beyond])
        for mask in masks[1:-3]:
            block = jnp.concatenate([block, exchange(block, mask)], axis=0)
        run = functools.partial(project, order, rows, batch, weight_in)
        state = None
        groups = spread(block, masks[-3:])
        for k, names in enumerate([(0, 4), (1, 5), (2, 6)]):
            gains[k], state = run([(g, groups[g]) for g in names], gains[k], state)
        groups[3], state = lax.optimization_barrier((groups[3], state))
        groups[7] = exchange(groups[3], masks[-1])
        gains[3], state = run([(3, groups[3])], gains[3], state)
        gains[4], qkv = run([(7, groups[7])], gains[4], state, last=True,
                             outgoing=None if visit else outgoing)
        qkv = lax.all_to_all(qkv, "slot", split_axis=0, concat_axis=0, tiled=True)
        if visit == 0:
            pages = qkv.reshape(-1, qkv.shape[2])
        context = attend(own, lengths, qkv, columns, cache, pages, arrivals, visit)
        for mask in masks[:-3]:
            context = jnp.concatenate([context, exchange(context, mask)], axis=0)
        groups = spread(context, masks[-3:])
        updated = output(own, groups, weight_out, current, slots)
        current = next_segment(updated)
        if visit < CYCLE_STEPS - 1:
            beyond = next_segment(updated, masks[0])
    return current.reshape(hidden_rows.shape)


def solution(mesh):
    return jax.shard_map(
        shards,
        mesh=mesh,
        in_specs=(
            P("segment", None, None, "slot"),
            P("segment", "slot"),
            P("segment", None, "slot"),
            P("segment", None, "slot"),
            P("segment", None, None, "slot", None, None),
            P("segment", None, None, "slot"),
            P("segment", "slot", None, None, None),
            P("segment", None, None),
            P("segment", None, None),
            P("segment", None, None),
        ),
        out_specs=P("segment", None, None, "slot"),
        check_vma=False,
    )
```

```python
import functools

import jax
import jax.numpy as jnp
from jax import lax
from jax.experimental import pallas as pl
from jax.experimental.pallas import tpu as pltpu
from jax.sharding import PartitionSpec as P

QUERY_HEADS = 32
KEY_VALUE_HEADS = 4
HEAD_SIZE = 128
CYCLE_STEPS = 2
GROUP = QUERY_HEADS // KEY_VALUE_HEADS
KEY_WIDTH = KEY_VALUE_HEADS * HEAD_SIZE
LANES = 128

norm_eps = 1e-06
VMEM_LIMIT = 12 * 1024 * 1024


def params(**kw):
    return pltpu.CompilerParams(vmem_limit_bytes=VMEM_LIMIT, **kw)


def iota(shape, dim):
    return lax.broadcasted_iota(jnp.int32, shape, dim)


def exchange(block, mask):
    n = lax.axis_size("slot")
    return lax.ppermute(block, "slot", [(i, i ^ mask) for i in range(n)])


def spread(block, masks):
    across, over, core = masks
    second = exchange(block, across)
    third = exchange(block, over)
    fourth = exchange(second, over)
    groups = [block, second, third, fourth]
    return groups + [exchange(group, core) for group in groups]


def gather(block, phases):
    held = [([0], block)]
    for phase in phases:
        merged = block if len(held) == 1 else jnp.concatenate([b for _, b in held], axis=0)
        names = [m for n, _ in held for m in n]
        if phase == phases[-1] and len(phase) == 1:
            return held + [([phase[0] ^ m for m in n], exchange(b, phase[0])) for n, b in held]
        if len(held) > 1:
            held = [(names, merged)]
        held = held + [([m ^ n for n in names], exchange(merged, m)) for m in phase]


def next_segment(block, mask=0):
    n, slots = lax.axis_size("segment"), lax.axis_size("slot")
    route = [(s * slots + i, (s + 1) % n * slots + (i ^ mask)) for s in range(n)
             for i in range(slots)]
    return lax.ppermute(block, ("segment", "slot"), route)


def split_rows(index, slots, batch, slot_first):
    if slot_first:
        return index // batch, lax.rem(index, batch)
    return lax.rem(index, slots), index // slots


def slot_rows_first(slots, batch):
    rows = slots * batch
    to_slot, to_row = split_rows(iota((rows, rows), 0), slots, batch, True)
    from_slot, from_row = split_rows(iota((rows, rows), 1), slots, batch, False)
    return ((to_slot == from_slot) & (to_row == from_row)).astype(jnp.bfloat16)


def arrival_rows(own, slots, batch, arrivals):
    rows = slots * batch
    to_slot, to_row = split_rows(iota((rows, rows), 0), slots, batch, False)
    arrival, from_row = split_rows(iota((rows, rows), 1), slots, batch, True)
    from_slot = jnp.zeros_like(arrival)
    for place, mask in enumerate(arrivals):
        from_slot = jnp.where(arrival == place, mask, from_slot)
    return ((to_slot == (from_slot ^ own)) & (to_row == from_row)).astype(jnp.bfloat16)


def room_for(columns):
    return -(-(columns // 2) // LANES) * LANES


def pack_kernel(dest_ref, pages_ref, send_ref):
    own = lax.axis_index("slot")
    slots, page_tok, wide = send_ref.shape
    kv_width = pages_ref.shape[2]
    for p in range(pages_ref.shape[0]):
        send_ref[dest_ref[own, p], :, :kv_width] = pages_ref[p]
    for j in range(slots):
        send_ref[j, :, kv_width:] = jnp.zeros((page_tok, wide - kv_width), send_ref.dtype)


def pack(pages, dest, room):
    _, page_tok, kv_width = pages.shape
    whole = pl.BlockSpec(memory_space=pltpu.VMEM)
    scalars = pl.BlockSpec(memory_space=pltpu.SMEM)
    return pl.pallas_call(
        pack_kernel,
        out_shape=jax.ShapeDtypeStruct((dest.shape[0], page_tok, kv_width + room), pages.dtype),
        in_specs=[scalars, whole],
        out_specs=whole,
        compiler_params=params(),
        name="pack",
    )(dest, pages)


def project_kernel(w_ref, *refs, away, rows, carried, first, last, packed, batch):
    refs = list(refs)
    own = lax.axis_index("slot")
    x_refs = [refs.pop(0) for _ in away]
    kept = None if carried else refs.pop(0)
    acc_in, square_in = (None, None) if first else (refs.pop(0), refs.pop(0))
    if packed:
        refs.pop(0)
    if carried:
        kept = refs.pop(0)
    blocks, _, width = x_refs[0].shape
    columns, model_width = w_ref.shape
    acc = jnp.zeros((rows, columns), jnp.float32) if first else acc_in[...]
    square = jnp.zeros((rows, LANES), jnp.float32) if first else square_in[...]
    for g, masks in enumerate(away):
        for i in range(blocks):
            if carried:
                kept[g * blocks + i] = x_refs[g][i, rows:]
            x = x_refs[g][i, :rows]
            gain = kept[g * blocks + i].astype(jnp.float32)[:1]
            parts = []
            for r in range(0, width, LANES):
                part = x[:, r:r + LANES].astype(jnp.float32)
                square = square + part * part
                parts.append((part * gain[:, r:r + LANES]).astype(jnp.bfloat16))
            x = parts[0] if len(parts) == 1 else jnp.concatenate(parts, axis=1)
            here = pl.ds(pl.multiple_of((own ^ masks[i]) * width, width), width)
            acc = acc + lax.dot_general(x, w_ref[:, here], (((1,), (1,)), ((), ())),
                                        preferred_element_type=jnp.float32)
    if not last:
        refs[0][...] = acc
        refs[1][...] = square
        return
    sums = jnp.sum(square, axis=1, keepdims=True)
    out = (acc * lax.rsqrt(sums / model_width + norm_eps)).astype(jnp.bfloat16)
    slots = rows // batch
    out = jnp.dot(slot_rows_first(slots, batch), out, preferred_element_type=jnp.float32)
    half = columns // 2
    for j in range(slots):
        mine = out[j * batch:(j + 1) * batch]
        if packed:
            at = refs[0].shape[2] - room_for(columns)
            mine = jnp.concatenate([mine[:, :half], mine[:, half:]], axis=0)
            refs[0][j, :, at:at + half] = mine.astype(jnp.bfloat16)
        else:
            refs[0][j] = mine.astype(jnp.bfloat16)


def project(rows, batch, weight, groups, gains, state, last=False, outgoing=None):
    blocks, held, width = groups[0][1].shape
    columns = weight.shape[0]
    carried, first, packed = gains is None, state is None, outgoing is not None
    operands = [weight] + [x for _, x in groups] + ([] if carried else [gains])
    operands += [] if first else list(state)
    aliases = {}
    out_shape = []
    if carried:
        out_shape.append(jax.ShapeDtypeStruct((len(groups) * blocks, held - rows, width),
                                              jnp.bfloat16))
    if packed:
        aliases = {len(operands): len(out_shape)}
        operands.append(outgoing)
        out_shape.append(jax.ShapeDtypeStruct(outgoing.shape, outgoing.dtype))
    elif last:
        out_shape.append(jax.ShapeDtypeStruct((rows // batch, batch, columns), jnp.bfloat16))
    else:
        out_shape += [jax.ShapeDtypeStruct((rows, columns), jnp.float32),
                      jax.ShapeDtypeStruct((rows, LANES), jnp.float32)]
    whole = pl.BlockSpec(memory_space=pltpu.VMEM)
    work = rows * width * columns * blocks * len(groups)
    out = pl.pallas_call(
        functools.partial(project_kernel, away=[masks for masks, _ in groups], rows=rows,
                          carried=carried, first=first, last=last, packed=packed, batch=batch),
        out_shape=out_shape,
        in_specs=[whole] * len(operands),
        out_specs=[whole] * len(out_shape),
        input_output_aliases=aliases,
        compiler_params=params(),
        cost_estimate=pl.CostEstimate(flops=8 * work, bytes_accessed=2 * work // rows,
                                      transcendentals=0),
        name="project",
    )(*operands)
    if carried:
        gains, *out = out
    return gains, (out[0] if last else out)


def token_rows(own, dest_ref, row_ref, count_ref, page_tok):
    slots = dest_ref.shape[0]
    tokens = slots * page_tok
    mine = dest_ref[...] == own
    spread = (iota((slots, tokens), 1) // page_tok == iota((slots, tokens), 0)).astype(jnp.float32)

    def to_tokens(values):
        kept = jnp.where(mine, values, 0).astype(jnp.float32)
        by_token = lax.dot_general(kept, spread, (((0,), (0,)), ((), ())),
                                   preferred_element_type=jnp.float32)
        return jnp.sum(by_token, axis=0, keepdims=True)

    place = lax.rem(iota((1, tokens), 1), page_tok).astype(jnp.float32)
    live = place < to_tokens(count_ref[...])
    return jnp.where(live, to_tokens(row_ref[...]), -1.0).astype(jnp.int32)


def attend_kernel(len_ref, qkv_ref, cache_ref, pages_ref, dest_ref, page_row_ref, count_ref,
                  out_ref, *, visit, columns, packed):
    slots = qkv_ref.shape[0]
    batch, positions = cache_ref.shape[1:3]
    tokens = pages_ref.shape[0]
    pieces = []
    for j in range(slots):
        if packed:
            half = columns // 2
            piece = qkv_ref[j, :, qkv_ref.shape[2] - room_for(columns):].astype(jnp.float32)
            pieces += [piece[:batch, :half], piece[batch:2 * batch, :half]]
        else:
            pieces.append(qkv_ref[j].astype(jnp.float32))
    full = jnp.concatenate(pieces, axis=1)
    group_rows = GROUP * batch
    near = batch * positions
    near_pad = -(-(near + 16) // LANES) * LANES
    rows = KEY_VALUE_HEADS * group_rows
    nt = (((1,), (1,)), ((), ()))
    far_scores, near_scores, near_values = [], [], []
    key_at = QUERY_HEADS * HEAD_SIZE
    value_at = key_at + KEY_WIDTH
    for h in range(KEY_VALUE_HEADS):
        query = jnp.concatenate(
            [full[:, (h * GROUP + g) * HEAD_SIZE:(h * GROUP + g + 1) * HEAD_SIZE]
             for g in range(GROUP)], axis=0).astype(jnp.bfloat16)
        lo, hi = h * HEAD_SIZE, (h + 1) * HEAD_SIZE

        def nearby(cache_lo, fresh_lo):
            fresh = full[:, fresh_lo:fresh_lo + HEAD_SIZE]
            fresh = jnp.concatenate(
                [fresh, jnp.zeros((near_pad - near - batch, HEAD_SIZE), jnp.float32)], axis=0)
            old = [cache_ref[visit, b, :, cache_lo:cache_lo + HEAD_SIZE] for b in range(batch)]
            return jnp.concatenate(old + [fresh.astype(jnp.bfloat16)], axis=0)

        keys = nearby(lo, key_at + lo)
        near_values.append(nearby(KEY_WIDTH + lo, value_at + lo))
        far_scores.append(lax.dot_general(query, pages_ref[:, lo:hi], nt,
                                          preferred_element_type=jnp.float32))
        near_scores.append(lax.dot_general(query, keys, nt, preferred_element_type=jnp.float32))
    scale = HEAD_SIZE ** (-0.5)
    far = jnp.concatenate(far_scores, axis=0) * scale
    close = jnp.concatenate(near_scores, axis=0) * scale
    far_row = lax.rem(iota((rows, tokens), 0), batch)
    code = token_rows(lax.axis_index("slot"), dest_ref, page_row_ref, count_ref, tokens // slots)
    far = jnp.where(code == far_row + visit * batch, far, -1e30)
    row = lax.rem(iota((rows, near_pad), 0), batch)
    lane = iota((rows, near_pad), 1)
    lengths = jnp.zeros((rows, near_pad), jnp.int32)
    for b in range(batch):
        lengths = jnp.where(row == b, len_ref[visit:visit + 1, b:b + 1], lengths)
    position = lane - row * positions
    seen = (position >= 0) & (position < lengths) | (lane == near + row)
    close = jnp.where(seen, close, -1e30)
    top = jnp.maximum(jnp.max(far, axis=1, keepdims=True), jnp.max(close, axis=1, keepdims=True))
    far = jnp.exp(far - top)
    close = jnp.exp(close - top)
    denominator = jnp.sum(far, axis=1, keepdims=True) + jnp.sum(close, axis=1, keepdims=True)
    far = (far / denominator).astype(jnp.bfloat16)
    close = (close / denominator).astype(jnp.bfloat16)
    for h in range(KEY_VALUE_HEADS):
        mine = slice(h * group_rows, (h + 1) * group_rows)
        lo = KEY_WIDTH + h * HEAD_SIZE
        context = jnp.dot(far[mine], pages_ref[:, lo:lo + HEAD_SIZE],
                          preferred_element_type=jnp.float32)
        context = context + jnp.dot(close[mine], near_values[h],
                                    preferred_element_type=jnp.float32)
        for g in range(GROUP):
            at = (h * GROUP + g) * HEAD_SIZE
            out_ref[0, :, at:at + HEAD_SIZE] = context[g * batch:(g + 1) * batch].astype(
                jnp.bfloat16)


def attend(lengths, qkv, columns, cache, pages, arrivals, visit):
    batch = cache.shape[1]
    whole = pl.BlockSpec(memory_space=pltpu.VMEM)
    operands = [lengths, qkv, cache, pages, *arrivals]
    return pl.pallas_call(
        functools.partial(attend_kernel, visit=visit, columns=columns,
                          packed=qkv.shape[2] != columns),
        out_shape=jax.ShapeDtypeStruct((1, batch, QUERY_HEADS * HEAD_SIZE), jnp.bfloat16),
        in_specs=[whole] * len(operands),
        out_specs=whole,
        compiler_params=params(),
        name="attend",
    )(*operands)


def output_kernel(*refs, slots, batch, arrivals):
    pieces, (w_ref, now_ref, out_ref) = refs[:-3], refs[-3:]
    features = w_ref.shape[0]
    depth = features // 4
    acc = jnp.zeros(out_ref.shape, jnp.float32)
    for k in range(0, features, depth):
        left = jnp.concatenate(
            [piece[i, :, k:k + depth].astype(jnp.float32)
             for piece in pieces for i in range(piece.shape[0])], axis=0)
        acc = acc + jnp.dot(left.astype(jnp.bfloat16), w_ref[k:k + depth],
                            preferred_element_type=jnp.float32)
    move = arrival_rows(lax.axis_index("slot"), slots, batch, arrivals)
    moved = None
    for _ in range(3):
        part = acc.astype(jnp.bfloat16)
        acc = acc - part.astype(jnp.float32)
        part = jnp.dot(move, part, preferred_element_type=jnp.float32)
        moved = part if moved is None else moved + part
    out_ref[...] = (now_ref[...].astype(jnp.float32) + moved).astype(jnp.bfloat16)


def output(groups, weight, now, slots):
    arrivals = [m for n, _ in groups for m in n]
    pieces = [b for _, b in groups]
    batch = pieces[0].shape[1]
    whole = pl.BlockSpec(memory_space=pltpu.VMEM)
    return pl.pallas_call(
        functools.partial(output_kernel, slots=slots, batch=batch, arrivals=arrivals),
        out_shape=jax.ShapeDtypeStruct(now.shape, jnp.bfloat16),
        in_specs=[whole] * (len(pieces) + 2),
        out_specs=whole,
        compiler_params=params(),
        name="output",
    )(*pieces, weight, now)


def shards(hidden_rows, norm_gain, qkv_weight, out_weight, cache_kv, cache_len, page_kv,
           page_dest, page_row, page_count):
    slots = lax.axis_size("slot")
    batch = hidden_rows.shape[1]
    rows = batch * slots
    width = hidden_rows.shape[3]
    kv_width = cache_kv.shape[5]
    masks = [slots >> (k + 1) for k in range(slots.bit_length() - 1)]
    across, over, core = masks[-3:]
    phases = [[mask] for mask in masks[:-3]] + [[across ^ over, over, across], [core]]
    offsets = [masks[0], 0]
    for mask in masks[1:]:
        offsets = offsets + [mask ^ o for o in offsets]
    cache = cache_kv[0, :, :, 0]
    lengths = cache_len[0, :, :, 0]
    weight_in = qkv_weight[0].T
    weight_out = out_weight[0]
    current = hidden_rows.reshape(rows, width)
    columns = weight_in.shape[0]
    arrivals = (page_dest[0], page_row[0], page_count[0])
    gains = [None] * 5
    for visit in range(CYCLE_STEPS):
        if visit == 0:
            spare = jnp.zeros((15, width), norm_gain.dtype)
            block = jnp.concatenate([current, norm_gain, spare], axis=0)[None]
            block = jnp.concatenate([exchange(block, masks[0]), block], axis=0)
            outgoing = pack(page_kv[0, 0], page_dest[0], room_for(columns))
            block, outgoing = lax.optimization_barrier((block, outgoing))
        else:
            block = jnp.stack([beyond, current])
        for mask in masks[1:-3]:
            block = jnp.concatenate([block, exchange(block, mask)], axis=0)
        size = slots // 8
        away = [offsets[g * size:(g + 1) * size] for g in range(8)]
        run = functools.partial(project, rows, batch, weight_in)
        state = None
        groups = spread(block, masks[-3:])
        for k, names in enumerate([(0, 4), (1, 5), (2, 6)]):
            gains[k], state = run([(away[g], groups[g]) for g in names], gains[k], state)
        groups[3], state = lax.optimization_barrier((groups[3], state))
        groups[7] = exchange(groups[3], masks[-1])
        gains[3], state = run([(away[3], groups[3])], gains[3], state)
        gains[4], qkv = run([(away[7], groups[7])], gains[4], state, last=True,
                             outgoing=None if visit else outgoing)
        qkv = lax.all_to_all(qkv, "slot", split_axis=0, concat_axis=0, tiled=True)
        if visit == 0:
            pages = qkv.reshape(-1, qkv.shape[2])
        context = attend(lengths, qkv, columns, cache, pages, arrivals, visit)
        groups = gather(context, phases)
        updated = output(groups, weight_out, current, slots)
        current = next_segment(updated)
        if visit < CYCLE_STEPS - 1:
            beyond = next_segment(updated, masks[0])
    return current.reshape(hidden_rows.shape)


def solution(mesh):
    return jax.shard_map(
        shards,
        mesh=mesh,
        in_specs=(
            P("segment", None, None, "slot"),
            P("segment", "slot"),
            P("segment", None, "slot"),
            P("segment", None, "slot"),
            P("segment", None, None, "slot", None, None),
            P("segment", None, None, "slot"),
            P("segment", "slot", None, None, None),
            P("segment", None, None),
            P("segment", None, None),
            P("segment", None, None),
        ),
        out_specs=P("segment", None, None, "slot"),
        check_vma=False,
    )
```

```python
import functools

import jax
import jax.numpy as jnp
from jax import lax
from jax.experimental import pallas as pl
from jax.experimental.pallas import tpu as pltpu
from jax.sharding import PartitionSpec as P

QUERY_HEADS = 32
KEY_VALUE_HEADS = 4
HEAD_SIZE = 128
CYCLE_STEPS = 2
GROUP = QUERY_HEADS // KEY_VALUE_HEADS
KEY_WIDTH = KEY_VALUE_HEADS * HEAD_SIZE
LANES = 128

norm_eps = 1e-06
VMEM_LIMIT = 12 * 1024 * 1024


def params(**kw):
    return pltpu.CompilerParams(vmem_limit_bytes=VMEM_LIMIT, **kw)


def iota(shape, dim):
    return lax.broadcasted_iota(jnp.int32, shape, dim)


def exchange(block, mask):
    n = lax.axis_size("slot")
    return lax.ppermute(block, "slot", [(i, i ^ mask) for i in range(n)])


def gather(block, phases):
    held = [([0], block)]
    for phase in phases:
        merged = block if len(held) == 1 else jnp.concatenate([b for _, b in held], axis=0)
        names = [m for n, _ in held for m in n]
        if phase == phases[-1] and len(phase) == 1:
            return held + [([phase[0] ^ m for m in n], exchange(b, phase[0])) for n, b in held]
        if len(held) > 1:
            held = [(names, merged)]
        held = held + [([m ^ n for n in names], exchange(merged, m)) for m in phase]


def next_segment(block, mask=0):
    n, slots = lax.axis_size("segment"), lax.axis_size("slot")
    route = [(s * slots + i, (s + 1) % n * slots + (i ^ mask)) for s in range(n)
             for i in range(slots)]
    return lax.ppermute(block, ("segment", "slot"), route)


def split_rows(index, slots, batch, slot_first):
    if slot_first:
        return index // batch, lax.rem(index, batch)
    return lax.rem(index, slots), index // slots


def slot_rows_first(slots, batch):
    rows = slots * batch
    to_slot, to_row = split_rows(iota((rows, rows), 0), slots, batch, True)
    from_slot, from_row = split_rows(iota((rows, rows), 1), slots, batch, False)
    return ((to_slot == from_slot) & (to_row == from_row)).astype(jnp.bfloat16)


def arrival_rows(own, slots, batch, arrivals):
    rows = slots * batch
    to_slot, to_row = split_rows(iota((rows, rows), 0), slots, batch, False)
    arrival, from_row = split_rows(iota((rows, rows), 1), slots, batch, True)
    from_slot = jnp.zeros_like(arrival)
    for place, mask in enumerate(arrivals):
        from_slot = jnp.where(arrival == place, mask, from_slot)
    return ((to_slot == (from_slot ^ own)) & (to_row == from_row)).astype(jnp.bfloat16)


def room_for(columns):
    return -(-(columns // 2) // LANES) * LANES


def pack_kernel(dest_ref, pages_ref, send_ref):
    own = lax.axis_index("slot")
    slots, page_tok, wide = send_ref.shape
    kv_width = pages_ref.shape[2]
    for p in range(pages_ref.shape[0]):
        send_ref[dest_ref[own, p], :, :kv_width] = pages_ref[p]
    for j in range(slots):
        send_ref[j, :, kv_width:] = jnp.zeros((page_tok, wide - kv_width), send_ref.dtype)


def pack(pages, dest, room):
    _, page_tok, kv_width = pages.shape
    whole = pl.BlockSpec(memory_space=pltpu.VMEM)
    scalars = pl.BlockSpec(memory_space=pltpu.SMEM)
    return pl.pallas_call(
        pack_kernel,
        out_shape=jax.ShapeDtypeStruct((dest.shape[0], page_tok, kv_width + room), pages.dtype),
        in_specs=[scalars, whole],
        out_specs=whole,
        compiler_params=params(),
        name="pack",
    )(dest, pages)


def project_kernel(w_ref, *refs, away, rows, carried, first, last, packed, batch):
    refs = list(refs)
    own = lax.axis_index("slot")
    x_refs = [refs.pop(0) for _ in away]
    kept = None if carried else refs.pop(0)
    acc_in, square_in = (None, None) if first else (refs.pop(0), refs.pop(0))
    if packed:
        refs.pop(0)
    if carried:
        kept = refs.pop(0)
    blocks, _, width = x_refs[0].shape
    columns, model_width = w_ref.shape
    acc = jnp.zeros((rows, columns), jnp.float32) if first else acc_in[...]
    square = jnp.zeros((rows, LANES), jnp.float32) if first else square_in[...]
    for g, masks in enumerate(away):
        for i in range(blocks):
            if carried:
                kept[g * blocks + i] = x_refs[g][i, rows:]
            x = x_refs[g][i, :rows]
            gain = kept[g * blocks + i].astype(jnp.float32)[:1]
            parts = []
            for r in range(0, width, LANES):
                part = x[:, r:r + LANES].astype(jnp.float32)
                square = square + part * part
                parts.append((part * gain[:, r:r + LANES]).astype(jnp.bfloat16))
            x = parts[0] if len(parts) == 1 else jnp.concatenate(parts, axis=1)
            here = pl.ds(pl.multiple_of((own ^ masks[i]) * width, width), width)
            acc = acc + lax.dot_general(x, w_ref[:, here], (((1,), (1,)), ((), ())),
                                        preferred_element_type=jnp.float32)
    if not last:
        refs[0][...] = acc
        refs[1][...] = square
        return
    sums = jnp.sum(square, axis=1, keepdims=True)
    out = (acc * lax.rsqrt(sums / model_width + norm_eps)).astype(jnp.bfloat16)
    slots = rows // batch
    out = jnp.dot(slot_rows_first(slots, batch), out, preferred_element_type=jnp.float32)
    half = columns // 2
    for j in range(slots):
        mine = out[j * batch:(j + 1) * batch]
        if packed:
            at = refs[0].shape[2] - room_for(columns)
            mine = jnp.concatenate([mine[:, :half], mine[:, half:]], axis=0)
            refs[0][j, :, at:at + half] = mine.astype(jnp.bfloat16)
        else:
            refs[0][j] = mine.astype(jnp.bfloat16)


def project(rows, batch, weight, groups, gains, state, last=False, outgoing=None):
    blocks, held, width = groups[0][1].shape
    columns = weight.shape[0]
    carried, first, packed = gains is None, state is None, outgoing is not None
    operands = [weight] + [x for _, x in groups] + ([] if carried else [gains])
    operands += [] if first else list(state)
    aliases = {}
    out_shape = []
    if carried:
        out_shape.append(jax.ShapeDtypeStruct((len(groups) * blocks, held - rows, width),
                                              jnp.bfloat16))
    if packed:
        aliases = {len(operands): len(out_shape)}
        operands.append(outgoing)
        out_shape.append(jax.ShapeDtypeStruct(outgoing.shape, outgoing.dtype))
    elif last:
        out_shape.append(jax.ShapeDtypeStruct((rows // batch, batch, columns), jnp.bfloat16))
    else:
        out_shape += [jax.ShapeDtypeStruct((rows, columns), jnp.float32),
                      jax.ShapeDtypeStruct((rows, LANES), jnp.float32)]
    whole = pl.BlockSpec(memory_space=pltpu.VMEM)
    work = rows * width * columns * blocks * len(groups)
    out = pl.pallas_call(
        functools.partial(project_kernel, away=[masks for masks, _ in groups], rows=rows,
                          carried=carried, first=first, last=last, packed=packed, batch=batch),
        out_shape=out_shape,
        in_specs=[whole] * len(operands),
        out_specs=[whole] * len(out_shape),
        input_output_aliases=aliases,
        compiler_params=params(),
        cost_estimate=pl.CostEstimate(flops=8 * work, bytes_accessed=2 * work // rows,
                                      transcendentals=0),
        name="project",
    )(*operands)
    if carried:
        gains, *out = out
    return gains, (out[0] if last else out)


def token_rows(own, dest_ref, row_ref, count_ref, page_tok):
    slots = dest_ref.shape[0]
    tokens = slots * page_tok
    mine = dest_ref[...] == own
    spread = (iota((slots, tokens), 1) // page_tok == iota((slots, tokens), 0)).astype(jnp.float32)

    def to_tokens(values):
        kept = jnp.where(mine, values, 0).astype(jnp.float32)
        by_token = lax.dot_general(kept, spread, (((0,), (0,)), ((), ())),
                                   preferred_element_type=jnp.float32)
        return jnp.sum(by_token, axis=0, keepdims=True)

    place = lax.rem(iota((1, tokens), 1), page_tok).astype(jnp.float32)
    live = place < to_tokens(count_ref[...])
    return jnp.where(live, to_tokens(row_ref[...]), -1.0).astype(jnp.int32)


def attend_kernel(len_ref, qkv_ref, cache_ref, pages_ref, dest_ref, page_row_ref, count_ref,
                  out_ref, *, visit, columns, packed):
    slots = qkv_ref.shape[0]
    batch, positions = cache_ref.shape[1:3]
    tokens = pages_ref.shape[0]
    pieces = []
    for j in range(slots):
        if packed:
            half = columns // 2
            piece = qkv_ref[j, :, qkv_ref.shape[2] - room_for(columns):].astype(jnp.float32)
            pieces += [piece[:batch, :half], piece[batch:2 * batch, :half]]
        else:
            pieces.append(qkv_ref[j].astype(jnp.float32))
    full = jnp.concatenate(pieces, axis=1)
    group_rows = GROUP * batch
    near = batch * positions
    near_pad = -(-(near + 16) // LANES) * LANES
    rows = KEY_VALUE_HEADS * group_rows
    nt = (((1,), (1,)), ((), ()))
    far_scores, near_scores, near_values = [], [], []
    key_at = QUERY_HEADS * HEAD_SIZE
    value_at = key_at + KEY_WIDTH
    for h in range(KEY_VALUE_HEADS):
        query = jnp.concatenate(
            [full[:, (h * GROUP + g) * HEAD_SIZE:(h * GROUP + g + 1) * HEAD_SIZE]
             for g in range(GROUP)], axis=0).astype(jnp.bfloat16)
        lo, hi = h * HEAD_SIZE, (h + 1) * HEAD_SIZE

        def nearby(cache_lo, fresh_lo):
            fresh = full[:, fresh_lo:fresh_lo + HEAD_SIZE]
            fresh = jnp.concatenate(
                [fresh, jnp.zeros((near_pad - near - batch, HEAD_SIZE), jnp.float32)], axis=0)
            old = [cache_ref[visit, b, :, cache_lo:cache_lo + HEAD_SIZE] for b in range(batch)]
            return jnp.concatenate(old + [fresh.astype(jnp.bfloat16)], axis=0)

        keys = nearby(lo, key_at + lo)
        near_values.append(nearby(KEY_WIDTH + lo, value_at + lo))
        far_scores.append(lax.dot_general(query, pages_ref[:, lo:hi], nt,
                                          preferred_element_type=jnp.float32))
        near_scores.append(lax.dot_general(query, keys, nt, preferred_element_type=jnp.float32))
    scale = HEAD_SIZE ** (-0.5)
    far = jnp.concatenate(far_scores, axis=0) * scale
    close = jnp.concatenate(near_scores, axis=0) * scale
    far_row = lax.rem(iota((rows, tokens), 0), batch)
    code = token_rows(lax.axis_index("slot"), dest_ref, page_row_ref, count_ref, tokens // slots)
    far = jnp.where(code == far_row + visit * batch, far, -1e30)
    row = lax.rem(iota((rows, near_pad), 0), batch)
    lane = iota((rows, near_pad), 1)
    lengths = jnp.zeros((rows, near_pad), jnp.int32)
    for b in range(batch):
        lengths = jnp.where(row == b, len_ref[visit:visit + 1, b:b + 1], lengths)
    position = lane - row * positions
    seen = (position >= 0) & (position < lengths) | (lane == near + row)
    close = jnp.where(seen, close, -1e30)
    top = jnp.maximum(jnp.max(far, axis=1, keepdims=True), jnp.max(close, axis=1, keepdims=True))
    far = jnp.exp(far - top)
    close = jnp.exp(close - top)
    denominator = jnp.sum(far, axis=1, keepdims=True) + jnp.sum(close, axis=1, keepdims=True)
    far = (far / denominator).astype(jnp.bfloat16)
    close = (close / denominator).astype(jnp.bfloat16)
    for h in range(KEY_VALUE_HEADS):
        mine = slice(h * group_rows, (h + 1) * group_rows)
        lo = KEY_WIDTH + h * HEAD_SIZE
        context = jnp.dot(far[mine], pages_ref[:, lo:lo + HEAD_SIZE],
                          preferred_element_type=jnp.float32)
        context = context + jnp.dot(close[mine], near_values[h],
                                    preferred_element_type=jnp.float32)
        for g in range(GROUP):
            at = (h * GROUP + g) * HEAD_SIZE
            out_ref[0, :, at:at + HEAD_SIZE] = context[g * batch:(g + 1) * batch].astype(
                jnp.bfloat16)


def attend(lengths, qkv, columns, cache, pages, arrivals, visit):
    batch = cache.shape[1]
    whole = pl.BlockSpec(memory_space=pltpu.VMEM)
    operands = [lengths, qkv, cache, pages, *arrivals]
    return pl.pallas_call(
        functools.partial(attend_kernel, visit=visit, columns=columns,
                          packed=qkv.shape[2] != columns),
        out_shape=jax.ShapeDtypeStruct((1, batch, QUERY_HEADS * HEAD_SIZE), jnp.bfloat16),
        in_specs=[whole] * len(operands),
        out_specs=whole,
        compiler_params=params(),
        name="attend",
    )(*operands)


def output_kernel(*refs, slots, batch, arrivals):
    pieces, (w_ref, now_ref, out_ref) = refs[:-3], refs[-3:]
    features = w_ref.shape[0]
    depth = features // 4
    acc = jnp.zeros(out_ref.shape, jnp.float32)
    for k in range(0, features, depth):
        left = jnp.concatenate(
            [piece[i, :, k:k + depth].astype(jnp.float32)
             for piece in pieces for i in range(piece.shape[0])], axis=0)
        acc = acc + jnp.dot(left.astype(jnp.bfloat16), w_ref[k:k + depth],
                            preferred_element_type=jnp.float32)
    move = arrival_rows(lax.axis_index("slot"), slots, batch, arrivals)
    moved = None
    for _ in range(3):
        part = acc.astype(jnp.bfloat16)
        acc = acc - part.astype(jnp.float32)
        part = jnp.dot(move, part, preferred_element_type=jnp.float32)
        moved = part if moved is None else moved + part
    out_ref[...] = (now_ref[...].astype(jnp.float32) + moved).astype(jnp.bfloat16)


def output(groups, weight, now, slots):
    arrivals = [m for n, _ in groups for m in n]
    pieces = [b for _, b in groups]
    batch = pieces[0].shape[1]
    whole = pl.BlockSpec(memory_space=pltpu.VMEM)
    return pl.pallas_call(
        functools.partial(output_kernel, slots=slots, batch=batch, arrivals=arrivals),
        out_shape=jax.ShapeDtypeStruct(now.shape, jnp.bfloat16),
        in_specs=[whole] * (len(pieces) + 2),
        out_specs=whole,
        compiler_params=params(),
        name="output",
    )(*pieces, weight, now)


def shards(hidden_rows, norm_gain, qkv_weight, out_weight, cache_kv, cache_len, page_kv,
           page_dest, page_row, page_count):
    slots = lax.axis_size("slot")
    batch = hidden_rows.shape[1]
    rows = batch * slots
    width = hidden_rows.shape[3]
    kv_width = cache_kv.shape[5]
    masks = [slots >> (k + 1) for k in range(slots.bit_length() - 1)]
    across, over, core = masks[-3:]
    phases = [[mask] for mask in masks[:-3]] + [[across ^ over, over, across], [core]]
    offsets = [masks[0], 0]
    for mask in masks[1:]:
        offsets = offsets + [mask ^ o for o in offsets]
    cache = cache_kv[0, :, :, 0]
    lengths = cache_len[0, :, :, 0]
    weight_in = qkv_weight[0].T
    weight_out = out_weight[0]
    current = hidden_rows.reshape(rows, width)
    columns = weight_in.shape[0]
    arrivals = (page_dest[0], page_row[0], page_count[0])
    gains = [None] * 5
    for visit in range(CYCLE_STEPS):
        if visit == 0:
            spare = jnp.zeros((15, width), norm_gain.dtype)
            block = jnp.concatenate([current, norm_gain, spare], axis=0)[None]
            block = jnp.concatenate([exchange(block, masks[0]), block], axis=0)
            outgoing = pack(page_kv[0, 0], page_dest[0], room_for(columns))
            block, outgoing = lax.optimization_barrier((block, outgoing))
        else:
            block = jnp.stack([beyond, current])
        for mask in masks[1:-3]:
            block = jnp.concatenate([block, exchange(block, mask)], axis=0)
        size = slots // 8
        away = [offsets[g * size:(g + 1) * size] for g in range(8)]
        run = functools.partial(project, rows, batch, weight_in)
        second = exchange(block, across)
        third = exchange(block, over)
        pair = exchange(block, core)
        fourth = exchange(second, over)
        gains[0], state = run([(away[0], block), (away[4], pair)], gains[0], None)
        gains[1], state = run([(away[1], second), (away[2], third)], gains[1], state)
        second, third, state = lax.optimization_barrier((second, third, state))
        others = [exchange(x, core) for x in (second, third)]
        fourth, state = lax.optimization_barrier((fourth, state))
        corner = exchange(fourth, core)
        gains[3], state = run([(away[3], fourth), *zip(away[5:7], others)], gains[3], state)
        gains[4], qkv = run([(away[7], corner)], gains[4], state, last=True,
                             outgoing=None if visit else outgoing)
        qkv = lax.all_to_all(qkv, "slot", split_axis=0, concat_axis=0, tiled=True)
        if visit == 0:
            pages = qkv.reshape(-1, qkv.shape[2])
        context = attend(lengths, qkv, columns, cache, pages, arrivals, visit)
        groups = gather(context, phases)
        updated = output(groups, weight_out, current, slots)
        current = next_segment(updated)
        if visit < CYCLE_STEPS - 1:
            beyond = next_segment(updated, masks[0])
    return current.reshape(hidden_rows.shape)


def solution(mesh):
    return jax.shard_map(
        shards,
        mesh=mesh,
        in_specs=(
            P("segment", None, None, "slot"),
            P("segment", "slot"),
            P("segment", None, "slot"),
            P("segment", None, "slot"),
            P("segment", None, None, "slot", None, None),
            P("segment", None, None, "slot"),
            P("segment", "slot", None, None, None),
            P("segment", None, None),
            P("segment", None, None),
            P("segment", None, None),
        ),
        out_specs=P("segment", None, None, "slot"),
        check_vma=False,
    )
```

```python
import functools

import jax
import jax.numpy as jnp
from jax import lax
from jax.experimental import pallas as pl
from jax.experimental.pallas import tpu as pltpu
from jax.sharding import PartitionSpec as P

QUERY_HEADS = 32
KEY_VALUE_HEADS = 4
HEAD_SIZE = 128
CYCLE_STEPS = 2
GROUP = QUERY_HEADS // KEY_VALUE_HEADS
KEY_WIDTH = KEY_VALUE_HEADS * HEAD_SIZE
LANES = 128

norm_eps = 1e-06
VMEM_LIMIT = 12 * 1024 * 1024


def params(**kw):
    return pltpu.CompilerParams(vmem_limit_bytes=VMEM_LIMIT, **kw)


def iota(shape, dim):
    return lax.broadcasted_iota(jnp.int32, shape, dim)


def exchange(block, mask):
    n = lax.axis_size("slot")
    return lax.ppermute(block, "slot", [(i, i ^ mask) for i in range(n)])


def gather(block, phases):
    held = [([0], block)]
    for phase in phases:
        merged = block if len(held) == 1 else jnp.concatenate([b for _, b in held], axis=0)
        names = [m for n, _ in held for m in n]
        if phase == phases[-1]:
            core = phase[0]
            for some in [[0, 3], [2], [1]]:
                both = [held[k] for k in some]
                away = [core ^ m for n, _ in both for m in n]
                both = [b for _, b in both]
                both = both[0] if len(both) == 1 else jnp.concatenate(both, axis=0)
                held = held + [(away, exchange(both, core))]
            return held
        if len(held) > 1:
            held = [(names, merged)]
        held = held + [([m ^ n for n in names], exchange(merged, m)) for m in phase]


def next_segment(block, mask=0):
    n, slots = lax.axis_size("segment"), lax.axis_size("slot")
    route = [(s * slots + i, (s + 1) % n * slots + (i ^ mask)) for s in range(n)
             for i in range(slots)]
    return lax.ppermute(block, ("segment", "slot"), route)


def split_rows(index, slots, batch, slot_first):
    if slot_first:
        return index // batch, lax.rem(index, batch)
    return lax.rem(index, slots), index // slots


def slot_rows_first(slots, batch):
    rows = slots * batch
    to_slot, to_row = split_rows(iota((rows, rows), 0), slots, batch, True)
    from_slot, from_row = split_rows(iota((rows, rows), 1), slots, batch, False)
    return ((to_slot == from_slot) & (to_row == from_row)).astype(jnp.bfloat16)


def arrival_rows(own, slots, batch, arrivals):
    rows = slots * batch
    to_slot, to_row = split_rows(iota((rows, rows), 0), slots, batch, False)
    arrival, from_row = split_rows(iota((rows, rows), 1), slots, batch, True)
    from_slot = jnp.zeros_like(arrival)
    for place, mask in enumerate(arrivals):
        from_slot = jnp.where(arrival == place, mask, from_slot)
    return ((to_slot == (from_slot ^ own)) & (to_row == from_row)).astype(jnp.bfloat16)


def room_for(columns):
    return -(-(columns // 2) // LANES) * LANES


def pack_kernel(dest_ref, pages_ref, x_ref, gain_ref, send_ref, x_out, gain_out):
    x_out[...] = x_ref[...]
    gain_out[...] = gain_ref[...]
    own = lax.axis_index("slot")
    slots, page_tok, wide = send_ref.shape
    kv_width = pages_ref.shape[2]
    for p in range(pages_ref.shape[0]):
        send_ref[dest_ref[own, p], :, :kv_width] = pages_ref[p]
    for j in range(slots):
        send_ref[j, :, kv_width:] = jnp.zeros((page_tok, wide - kv_width), send_ref.dtype)


def pack(pages, dest, x, gain, room):
    _, page_tok, kv_width = pages.shape
    whole = pl.BlockSpec(memory_space=pltpu.VMEM)
    scalars = pl.BlockSpec(memory_space=pltpu.SMEM)
    return pl.pallas_call(
        pack_kernel,
        out_shape=[
            jax.ShapeDtypeStruct((dest.shape[0], page_tok, kv_width + room), pages.dtype),
            jax.ShapeDtypeStruct(x.shape, x.dtype),
            jax.ShapeDtypeStruct(gain.shape, gain.dtype),
        ],
        in_specs=[scalars] + [whole] * 3,
        out_specs=[whole] * 3,
        compiler_params=params(),
        name="pack",
    )(dest, pages, x, gain)


def project_kernel(w_ref, *refs, away, rows, carried, first, last, packed, batch):
    refs = list(refs)
    own = lax.axis_index("slot")
    x_refs = [refs.pop(0) for _ in away]
    kept = None if carried else refs.pop(0)
    acc_in, square_in = (None, None) if first else (refs.pop(0), refs.pop(0))
    if packed:
        refs.pop(0)
    if carried:
        kept = refs.pop(0)
    blocks, width = len(away[0]), x_refs[0].shape[1]
    columns, model_width = w_ref.shape
    acc = jnp.zeros((rows, columns), jnp.float32) if first else acc_in[...]
    square = jnp.zeros((rows, LANES), jnp.float32) if first else square_in[...]
    for g, masks in enumerate(away):
        if carried:
            kept[g] = x_refs[g][blocks * rows:]
        gains = kept[g].astype(jnp.float32)
        for i in range(blocks):
            x = x_refs[g][i * rows:(i + 1) * rows]
            gain = gains[i:i + 1]
            parts = []
            for r in range(0, width, LANES):
                part = x[:, r:r + LANES].astype(jnp.float32)
                square = square + part * part
                parts.append((part * gain[:, r:r + LANES]).astype(jnp.bfloat16))
            x = parts[0] if len(parts) == 1 else jnp.concatenate(parts, axis=1)
            here = pl.ds(pl.multiple_of((own ^ masks[i]) * width, width), width)
            acc = acc + lax.dot_general(x, w_ref[:, here], (((1,), (1,)), ((), ())),
                                        preferred_element_type=jnp.float32)
    if not last:
        refs[0][...] = acc
        refs[1][...] = square
        return
    sums = jnp.sum(square, axis=1, keepdims=True)
    out = (acc * lax.rsqrt(sums / model_width + norm_eps)).astype(jnp.bfloat16)
    slots = rows // batch
    out = jnp.dot(slot_rows_first(slots, batch), out, preferred_element_type=jnp.float32)
    half = columns // 2
    for j in range(slots):
        mine = out[j * batch:(j + 1) * batch]
        if packed:
            at = refs[0].shape[2] - room_for(columns)
            mine = jnp.concatenate([mine[:, :half], mine[:, half:]], axis=0)
            refs[0][j, :, at:at + half] = mine.astype(jnp.bfloat16)
        else:
            refs[0][j] = mine.astype(jnp.bfloat16)


def project(rows, batch, weight, groups, gains, state, last=False, outgoing=None):
    blocks, (held, width) = len(groups[0][0]), groups[0][1].shape
    columns = weight.shape[0]
    carried, first, packed = gains is None, state is None, outgoing is not None
    operands = [weight] + [x for _, x in groups] + ([] if carried else [gains])
    operands += [] if first else list(state)
    aliases = {}
    out_shape = []
    if carried:
        out_shape.append(jax.ShapeDtypeStruct((len(groups), held - blocks * rows, width),
                                              jnp.bfloat16))
    if packed:
        aliases = {len(operands): len(out_shape)}
        operands.append(outgoing)
        out_shape.append(jax.ShapeDtypeStruct(outgoing.shape, outgoing.dtype))
    elif last:
        out_shape.append(jax.ShapeDtypeStruct((rows // batch, batch, columns), jnp.bfloat16))
    else:
        out_shape += [jax.ShapeDtypeStruct((rows, columns), jnp.float32),
                      jax.ShapeDtypeStruct((rows, LANES), jnp.float32)]
    whole = pl.BlockSpec(memory_space=pltpu.VMEM)
    work = rows * width * columns * blocks * len(groups)
    out = pl.pallas_call(
        functools.partial(project_kernel, away=[masks for masks, _ in groups], rows=rows,
                          carried=carried, first=first, last=last, packed=packed, batch=batch),
        out_shape=out_shape,
        in_specs=[whole] * len(operands),
        out_specs=[whole] * len(out_shape),
        input_output_aliases=aliases,
        compiler_params=params(),
        cost_estimate=pl.CostEstimate(flops=8 * work, bytes_accessed=2 * work // rows,
                                      transcendentals=0),
        name="project",
    )(*operands)
    if carried:
        gains, *out = out
    return gains, (out[0] if last else out)


def token_rows(own, dest_ref, row_ref, count_ref, page_tok):
    slots = dest_ref.shape[0]
    tokens = slots * page_tok
    mine = dest_ref[...] == own
    spread = (iota((slots, tokens), 1) // page_tok == iota((slots, tokens), 0)).astype(jnp.float32)

    def to_tokens(values):
        kept = jnp.where(mine, values, 0).astype(jnp.float32)
        by_token = lax.dot_general(kept, spread, (((0,), (0,)), ((), ())),
                                   preferred_element_type=jnp.float32)
        return jnp.sum(by_token, axis=0, keepdims=True)

    place = lax.rem(iota((1, tokens), 1), page_tok).astype(jnp.float32)
    live = place < to_tokens(count_ref[...])
    return jnp.where(live, to_tokens(row_ref[...]), -1.0).astype(jnp.int32)


def attend_kernel(len_ref, qkv_ref, cache_ref, pages_ref, dest_ref, page_row_ref, count_ref,
                  out_ref, *, visit, columns, packed):
    slots = qkv_ref.shape[0]
    batch, positions = cache_ref.shape[1:3]
    tokens = pages_ref.shape[0]
    pieces = []
    for j in range(slots):
        if packed:
            half = columns // 2
            piece = qkv_ref[j, :, qkv_ref.shape[2] - room_for(columns):].astype(jnp.float32)
            pieces += [piece[:batch, :half], piece[batch:2 * batch, :half]]
        else:
            pieces.append(qkv_ref[j].astype(jnp.float32))
    full = jnp.concatenate(pieces, axis=1)
    group_rows = GROUP * batch
    near = batch * positions
    near_pad = -(-(near + 16) // LANES) * LANES
    rows = KEY_VALUE_HEADS * group_rows
    nt = (((1,), (1,)), ((), ()))
    far_scores, near_scores, near_values = [], [], []
    key_at = QUERY_HEADS * HEAD_SIZE
    value_at = key_at + KEY_WIDTH
    for h in range(KEY_VALUE_HEADS):
        query = jnp.concatenate(
            [full[:, (h * GROUP + g) * HEAD_SIZE:(h * GROUP + g + 1) * HEAD_SIZE]
             for g in range(GROUP)], axis=0).astype(jnp.bfloat16)
        lo, hi = h * HEAD_SIZE, (h + 1) * HEAD_SIZE

        def nearby(cache_lo, fresh_lo):
            fresh = full[:, fresh_lo:fresh_lo + HEAD_SIZE]
            fresh = jnp.concatenate(
                [fresh, jnp.zeros((near_pad - near - batch, HEAD_SIZE), jnp.float32)], axis=0)
            old = [cache_ref[visit, b, :, cache_lo:cache_lo + HEAD_SIZE] for b in range(batch)]
            return jnp.concatenate(old + [fresh.astype(jnp.bfloat16)], axis=0)

        keys = nearby(lo, key_at + lo)
        near_values.append(nearby(KEY_WIDTH + lo, value_at + lo))
        far_scores.append(lax.dot_general(query, pages_ref[:, lo:hi], nt,
                                          preferred_element_type=jnp.float32))
        near_scores.append(lax.dot_general(query, keys, nt, preferred_element_type=jnp.float32))
    scale = HEAD_SIZE ** (-0.5)
    far = jnp.concatenate(far_scores, axis=0) * scale
    close = jnp.concatenate(near_scores, axis=0) * scale
    far_row = lax.rem(iota((rows, tokens), 0), batch)
    code = token_rows(lax.axis_index("slot"), dest_ref, page_row_ref, count_ref, tokens // slots)
    far = jnp.where(code == far_row + visit * batch, far, -1e30)
    row = lax.rem(iota((rows, near_pad), 0), batch)
    lane = iota((rows, near_pad), 1)
    lengths = jnp.zeros((rows, near_pad), jnp.int32)
    for b in range(batch):
        lengths = jnp.where(row == b, len_ref[visit:visit + 1, b:b + 1], lengths)
    position = lane - row * positions
    seen = (position >= 0) & (position < lengths) | (lane == near + row)
    close = jnp.where(seen, close, -1e30)
    top = jnp.maximum(jnp.max(far, axis=1, keepdims=True), jnp.max(close, axis=1, keepdims=True))
    far = jnp.exp(far - top)
    close = jnp.exp(close - top)
    denominator = jnp.sum(far, axis=1, keepdims=True) + jnp.sum(close, axis=1, keepdims=True)
    far = (far / denominator).astype(jnp.bfloat16)
    close = (close / denominator).astype(jnp.bfloat16)
    for h in range(KEY_VALUE_HEADS):
        mine = slice(h * group_rows, (h + 1) * group_rows)
        lo = KEY_WIDTH + h * HEAD_SIZE
        context = jnp.dot(far[mine], pages_ref[:, lo:lo + HEAD_SIZE],
                          preferred_element_type=jnp.float32)
        context = context + jnp.dot(close[mine], near_values[h],
                                    preferred_element_type=jnp.float32)
        for g in range(GROUP):
            at = (h * GROUP + g) * HEAD_SIZE
            out_ref[0, :, at:at + HEAD_SIZE] = context[g * batch:(g + 1) * batch].astype(
                jnp.bfloat16)


def attend(lengths, qkv, columns, cache, pages, arrivals, visit):
    batch = cache.shape[1]
    whole = pl.BlockSpec(memory_space=pltpu.VMEM)
    operands = [lengths, qkv, cache, pages, *arrivals]
    return pl.pallas_call(
        functools.partial(attend_kernel, visit=visit, columns=columns,
                          packed=qkv.shape[2] != columns),
        out_shape=jax.ShapeDtypeStruct((1, batch, QUERY_HEADS * HEAD_SIZE), jnp.bfloat16),
        in_specs=[whole] * len(operands),
        out_specs=whole,
        compiler_params=params(),
        name="attend",
    )(*operands)


def output_kernel(*refs, slots, batch, arrivals):
    pieces, (w_ref, now_ref, out_ref) = refs[:-3], refs[-3:]
    features = w_ref.shape[0]
    depth = features // 4
    acc = jnp.zeros(out_ref.shape, jnp.float32)
    for k in range(0, features, depth):
        left = jnp.concatenate(
            [piece[i, :, k:k + depth].astype(jnp.float32)
             for piece in pieces for i in range(piece.shape[0])], axis=0)
        acc = acc + jnp.dot(left.astype(jnp.bfloat16), w_ref[k:k + depth],
                            preferred_element_type=jnp.float32)
    move = arrival_rows(lax.axis_index("slot"), slots, batch, arrivals)
    moved = None
    for _ in range(3):
        part = acc.astype(jnp.bfloat16)
        acc = acc - part.astype(jnp.float32)
        part = jnp.dot(move, part, preferred_element_type=jnp.float32)
        moved = part if moved is None else moved + part
    out_ref[...] = (now_ref[...].astype(jnp.float32) + moved).astype(jnp.bfloat16)


def output(groups, weight, now, slots):
    arrivals = [m for n, _ in groups for m in n]
    pieces = [b for _, b in groups]
    batch = pieces[0].shape[1]
    whole = pl.BlockSpec(memory_space=pltpu.VMEM)
    return pl.pallas_call(
        functools.partial(output_kernel, slots=slots, batch=batch, arrivals=arrivals),
        out_shape=jax.ShapeDtypeStruct(now.shape, jnp.bfloat16),
        in_specs=[whole] * (len(pieces) + 2),
        out_specs=whole,
        compiler_params=params(),
        name="output",
    )(*pieces, weight, now)


def shards(hidden_rows, norm_gain, qkv_weight, out_weight, cache_kv, cache_len, page_kv,
           page_dest, page_row, page_count):
    slots = lax.axis_size("slot")
    batch = hidden_rows.shape[1]
    rows = batch * slots
    width = hidden_rows.shape[3]
    kv_width = cache_kv.shape[5]
    masks = [slots >> (k + 1) for k in range(slots.bit_length() - 1)]
    across, over, core = masks[-3:]
    phases = [[mask] for mask in masks[:-3]] + [[across, over, across ^ over], [core]]
    offsets = [masks[0], 0]
    for mask in masks[1:]:
        offsets = offsets + [mask ^ o for o in offsets]
    cache = cache_kv[0, :, :, 0]
    lengths = cache_len[0, :, :, 0]
    weight_in = qkv_weight[0].T
    weight_out = out_weight[0]
    current = hidden_rows.reshape(rows, width)
    columns = weight_in.shape[0]
    arrivals = (page_dest[0], page_row[0], page_count[0])
    gains = [None] * 5
    for visit in range(CYCLE_STEPS):
        if visit == 0:
            block, gain = exchange(current, masks[0]), exchange(norm_gain, masks[0])
            outgoing, current, mine = pack(page_kv[0, 0], page_dest[0], current, norm_gain,
                                           room_for(columns))
            block, gain = jnp.concatenate([block, current]), jnp.concatenate([gain, mine])
        else:
            block = jnp.concatenate([beyond, current])
        for mask in masks[1:-3]:
            block = jnp.concatenate([block, exchange(block, mask)])
            if visit == 0:
                gain = jnp.concatenate([gain, exchange(gain, mask)])
        if visit == 0:
            spare = jnp.zeros((-gain.shape[0] % 16, width), gain.dtype)
            block = jnp.concatenate([block, gain, spare])
        size = slots // 8
        away = [offsets[g * size:(g + 1) * size] for g in range(8)]
        run = functools.partial(project, rows, batch, weight_in)
        second = exchange(block, across)
        third = exchange(block, over)
        pair = exchange(block, core)
        fourth = exchange(second, over)
        gains[0], state = run([(away[0], block), (away[4], pair)], gains[0], None)
        gains[1], state = run([(away[1], second), (away[2], third)], gains[1], state)
        second, third, state = lax.optimization_barrier((second, third, state))
        others = [exchange(x, core) for x in (second, third)]
        fourth, state = lax.optimization_barrier((fourth, state))
        corner = exchange(fourth, core)
        gains[3], state = run([(away[3], fourth), *zip(away[5:7], others)], gains[3], state)
        gains[4], qkv = run([(away[7], corner)], gains[4], state, last=True,
                             outgoing=None if visit else outgoing)
        qkv = lax.all_to_all(qkv, "slot", split_axis=0, concat_axis=0, tiled=True)
        if visit == 0:
            pages = qkv.reshape(-1, qkv.shape[2])
        context = attend(lengths, qkv, columns, cache, pages, arrivals, visit)
        groups = gather(context, phases)
        updated = output(groups, weight_out, current, slots)
        current = next_segment(updated)
        if visit < CYCLE_STEPS - 1:
            beyond = next_segment(updated, masks[0])
    return current.reshape(hidden_rows.shape)


def solution(mesh):
    return jax.shard_map(
        shards,
        mesh=mesh,
        in_specs=(
            P("segment", None, None, "slot"),
            P("segment", "slot"),
            P("segment", None, "slot"),
            P("segment", None, "slot"),
            P("segment", None, None, "slot", None, None),
            P("segment", None, None, "slot"),
            P("segment", "slot", None, None, None),
            P("segment", None, None),
            P("segment", None, None),
            P("segment", None, None),
        ),
        out_specs=P("segment", None, None, "slot"),
        check_vma=False,
    )
```

```python
import functools

import jax
import jax.numpy as jnp
from jax import lax
from jax.experimental import pallas as pl
from jax.experimental.pallas import tpu as pltpu
from jax.sharding import PartitionSpec as P

QUERY_HEADS = 32
KEY_VALUE_HEADS = 4
HEAD_SIZE = 128
CYCLE_STEPS = 2
GROUP = QUERY_HEADS // KEY_VALUE_HEADS
KEY_WIDTH = KEY_VALUE_HEADS * HEAD_SIZE
LANES = 128

norm_eps = 1e-06
VMEM_LIMIT = 12 * 1024 * 1024


def params(**kw):
    return pltpu.CompilerParams(vmem_limit_bytes=VMEM_LIMIT, **kw)


def iota(shape, dim):
    return lax.broadcasted_iota(jnp.int32, shape, dim)


def exchange(block, mask):
    n = lax.axis_size("slot")
    return lax.ppermute(block, "slot", [(i, i ^ mask) for i in range(n)])


def gather(block, phases):
    held = [([0], block)]
    for phase in phases:
        merged = block if len(held) == 1 else jnp.concatenate([b for _, b in held], axis=0)
        names = [m for n, _ in held for m in n]
        if phase == phases[-1]:
            core = phase[0]
            for some in [[0, 3], [2], [1]]:
                both = [held[k] for k in some]
                away = [core ^ m for n, _ in both for m in n]
                both = [b for _, b in both]
                both = both[0] if len(both) == 1 else jnp.concatenate(both, axis=0)
                held = held + [(away, exchange(both, core))]
            return held
        if len(held) > 1:
            held = [(names, merged)]
        held = held + [([m ^ n for n in names], exchange(merged, m)) for m in phase]


def next_segment(block, mask=0):
    n, slots = lax.axis_size("segment"), lax.axis_size("slot")
    route = [(s * slots + i, (s + 1) % n * slots + (i ^ mask)) for s in range(n)
             for i in range(slots)]
    return lax.ppermute(block, ("segment", "slot"), route)


def split_rows(index, slots, batch, slot_first):
    if slot_first:
        return index // batch, lax.rem(index, batch)
    return lax.rem(index, slots), index // slots


def slot_rows_first(slots, batch):
    rows = slots * batch
    to_slot, to_row = split_rows(iota((rows, rows), 0), slots, batch, True)
    from_slot, from_row = split_rows(iota((rows, rows), 1), slots, batch, False)
    return ((to_slot == from_slot) & (to_row == from_row)).astype(jnp.bfloat16)


def arrival_rows(own, slots, batch, arrivals):
    rows = slots * batch
    to_slot, to_row = split_rows(iota((rows, rows), 0), slots, batch, False)
    arrival, from_row = split_rows(iota((rows, rows), 1), slots, batch, True)
    from_slot = jnp.zeros_like(arrival)
    for place, mask in enumerate(arrivals):
        from_slot = jnp.where(arrival == place, mask, from_slot)
    return ((to_slot == (from_slot ^ own)) & (to_row == from_row)).astype(jnp.bfloat16)


def room_for(columns):
    return -(-(columns // 2) // LANES) * LANES


def pack_kernel(dest_ref, pages_ref, x_ref, gain_ref, send_ref, x_out, gain_out):
    x_out[...] = x_ref[...]
    gain_out[...] = gain_ref[...]
    own = lax.axis_index("slot")
    slots, page_tok, wide = send_ref.shape
    kv_width = pages_ref.shape[2]
    for p in range(pages_ref.shape[0]):
        send_ref[dest_ref[own, p], :, :kv_width] = pages_ref[p]
    for j in range(slots):
        send_ref[j, :, kv_width:] = jnp.zeros((page_tok, wide - kv_width), send_ref.dtype)


def pack(pages, dest, x, gain, room):
    _, page_tok, kv_width = pages.shape
    whole = pl.BlockSpec(memory_space=pltpu.VMEM)
    scalars = pl.BlockSpec(memory_space=pltpu.SMEM)
    return pl.pallas_call(
        pack_kernel,
        out_shape=[
            jax.ShapeDtypeStruct((dest.shape[0], page_tok, kv_width + room), pages.dtype),
            jax.ShapeDtypeStruct(x.shape, x.dtype),
            jax.ShapeDtypeStruct(gain.shape, gain.dtype),
        ],
        in_specs=[scalars] + [whole] * 3,
        out_specs=[whole] * 3,
        compiler_params=params(),
        name="pack",
    )(dest, pages, x, gain)


def project_kernel(w_ref, *refs, away, rows, carried, first, last, packed, batch):
    refs = list(refs)
    own = lax.axis_index("slot")
    x_refs = [refs.pop(0) for _ in away]
    kept = None if carried else refs.pop(0)
    acc_in, square_in = (None, None) if first else (refs.pop(0), refs.pop(0))
    if packed:
        refs.pop(0)
    if carried:
        kept = refs.pop(0)
    blocks, width = len(away[0]), x_refs[0].shape[1]
    columns, model_width = w_ref.shape
    acc = jnp.zeros((rows, columns), jnp.float32) if first else acc_in[...]
    square = jnp.zeros((rows, LANES), jnp.float32) if first else square_in[...]
    for g, masks in enumerate(away):
        if carried:
            kept[g] = x_refs[g][blocks * rows:]
        gains = kept[g].astype(jnp.float32)
        for i in range(blocks):
            x = x_refs[g][i * rows:(i + 1) * rows]
            gain = gains[i:i + 1]
            parts = []
            for r in range(0, width, LANES):
                part = x[:, r:r + LANES].astype(jnp.float32)
                square = square + part * part
                parts.append((part * gain[:, r:r + LANES]).astype(jnp.bfloat16))
            x = parts[0] if len(parts) == 1 else jnp.concatenate(parts, axis=1)
            here = pl.ds(pl.multiple_of((own ^ masks[i]) * width, width), width)
            acc = acc + lax.dot_general(x, w_ref[:, here], (((1,), (1,)), ((), ())),
                                        preferred_element_type=jnp.float32)
    if not last:
        refs[0][...] = acc
        refs[1][...] = square
        return
    sums = jnp.sum(square, axis=1, keepdims=True)
    out = (acc * lax.rsqrt(sums / model_width + norm_eps)).astype(jnp.bfloat16)
    slots = rows // batch
    out = jnp.dot(slot_rows_first(slots, batch), out, preferred_element_type=jnp.float32)
    half = columns // 2
    for j in range(slots):
        mine = out[j * batch:(j + 1) * batch]
        if packed:
            at = refs[0].shape[2] - room_for(columns)
            mine = jnp.concatenate([mine[:, :half], mine[:, half:]], axis=0)
            refs[0][j, :, at:at + half] = mine.astype(jnp.bfloat16)
        else:
            refs[0][j] = mine.astype(jnp.bfloat16)


def project(rows, batch, weight, groups, gains, state, last=False, outgoing=None):
    blocks, (held, width) = len(groups[0][0]), groups[0][1].shape
    columns = weight.shape[0]
    carried, first, packed = gains is None, state is None, outgoing is not None
    operands = [weight] + [x for _, x in groups] + ([] if carried else [gains])
    operands += [] if first else list(state)
    aliases = {}
    out_shape = []
    if carried:
        out_shape.append(jax.ShapeDtypeStruct((len(groups), held - blocks * rows, width),
                                              jnp.bfloat16))
    if packed:
        aliases = {len(operands): len(out_shape)}
        operands.append(outgoing)
        out_shape.append(jax.ShapeDtypeStruct(outgoing.shape, outgoing.dtype))
    elif last:
        out_shape.append(jax.ShapeDtypeStruct((rows // batch, batch, columns), jnp.bfloat16))
    else:
        out_shape += [jax.ShapeDtypeStruct((rows, columns), jnp.float32),
                      jax.ShapeDtypeStruct((rows, LANES), jnp.float32)]
    whole = pl.BlockSpec(memory_space=pltpu.VMEM)
    work = rows * width * columns * blocks * len(groups)
    out = pl.pallas_call(
        functools.partial(project_kernel, away=[masks for masks, _ in groups], rows=rows,
                          carried=carried, first=first, last=last, packed=packed, batch=batch),
        out_shape=out_shape,
        in_specs=[whole] * len(operands),
        out_specs=[whole] * len(out_shape),
        input_output_aliases=aliases,
        compiler_params=params(),
        cost_estimate=pl.CostEstimate(flops=8 * work, bytes_accessed=2 * work // rows,
                                      transcendentals=0),
        name="project",
    )(*operands)
    if carried:
        gains, *out = out
    return gains, (out[0] if last else out)


def token_rows(own, dest_ref, row_ref, count_ref, page_tok):
    slots = dest_ref.shape[0]
    tokens = slots * page_tok
    mine = dest_ref[...] == own
    spread = (iota((slots, tokens), 1) // page_tok == iota((slots, tokens), 0)).astype(jnp.float32)

    def to_tokens(values):
        kept = jnp.where(mine, values, 0).astype(jnp.float32)
        by_token = lax.dot_general(kept, spread, (((0,), (0,)), ((), ())),
                                   preferred_element_type=jnp.float32)
        return jnp.sum(by_token, axis=0, keepdims=True)

    place = lax.rem(iota((1, tokens), 1), page_tok).astype(jnp.float32)
    live = place < to_tokens(count_ref[...])
    return jnp.where(live, to_tokens(row_ref[...]), -1.0).astype(jnp.int32)


def attend_kernel(len_ref, qkv_ref, cache_ref, pages_ref, dest_ref, page_row_ref, count_ref,
                  out_ref, *, visit, columns, packed):
    slots = qkv_ref.shape[0]
    batch, positions = cache_ref.shape[1:3]
    tokens = pages_ref.shape[0]
    pieces = []
    for j in range(slots):
        if packed:
            half = columns // 2
            piece = qkv_ref[j, :, qkv_ref.shape[2] - room_for(columns):].astype(jnp.float32)
            pieces += [piece[:batch, :half], piece[batch:2 * batch, :half]]
        else:
            pieces.append(qkv_ref[j].astype(jnp.float32))
    full = jnp.concatenate(pieces, axis=1)
    group_rows = GROUP * batch
    near = batch * positions
    near_pad = -(-(near + 16) // LANES) * LANES
    rows = KEY_VALUE_HEADS * group_rows
    nt = (((1,), (1,)), ((), ()))
    far_scores, near_scores, near_values = [], [], []
    key_at = QUERY_HEADS * HEAD_SIZE
    value_at = key_at + KEY_WIDTH
    for h in range(KEY_VALUE_HEADS):
        query = jnp.concatenate(
            [full[:, (h * GROUP + g) * HEAD_SIZE:(h * GROUP + g + 1) * HEAD_SIZE]
             for g in range(GROUP)], axis=0).astype(jnp.bfloat16)
        lo, hi = h * HEAD_SIZE, (h + 1) * HEAD_SIZE

        def nearby(cache_lo, fresh_lo):
            fresh = full[:, fresh_lo:fresh_lo + HEAD_SIZE]
            fresh = jnp.concatenate(
                [fresh, jnp.zeros((near_pad - near - batch, HEAD_SIZE), jnp.float32)], axis=0)
            old = [cache_ref[visit, b, :, cache_lo:cache_lo + HEAD_SIZE] for b in range(batch)]
            return jnp.concatenate(old + [fresh.astype(jnp.bfloat16)], axis=0)

        keys = nearby(lo, key_at + lo)
        near_values.append(nearby(KEY_WIDTH + lo, value_at + lo))
        far_scores.append(lax.dot_general(query, pages_ref[:, lo:hi], nt,
                                          preferred_element_type=jnp.float32))
        near_scores.append(lax.dot_general(query, keys, nt, preferred_element_type=jnp.float32))
    scale = HEAD_SIZE ** (-0.5)
    far = jnp.concatenate(far_scores, axis=0) * scale
    close = jnp.concatenate(near_scores, axis=0) * scale
    far_row = lax.rem(iota((rows, tokens), 0), batch)
    code = token_rows(lax.axis_index("slot"), dest_ref, page_row_ref, count_ref, tokens // slots)
    far = jnp.where(code == far_row + visit * batch, far, -1e30)
    row = lax.rem(iota((rows, near_pad), 0), batch)
    lane = iota((rows, near_pad), 1)
    lengths = jnp.zeros((rows, near_pad), jnp.int32)
    for b in range(batch):
        lengths = jnp.where(row == b, len_ref[visit:visit + 1, b:b + 1], lengths)
    position = lane - row * positions
    seen = (position >= 0) & (position < lengths) | (lane == near + row)
    close = jnp.where(seen, close, -1e30)
    top = jnp.maximum(jnp.max(far, axis=1, keepdims=True), jnp.max(close, axis=1, keepdims=True))
    far = jnp.exp(far - top)
    close = jnp.exp(close - top)
    denominator = jnp.sum(far, axis=1, keepdims=True) + jnp.sum(close, axis=1, keepdims=True)
    far = (far / denominator).astype(jnp.bfloat16)
    close = (close / denominator).astype(jnp.bfloat16)
    for h in range(KEY_VALUE_HEADS):
        mine = slice(h * group_rows, (h + 1) * group_rows)
        lo = KEY_WIDTH + h * HEAD_SIZE
        context = jnp.dot(far[mine], pages_ref[:, lo:lo + HEAD_SIZE],
                          preferred_element_type=jnp.float32)
        context = context + jnp.dot(close[mine], near_values[h],
                                    preferred_element_type=jnp.float32)
        for g in range(GROUP):
            at = (h * GROUP + g) * HEAD_SIZE
            out_ref[0, :, at:at + HEAD_SIZE] = context[g * batch:(g + 1) * batch].astype(
                jnp.bfloat16)


def attend(lengths, qkv, columns, cache, pages, arrivals, visit):
    batch = cache.shape[1]
    whole = pl.BlockSpec(memory_space=pltpu.VMEM)
    operands = [lengths, qkv, cache, pages, *arrivals]
    return pl.pallas_call(
        functools.partial(attend_kernel, visit=visit, columns=columns,
                          packed=qkv.shape[2] != columns),
        out_shape=jax.ShapeDtypeStruct((1, batch, QUERY_HEADS * HEAD_SIZE), jnp.bfloat16),
        in_specs=[whole] * len(operands),
        out_specs=whole,
        compiler_params=params(),
        name="attend",
    )(*operands)


def output_kernel(*refs, slots, batch, arrivals):
    pieces, (w_ref, now_ref, out_ref) = refs[:-3], refs[-3:]
    features = w_ref.shape[0]
    depth = features // 4
    acc = jnp.zeros(out_ref.shape, jnp.float32)
    for k in range(0, features, depth):
        left = jnp.concatenate(
            [piece[i, :, k:k + depth].astype(jnp.float32)
             for piece in pieces for i in range(piece.shape[0])], axis=0)
        acc = acc + jnp.dot(left.astype(jnp.bfloat16), w_ref[k:k + depth],
                            preferred_element_type=jnp.float32)
    move = arrival_rows(lax.axis_index("slot"), slots, batch, arrivals)
    now = lax.dot_general(move, now_ref[...], (((0,), (0,)), ((), ())),
                          preferred_element_type=jnp.float32)
    updated = (now + acc).astype(jnp.bfloat16)
    out_ref[...] = jnp.dot(move, updated, preferred_element_type=jnp.float32).astype(jnp.bfloat16)


def output(groups, weight, now, slots):
    arrivals = [m for n, _ in groups for m in n]
    pieces = [b for _, b in groups]
    batch = pieces[0].shape[1]
    whole = pl.BlockSpec(memory_space=pltpu.VMEM)
    return pl.pallas_call(
        functools.partial(output_kernel, slots=slots, batch=batch, arrivals=arrivals),
        out_shape=jax.ShapeDtypeStruct(now.shape, jnp.bfloat16),
        in_specs=[whole] * (len(pieces) + 2),
        out_specs=whole,
        compiler_params=params(),
        name="output",
    )(*pieces, weight, now)


def shards(hidden_rows, norm_gain, qkv_weight, out_weight, cache_kv, cache_len, page_kv,
           page_dest, page_row, page_count):
    slots = lax.axis_size("slot")
    batch = hidden_rows.shape[1]
    rows = batch * slots
    width = hidden_rows.shape[3]
    kv_width = cache_kv.shape[5]
    masks = [slots >> (k + 1) for k in range(slots.bit_length() - 1)]
    across, over, core = masks[-3:]
    phases = [[mask] for mask in masks[:-3]] + [[across, over, across ^ over], [core]]
    offsets = [masks[0], 0]
    for mask in masks[1:]:
        offsets = offsets + [mask ^ o for o in offsets]
    cache = cache_kv[0, :, :, 0]
    lengths = cache_len[0, :, :, 0]
    weight_in = qkv_weight[0].T
    weight_out = out_weight[0]
    current = hidden_rows.reshape(rows, width)
    columns = weight_in.shape[0]
    arrivals = (page_dest[0], page_row[0], page_count[0])
    gains = [None] * 5
    for visit in range(CYCLE_STEPS):
        if visit == 0:
            block, gain = exchange(current, masks[0]), exchange(norm_gain, masks[0])
            outgoing, current, mine = pack(page_kv[0, 0], page_dest[0], current, norm_gain,
                                           room_for(columns))
            block, gain = jnp.concatenate([block, current]), jnp.concatenate([gain, mine])
        else:
            block = jnp.concatenate([beyond, current])
        for mask in masks[1:-3]:
            block = jnp.concatenate([block, exchange(block, mask)])
            if visit == 0:
                gain = jnp.concatenate([gain, exchange(gain, mask)])
        if visit == 0:
            spare = jnp.zeros((-gain.shape[0] % 16, width), gain.dtype)
            block = jnp.concatenate([block, gain, spare])
        size = slots // 8
        away = [offsets[g * size:(g + 1) * size] for g in range(8)]
        run = functools.partial(project, rows, batch, weight_in)
        second = exchange(block, across)
        third = exchange(block, over)
        pair = exchange(block, core)
        fourth = exchange(second, over)
        gains[0], state = run([(away[0], block), (away[4], pair)], gains[0], None)
        gains[1], state = run([(away[1], second), (away[2], third)], gains[1], state)
        second, third, state = lax.optimization_barrier((second, third, state))
        others = [exchange(x, core) for x in (second, third)]
        fourth, state = lax.optimization_barrier((fourth, state))
        corner = exchange(fourth, core)
        gains[3], state = run([(away[3], fourth), *zip(away[5:7], others)], gains[3], state)
        gains[4], qkv = run([(away[7], corner)], gains[4], state, last=True,
                             outgoing=None if visit else outgoing)
        qkv = lax.all_to_all(qkv, "slot", split_axis=0, concat_axis=0, tiled=True)
        if visit == 0:
            pages = qkv.reshape(-1, qkv.shape[2])
        context = attend(lengths, qkv, columns, cache, pages, arrivals, visit)
        groups = gather(context, phases)
        updated = output(groups, weight_out, current, slots)
        current = next_segment(updated)
        if visit < CYCLE_STEPS - 1:
            beyond = next_segment(updated, masks[0])
    return current.reshape(hidden_rows.shape)


def solution(mesh):
    return jax.shard_map(
        shards,
        mesh=mesh,
        in_specs=(
            P("segment", None, None, "slot"),
            P("segment", "slot"),
            P("segment", None, "slot"),
            P("segment", None, "slot"),
            P("segment", None, None, "slot", None, None),
            P("segment", None, None, "slot"),
            P("segment", "slot", None, None, None),
            P("segment", None, None),
            P("segment", None, None),
            P("segment", None, None),
        ),
        out_specs=P("segment", None, None, "slot"),
        check_vma=False,
    )
```

```python
import functools

import jax
import jax.numpy as jnp
from jax import lax
from jax.experimental import pallas as pl
from jax.experimental.pallas import tpu as pltpu
from jax.sharding import PartitionSpec as P

QUERY_HEADS = 32
KEY_VALUE_HEADS = 4
HEAD_SIZE = 128
CYCLE_STEPS = 2
GROUP = QUERY_HEADS // KEY_VALUE_HEADS
KEY_WIDTH = KEY_VALUE_HEADS * HEAD_SIZE
LANES = 128

norm_eps = 1e-06
VMEM_LIMIT = 12 * 1024 * 1024


def params(**kw):
    return pltpu.CompilerParams(vmem_limit_bytes=VMEM_LIMIT, **kw)


def iota(shape, dim):
    return lax.broadcasted_iota(jnp.int32, shape, dim)


def exchange(block, mask):
    n = lax.axis_size("slot")
    return lax.ppermute(block, "slot", [(i, i ^ mask) for i in range(n)])


def gather(block, phases):
    held = [([0], block)]
    for phase in phases:
        merged = block if len(held) == 1 else jnp.concatenate([b for _, b in held], axis=0)
        names = [m for n, _ in held for m in n]
        if phase == phases[-1]:
            core = phase[0]
            for some in [[0, 3], [2], [1]]:
                both = [held[k] for k in some]
                away = [core ^ m for n, _ in both for m in n]
                both = [b for _, b in both]
                both = both[0] if len(both) == 1 else jnp.concatenate(both, axis=0)
                held = held + [(away, exchange(both, core))]
            return held
        if len(held) > 1:
            held = [(names, merged)]
        held = held + [([m ^ n for n in names], exchange(merged, m)) for m in phase]


def next_segment(block, mask=0):
    n, slots = lax.axis_size("segment"), lax.axis_size("slot")
    route = [(s * slots + i, (s + 1) % n * slots + (i ^ mask)) for s in range(n)
             for i in range(slots)]
    return lax.ppermute(block, ("segment", "slot"), route)


def split_rows(index, slots, batch, slot_first):
    if slot_first:
        return index // batch, lax.rem(index, batch)
    return lax.rem(index, slots), index // slots


def slot_rows_first(slots, batch):
    rows = slots * batch
    to_slot, to_row = split_rows(iota((rows, rows), 0), slots, batch, True)
    from_slot, from_row = split_rows(iota((rows, rows), 1), slots, batch, False)
    return ((to_slot == from_slot) & (to_row == from_row)).astype(jnp.bfloat16)


def arrival_rows(own, slots, batch, arrivals):
    rows = slots * batch
    to_slot, to_row = split_rows(iota((rows, rows), 0), slots, batch, False)
    arrival, from_row = split_rows(iota((rows, rows), 1), slots, batch, True)
    from_slot = jnp.zeros_like(arrival)
    for place, mask in enumerate(arrivals):
        from_slot = jnp.where(arrival == place, mask, from_slot)
    return ((to_slot == (from_slot ^ own)) & (to_row == from_row)).astype(jnp.bfloat16)


def room_for(columns):
    return -(-(columns // 2) // LANES) * LANES


def pack_kernel(dest_ref, pages_ref, x_ref, gain_ref, send_ref, x_out, gain_out):
    x_out[...] = x_ref[...]
    gain_out[...] = gain_ref[...]
    own = lax.axis_index("slot")
    slots, page_tok, wide = send_ref.shape
    kv_width = pages_ref.shape[2]
    for p in range(pages_ref.shape[0]):
        send_ref[dest_ref[own, p], :, :kv_width] = pages_ref[p]
    for j in range(slots):
        send_ref[j, :, kv_width:] = jnp.zeros((page_tok, wide - kv_width), send_ref.dtype)


def pack(pages, dest, x, gain, room):
    _, page_tok, kv_width = pages.shape
    whole = pl.BlockSpec(memory_space=pltpu.VMEM)
    scalars = pl.BlockSpec(memory_space=pltpu.SMEM)
    return pl.pallas_call(
        pack_kernel,
        out_shape=[
            jax.ShapeDtypeStruct((dest.shape[0], page_tok, kv_width + room), pages.dtype),
            jax.ShapeDtypeStruct(x.shape, x.dtype),
            jax.ShapeDtypeStruct(gain.shape, gain.dtype),
        ],
        in_specs=[scalars] + [whole] * 3,
        out_specs=[whole] * 3,
        compiler_params=params(),
        name="pack",
    )(dest, pages, x, gain)


def project_kernel(w_ref, *refs, away, rows, carried, first, last, packed, batch):
    refs = list(refs)
    own = lax.axis_index("slot")
    x_refs = [refs.pop(0) for _ in away]
    kept = None if carried else refs.pop(0)
    acc_in, square_in = (None, None) if first else (refs.pop(0), refs.pop(0))
    pages_ref = refs.pop(0) if packed else None
    if carried:
        kept = refs.pop(0)
    blocks, width = len(away[0]), x_refs[0].shape[1]
    columns, model_width = w_ref.shape
    acc = jnp.zeros((rows, columns), jnp.float32) if first else acc_in[...]
    square = jnp.zeros((rows, LANES), jnp.float32) if first else square_in[...]
    for g, masks in enumerate(away):
        if carried:
            kept[g] = x_refs[g][blocks * rows:]
        gains = kept[g].astype(jnp.float32)
        for i in range(blocks):
            x = x_refs[g][i * rows:(i + 1) * rows]
            gain = gains[i:i + 1]
            parts = []
            for r in range(0, width, LANES):
                part = x[:, r:r + LANES].astype(jnp.float32)
                square = square + part * part
                parts.append((part * gain[:, r:r + LANES]).astype(jnp.bfloat16))
            x = parts[0] if len(parts) == 1 else jnp.concatenate(parts, axis=1)
            here = pl.ds(pl.multiple_of((own ^ masks[i]) * width, width), width)
            acc = acc + lax.dot_general(x, w_ref[:, here], (((1,), (1,)), ((), ())),
                                        preferred_element_type=jnp.float32)
    if not last:
        refs[0][...] = acc
        refs[1][...] = square
        return
    sums = jnp.sum(square, axis=1, keepdims=True)
    out = (acc * lax.rsqrt(sums / model_width + norm_eps)).astype(jnp.bfloat16)
    slots = rows // batch
    out = jnp.dot(slot_rows_first(slots, batch), out, preferred_element_type=jnp.float32)
    half = columns // 2
    for j in range(slots):
        mine = out[j * batch:(j + 1) * batch]
        if packed:
            at = refs[0].shape[2] - room_for(columns)
            mine = jnp.concatenate([mine[:, :half], mine[:, half:]], axis=0)
            refs[0][j] = pages_ref[j]
            refs[0][j, :, at:at + half] = mine.astype(jnp.bfloat16)
        else:
            refs[0][j] = mine.astype(jnp.bfloat16)


def project(rows, batch, weight, groups, gains, state, last=False, outgoing=None):
    blocks, (held, width) = len(groups[0][0]), groups[0][1].shape
    columns = weight.shape[0]
    carried, first, packed = gains is None, state is None, outgoing is not None
    operands = [weight] + [x for _, x in groups] + ([] if carried else [gains])
    operands += [] if first else list(state)
    out_shape = []
    if carried:
        out_shape.append(jax.ShapeDtypeStruct((len(groups), held - blocks * rows, width),
                                              jnp.bfloat16))
    if packed:
        operands.append(outgoing)
        out_shape.append(jax.ShapeDtypeStruct(outgoing.shape, outgoing.dtype))
    elif last:
        out_shape.append(jax.ShapeDtypeStruct((rows // batch, batch, columns), jnp.bfloat16))
    else:
        out_shape += [jax.ShapeDtypeStruct((rows, columns), jnp.float32),
                      jax.ShapeDtypeStruct((rows, LANES), jnp.float32)]
    whole = pl.BlockSpec(memory_space=pltpu.VMEM)
    work = rows * width * columns * blocks * len(groups)
    out = pl.pallas_call(
        functools.partial(project_kernel, away=[masks for masks, _ in groups], rows=rows,
                          carried=carried, first=first, last=last, packed=packed, batch=batch),
        out_shape=out_shape,
        in_specs=[whole] * len(operands),
        out_specs=[whole] * len(out_shape),
        compiler_params=params(),
        cost_estimate=pl.CostEstimate(flops=8 * work, bytes_accessed=2 * work // rows,
                                      transcendentals=0),
        name="project",
    )(*operands)
    if carried:
        gains, *out = out
    return gains, (out[0] if last else out)


def token_rows(own, dest_ref, row_ref, count_ref, page_tok):
    slots = dest_ref.shape[0]
    tokens = slots * page_tok
    mine = dest_ref[...] == own
    spread = (iota((slots, tokens), 1) // page_tok == iota((slots, tokens), 0)).astype(jnp.float32)

    def to_tokens(values):
        kept = jnp.where(mine, values, 0).astype(jnp.float32)
        by_token = lax.dot_general(kept, spread, (((0,), (0,)), ((), ())),
                                   preferred_element_type=jnp.float32)
        return jnp.sum(by_token, axis=0, keepdims=True)

    place = lax.rem(iota((1, tokens), 1), page_tok).astype(jnp.float32)
    live = place < to_tokens(count_ref[...])
    return jnp.where(live, to_tokens(row_ref[...]), -1.0).astype(jnp.int32)


def attend_kernel(len_ref, qkv_ref, cache_ref, pages_ref, dest_ref, page_row_ref, count_ref,
                  out_ref, *, visit, columns, packed):
    slots = qkv_ref.shape[0]
    batch, positions = cache_ref.shape[1:3]
    tokens = pages_ref.shape[0]
    pieces = []
    for j in range(slots):
        if packed:
            half = columns // 2
            piece = qkv_ref[j, :, qkv_ref.shape[2] - room_for(columns):].astype(jnp.float32)
            pieces += [piece[:batch, :half], piece[batch:2 * batch, :half]]
        else:
            pieces.append(qkv_ref[j].astype(jnp.float32))
    full = jnp.concatenate(pieces, axis=1)
    group_rows = GROUP * batch
    near = batch * positions
    near_pad = -(-(near + 16) // LANES) * LANES
    rows = KEY_VALUE_HEADS * group_rows
    nt = (((1,), (1,)), ((), ()))
    far_scores, near_scores, near_values = [], [], []
    key_at = QUERY_HEADS * HEAD_SIZE
    value_at = key_at + KEY_WIDTH
    for h in range(KEY_VALUE_HEADS):
        query = jnp.concatenate(
            [full[:, (h * GROUP + g) * HEAD_SIZE:(h * GROUP + g + 1) * HEAD_SIZE]
             for g in range(GROUP)], axis=0).astype(jnp.bfloat16)
        lo, hi = h * HEAD_SIZE, (h + 1) * HEAD_SIZE

        def nearby(cache_lo, fresh_lo):
            fresh = full[:, fresh_lo:fresh_lo + HEAD_SIZE]
            fresh = jnp.concatenate(
                [fresh, jnp.zeros((near_pad - near - batch, HEAD_SIZE), jnp.float32)], axis=0)
            old = [cache_ref[visit, b, :, cache_lo:cache_lo + HEAD_SIZE] for b in range(batch)]
            return jnp.concatenate(old + [fresh.astype(jnp.bfloat16)], axis=0)

        keys = nearby(lo, key_at + lo)
        near_values.append(nearby(KEY_WIDTH + lo, value_at + lo))
        far_scores.append(lax.dot_general(query, pages_ref[:, lo:hi], nt,
                                          preferred_element_type=jnp.float32))
        near_scores.append(lax.dot_general(query, keys, nt, preferred_element_type=jnp.float32))
    scale = HEAD_SIZE ** (-0.5)
    far = jnp.concatenate(far_scores, axis=0) * scale
    close = jnp.concatenate(near_scores, axis=0) * scale
    far_row = lax.rem(iota((rows, tokens), 0), batch)
    code = token_rows(lax.axis_index("slot"), dest_ref, page_row_ref, count_ref, tokens // slots)
    far = jnp.where(code == far_row + visit * batch, far, -1e30)
    row = lax.rem(iota((rows, near_pad), 0), batch)
    lane = iota((rows, near_pad), 1)
    lengths = jnp.zeros((rows, near_pad), jnp.int32)
    for b in range(batch):
        lengths = jnp.where(row == b, len_ref[visit:visit + 1, b:b + 1], lengths)
    position = lane - row * positions
    seen = (position >= 0) & (position < lengths) | (lane == near + row)
    close = jnp.where(seen, close, -1e30)
    top = jnp.maximum(jnp.max(far, axis=1, keepdims=True), jnp.max(close, axis=1, keepdims=True))
    far = jnp.exp(far - top)
    close = jnp.exp(close - top)
    denominator = jnp.sum(far, axis=1, keepdims=True) + jnp.sum(close, axis=1, keepdims=True)
    far = (far / denominator).astype(jnp.bfloat16)
    close = (close / denominator).astype(jnp.bfloat16)
    for h in range(KEY_VALUE_HEADS):
        mine = slice(h * group_rows, (h + 1) * group_rows)
        lo = KEY_WIDTH + h * HEAD_SIZE
        context = jnp.dot(far[mine], pages_ref[:, lo:lo + HEAD_SIZE],
                          preferred_element_type=jnp.float32)
        context = context + jnp.dot(close[mine], near_values[h],
                                    preferred_element_type=jnp.float32)
        for g in range(GROUP):
            at = (h * GROUP + g) * HEAD_SIZE
            out_ref[0, :, at:at + HEAD_SIZE] = context[g * batch:(g + 1) * batch].astype(
                jnp.bfloat16)


def attend(lengths, qkv, columns, cache, pages, arrivals, visit):
    batch = cache.shape[1]
    whole = pl.BlockSpec(memory_space=pltpu.VMEM)
    operands = [lengths, qkv, cache, pages, *arrivals]
    return pl.pallas_call(
        functools.partial(attend_kernel, visit=visit, columns=columns,
                          packed=qkv.shape[2] != columns),
        out_shape=jax.ShapeDtypeStruct((1, batch, QUERY_HEADS * HEAD_SIZE), jnp.bfloat16),
        in_specs=[whole] * len(operands),
        out_specs=whole,
        compiler_params=params(),
        name="attend",
    )(*operands)


def output_kernel(*refs, slots, batch, arrivals):
    pieces, (w_ref, now_ref, out_ref) = refs[:-3], refs[-3:]
    features = w_ref.shape[0]
    depth = features // 4
    acc = jnp.zeros(out_ref.shape, jnp.float32)
    for k in range(0, features, depth):
        left = jnp.concatenate(
            [piece[i, :, k:k + depth].astype(jnp.float32)
             for piece in pieces for i in range(piece.shape[0])], axis=0)
        acc = acc + jnp.dot(left.astype(jnp.bfloat16), w_ref[k:k + depth],
                            preferred_element_type=jnp.float32)
    move = arrival_rows(lax.axis_index("slot"), slots, batch, arrivals)
    now = lax.dot_general(move, now_ref[...], (((0,), (0,)), ((), ())),
                          preferred_element_type=jnp.float32)
    updated = (now + acc).astype(jnp.bfloat16)
    out_ref[...] = jnp.dot(move, updated, preferred_element_type=jnp.float32).astype(jnp.bfloat16)


def output(groups, weight, now, slots):
    arrivals = [m for n, _ in groups for m in n]
    pieces = [b for _, b in groups]
    batch = pieces[0].shape[1]
    whole = pl.BlockSpec(memory_space=pltpu.VMEM)
    return pl.pallas_call(
        functools.partial(output_kernel, slots=slots, batch=batch, arrivals=arrivals),
        out_shape=jax.ShapeDtypeStruct(now.shape, jnp.bfloat16),
        in_specs=[whole] * (len(pieces) + 2),
        out_specs=whole,
        compiler_params=params(),
        name="output",
    )(*pieces, weight, now)


def shards(hidden_rows, norm_gain, qkv_weight, out_weight, cache_kv, cache_len, page_kv,
           page_dest, page_row, page_count):
    slots = lax.axis_size("slot")
    batch = hidden_rows.shape[1]
    rows = batch * slots
    width = hidden_rows.shape[3]
    kv_width = cache_kv.shape[5]
    masks = [slots >> (k + 1) for k in range(slots.bit_length() - 1)]
    across, over, core = masks[-3:]
    phases = [[mask] for mask in masks[:-3]] + [[across, over, across ^ over], [core]]
    offsets = [masks[0], 0]
    for mask in masks[1:]:
        offsets = offsets + [mask ^ o for o in offsets]
    cache = cache_kv[0, :, :, 0]
    lengths = cache_len[0, :, :, 0]
    weight_in = qkv_weight[0].T
    weight_out = out_weight[0]
    current = hidden_rows.reshape(rows, width)
    columns = weight_in.shape[0]
    arrivals = (page_dest[0], page_row[0], page_count[0])
    gains = [None] * 5
    for visit in range(CYCLE_STEPS):
        if visit == 0:
            block, gain = exchange(current, masks[0]), exchange(norm_gain, masks[0])
            outgoing, current, mine = pack(page_kv[0, 0], page_dest[0], current, norm_gain,
                                           room_for(columns))
            block, gain = jnp.concatenate([block, current]), jnp.concatenate([gain, mine])
        else:
            block = jnp.concatenate([beyond, current])
        for mask in masks[1:-3]:
            block = jnp.concatenate([block, exchange(block, mask)])
            if visit == 0:
                gain = jnp.concatenate([gain, exchange(gain, mask)])
        if visit == 0:
            spare = jnp.zeros((-gain.shape[0] % 16, width), gain.dtype)
            block = jnp.concatenate([block, gain, spare])
        size = slots // 8
        away = [offsets[g * size:(g + 1) * size] for g in range(8)]
        run = functools.partial(project, rows, batch, weight_in)
        second = exchange(block, across)
        third = exchange(block, over)
        pair = exchange(block, core)
        fourth = exchange(second, over)
        gains[0], state = run([(away[0], block), (away[4], pair)], gains[0], None)
        gains[1], state = run([(away[1], second), (away[2], third)], gains[1], state)
        second, third, state = lax.optimization_barrier((second, third, state))
        others = [exchange(x, core) for x in (second, third)]
        fourth, state = lax.optimization_barrier((fourth, state))
        corner = exchange(fourth, core)
        gains[3], state = run([(away[3], fourth), *zip(away[5:7], others)], gains[3], state)
        gains[4], qkv = run([(away[7], corner)], gains[4], state, last=True,
                             outgoing=None if visit else outgoing)
        qkv = lax.all_to_all(qkv, "slot", split_axis=0, concat_axis=0, tiled=True)
        if visit == 0:
            pages = qkv.reshape(-1, qkv.shape[2])
        context = attend(lengths, qkv, columns, cache, pages, arrivals, visit)
        groups = gather(context, phases)
        updated = output(groups, weight_out, current, slots)
        current = next_segment(updated)
        if visit < CYCLE_STEPS - 1:
            beyond = next_segment(updated, masks[0])
    return current.reshape(hidden_rows.shape)


def solution(mesh):
    return jax.shard_map(
        shards,
        mesh=mesh,
        in_specs=(
            P("segment", None, None, "slot"),
            P("segment", "slot"),
            P("segment", None, "slot"),
            P("segment", None, "slot"),
            P("segment", None, None, "slot", None, None),
            P("segment", None, None, "slot"),
            P("segment", "slot", None, None, None),
            P("segment", None, None),
            P("segment", None, None),
            P("segment", None, None),
        ),
        out_specs=P("segment", None, None, "slot"),
        check_vma=False,
    )
```

```python
import functools

import jax
import jax.numpy as jnp
from jax import lax
from jax.experimental import pallas as pl
from jax.experimental.pallas import tpu as pltpu
from jax.sharding import PartitionSpec as P

QUERY_HEADS = 32
KEY_VALUE_HEADS = 4
HEAD_SIZE = 128
CYCLE_STEPS = 2
GROUP = QUERY_HEADS // KEY_VALUE_HEADS
KEY_WIDTH = KEY_VALUE_HEADS * HEAD_SIZE
LANES = 128

norm_eps = 1e-06
VMEM_LIMIT = 12 * 1024 * 1024


def params(**kw):
    return pltpu.CompilerParams(vmem_limit_bytes=VMEM_LIMIT, **kw)


def iota(shape, dim):
    return lax.broadcasted_iota(jnp.int32, shape, dim)


def exchange(block, mask):
    n = lax.axis_size("slot")
    return lax.ppermute(block, "slot", [(i, i ^ mask) for i in range(n)])


def gather(block, phases):
    core = phases[-1][0]
    names, merged, crossed = [0], block, exchange(block, core)
    for phase in phases[:-2]:
        arrived = exchange(merged, phase[0])
        if merged is block:
            arrived, crossed = lax.optimization_barrier((arrived, crossed))
        names = names + [m ^ phase[0] for m in names]
        merged = jnp.concatenate([merged, arrived], axis=0)
    held = [(names, merged)]
    held += [([m ^ n for n in names], exchange(merged, m)) for m in phases[-2]]
    across = [([core], crossed)]
    for some in [[0, 3], [2], [1]]:
        away = [m ^ core for k in some for m in held[k][0]]
        parts = [held[k][1] for k in some]
        if 0 in some:
            away, parts[0] = away[1:], parts[0][1:]
        parts = parts[0] if len(parts) == 1 else jnp.concatenate(parts, axis=0)
        across.append((away, exchange(parts, core)))
    return held + across


def next_segment(block, mask=0):
    n, slots = lax.axis_size("segment"), lax.axis_size("slot")
    route = [(s * slots + i, (s + 1) % n * slots + (i ^ mask)) for s in range(n)
             for i in range(slots)]
    return lax.ppermute(block, ("segment", "slot"), route)


def split_rows(index, slots, batch, slot_first):
    if slot_first:
        return index // batch, lax.rem(index, batch)
    return lax.rem(index, slots), index // slots


def slot_rows_first(slots, batch):
    rows = slots * batch
    to_slot, to_row = split_rows(iota((rows, rows), 0), slots, batch, True)
    from_slot, from_row = split_rows(iota((rows, rows), 1), slots, batch, False)
    return ((to_slot == from_slot) & (to_row == from_row)).astype(jnp.bfloat16)


def arrival_rows(own, slots, batch, arrivals):
    rows = slots * batch
    to_slot, to_row = split_rows(iota((rows, rows), 0), slots, batch, False)
    arrival, from_row = split_rows(iota((rows, rows), 1), slots, batch, True)
    from_slot = jnp.zeros_like(arrival)
    for place, mask in enumerate(arrivals):
        from_slot = jnp.where(arrival == place, mask, from_slot)
    return ((to_slot == (from_slot ^ own)) & (to_row == from_row)).astype(jnp.bfloat16)


def room_for(columns):
    return -(-(columns // 2) // LANES) * LANES


def pack_kernel(dest_ref, pages_ref, x_ref, gain_ref, send_ref, x_out, gain_out):
    x_out[...] = x_ref[...]
    gain_out[...] = gain_ref[...]
    own = lax.axis_index("slot")
    slots, page_tok, wide = send_ref.shape
    kv_width = pages_ref.shape[2]
    for p in range(pages_ref.shape[0]):
        send_ref[dest_ref[own, p], :, :kv_width] = pages_ref[p]
    for j in range(slots):
        send_ref[j, :, kv_width:] = jnp.zeros((page_tok, wide - kv_width), send_ref.dtype)


def pack(pages, dest, x, gain, room):
    _, page_tok, kv_width = pages.shape
    whole = pl.BlockSpec(memory_space=pltpu.VMEM)
    scalars = pl.BlockSpec(memory_space=pltpu.SMEM)
    return pl.pallas_call(
        pack_kernel,
        out_shape=[
            jax.ShapeDtypeStruct((dest.shape[0], page_tok, kv_width + room), pages.dtype),
            jax.ShapeDtypeStruct(x.shape, x.dtype),
            jax.ShapeDtypeStruct(gain.shape, gain.dtype),
        ],
        in_specs=[scalars] + [whole] * 3,
        out_specs=[whole] * 3,
        compiler_params=params(),
        name="pack",
    )(dest, pages, x, gain)


def project_kernel(w_ref, *refs, away, rows, carried, first, last, packed, batch):
    refs = list(refs)
    own = lax.axis_index("slot")
    x_refs = [refs.pop(0) for _ in away]
    kept = None if carried else refs.pop(0)
    acc_in, square_in = (None, None) if first else (refs.pop(0), refs.pop(0))
    pages_ref = refs.pop(0) if packed else None
    if carried:
        kept = refs.pop(0)
    blocks, width = len(away[0]), x_refs[0].shape[1]
    columns, model_width = w_ref.shape
    acc = jnp.zeros((rows, columns), jnp.float32) if first else acc_in[...]
    square = jnp.zeros((rows, LANES), jnp.float32) if first else square_in[...]
    for g, masks in enumerate(away):
        if carried:
            kept[g] = x_refs[g][blocks * rows:]
        gains = kept[g].astype(jnp.float32)
        for i in range(blocks):
            x = x_refs[g][i * rows:(i + 1) * rows]
            gain = gains[i:i + 1]
            parts = []
            for r in range(0, width, LANES):
                part = x[:, r:r + LANES].astype(jnp.float32)
                square = square + part * part
                parts.append((part * gain[:, r:r + LANES]).astype(jnp.bfloat16))
            x = parts[0] if len(parts) == 1 else jnp.concatenate(parts, axis=1)
            here = pl.ds(pl.multiple_of((own ^ masks[i]) * width, width), width)
            acc = acc + lax.dot_general(x, w_ref[:, here], (((1,), (1,)), ((), ())),
                                        preferred_element_type=jnp.float32)
    if not last:
        refs[0][...] = acc
        refs[1][...] = square
        return
    sums = jnp.sum(square, axis=1, keepdims=True)
    out = (acc * lax.rsqrt(sums / model_width + norm_eps)).astype(jnp.bfloat16)
    slots = rows // batch
    out = jnp.dot(slot_rows_first(slots, batch), out, preferred_element_type=jnp.float32)
    half = columns // 2
    for j in range(slots):
        mine = out[j * batch:(j + 1) * batch]
        if packed:
            at = refs[0].shape[2] - room_for(columns)
            mine = jnp.concatenate([mine[:, :half], mine[:, half:]], axis=0)
            refs[0][j] = pages_ref[j]
            refs[0][j, :, at:at + half] = mine.astype(jnp.bfloat16)
        else:
            refs[0][j] = mine.astype(jnp.bfloat16)


def project(rows, batch, weight, groups, gains, state, last=False, outgoing=None):
    blocks, (held, width) = len(groups[0][0]), groups[0][1].shape
    columns = weight.shape[0]
    carried, first, packed = gains is None, state is None, outgoing is not None
    operands = [weight] + [x for _, x in groups] + ([] if carried else [gains])
    operands += [] if first else list(state)
    out_shape = []
    if carried:
        out_shape.append(jax.ShapeDtypeStruct((len(groups), held - blocks * rows, width),
                                              jnp.bfloat16))
    if packed:
        operands.append(outgoing)
        out_shape.append(jax.ShapeDtypeStruct(outgoing.shape, outgoing.dtype))
    elif last:
        out_shape.append(jax.ShapeDtypeStruct((rows // batch, batch, columns), jnp.bfloat16))
    else:
        out_shape += [jax.ShapeDtypeStruct((rows, columns), jnp.float32),
                      jax.ShapeDtypeStruct((rows, LANES), jnp.float32)]
    whole = pl.BlockSpec(memory_space=pltpu.VMEM)
    work = rows * width * columns * blocks * len(groups)
    out = pl.pallas_call(
        functools.partial(project_kernel, away=[masks for masks, _ in groups], rows=rows,
                          carried=carried, first=first, last=last, packed=packed, batch=batch),
        out_shape=out_shape,
        in_specs=[whole] * len(operands),
        out_specs=[whole] * len(out_shape),
        compiler_params=params(),
        cost_estimate=pl.CostEstimate(flops=8 * work, bytes_accessed=2 * work // rows,
                                      transcendentals=0),
        name="project",
    )(*operands)
    if carried:
        gains, *out = out
    return gains, (out[0] if last else out)


def token_rows(own, dest_ref, row_ref, count_ref, page_tok):
    slots = dest_ref.shape[0]
    tokens = slots * page_tok
    mine = dest_ref[...] == own
    spread = (iota((slots, tokens), 1) // page_tok == iota((slots, tokens), 0)).astype(jnp.float32)

    def to_tokens(values):
        kept = jnp.where(mine, values, 0).astype(jnp.float32)
        by_token = lax.dot_general(kept, spread, (((0,), (0,)), ((), ())),
                                   preferred_element_type=jnp.float32)
        return jnp.sum(by_token, axis=0, keepdims=True)

    place = lax.rem(iota((1, tokens), 1), page_tok).astype(jnp.float32)
    live = place < to_tokens(count_ref[...])
    return jnp.where(live, to_tokens(row_ref[...]), -1.0).astype(jnp.int32)


def attend_kernel(len_ref, qkv_ref, cache_ref, pages_ref, dest_ref, page_row_ref, count_ref,
                  out_ref, *, visit, columns, packed):
    slots = qkv_ref.shape[0]
    batch, positions = cache_ref.shape[1:3]
    tokens = pages_ref.shape[0]
    pieces = []
    for j in range(slots):
        if packed:
            half = columns // 2
            piece = qkv_ref[j, :, qkv_ref.shape[2] - room_for(columns):].astype(jnp.float32)
            pieces += [piece[:batch, :half], piece[batch:2 * batch, :half]]
        else:
            pieces.append(qkv_ref[j].astype(jnp.float32))
    full = jnp.concatenate(pieces, axis=1)
    group_rows = GROUP * batch
    near = batch * positions
    near_pad = -(-(near + 16) // LANES) * LANES
    rows = KEY_VALUE_HEADS * group_rows
    nt = (((1,), (1,)), ((), ()))
    far_scores, near_scores, near_values = [], [], []
    key_at = QUERY_HEADS * HEAD_SIZE
    value_at = key_at + KEY_WIDTH
    for h in range(KEY_VALUE_HEADS):
        query = jnp.concatenate(
            [full[:, (h * GROUP + g) * HEAD_SIZE:(h * GROUP + g + 1) * HEAD_SIZE]
             for g in range(GROUP)], axis=0).astype(jnp.bfloat16)
        lo, hi = h * HEAD_SIZE, (h + 1) * HEAD_SIZE

        def nearby(cache_lo, fresh_lo):
            fresh = full[:, fresh_lo:fresh_lo + HEAD_SIZE]
            fresh = jnp.concatenate(
                [fresh, jnp.zeros((near_pad - near - batch, HEAD_SIZE), jnp.float32)], axis=0)
            old = [cache_ref[visit, b, :, cache_lo:cache_lo + HEAD_SIZE] for b in range(batch)]
            return jnp.concatenate(old + [fresh.astype(jnp.bfloat16)], axis=0)

        keys = nearby(lo, key_at + lo)
        near_values.append(nearby(KEY_WIDTH + lo, value_at + lo))
        far_scores.append(lax.dot_general(query, pages_ref[:, lo:hi], nt,
                                          preferred_element_type=jnp.float32))
        near_scores.append(lax.dot_general(query, keys, nt, preferred_element_type=jnp.float32))
    scale = HEAD_SIZE ** (-0.5)
    far = jnp.concatenate(far_scores, axis=0) * scale
    close = jnp.concatenate(near_scores, axis=0) * scale
    far_row = lax.rem(iota((rows, tokens), 0), batch)
    code = token_rows(lax.axis_index("slot"), dest_ref, page_row_ref, count_ref, tokens // slots)
    far = jnp.where(code == far_row + visit * batch, far, -1e30)
    row = lax.rem(iota((rows, near_pad), 0), batch)
    lane = iota((rows, near_pad), 1)
    lengths = jnp.zeros((rows, near_pad), jnp.int32)
    for b in range(batch):
        lengths = jnp.where(row == b, len_ref[visit:visit + 1, b:b + 1], lengths)
    position = lane - row * positions
    seen = (position >= 0) & (position < lengths) | (lane == near + row)
    close = jnp.where(seen, close, -1e30)
    top = jnp.maximum(jnp.max(far, axis=1, keepdims=True), jnp.max(close, axis=1, keepdims=True))
    far = jnp.exp(far - top)
    close = jnp.exp(close - top)
    denominator = jnp.sum(far, axis=1, keepdims=True) + jnp.sum(close, axis=1, keepdims=True)
    far = (far / denominator).astype(jnp.bfloat16)
    close = (close / denominator).astype(jnp.bfloat16)
    for h in range(KEY_VALUE_HEADS):
        mine = slice(h * group_rows, (h + 1) * group_rows)
        lo = KEY_WIDTH + h * HEAD_SIZE
        context = jnp.dot(far[mine], pages_ref[:, lo:lo + HEAD_SIZE],
                          preferred_element_type=jnp.float32)
        context = context + jnp.dot(close[mine], near_values[h],
                                    preferred_element_type=jnp.float32)
        for g in range(GROUP):
            at = (h * GROUP + g) * HEAD_SIZE
            out_ref[0, :, at:at + HEAD_SIZE] = context[g * batch:(g + 1) * batch].astype(
                jnp.bfloat16)


def attend(lengths, qkv, columns, cache, pages, arrivals, visit):
    batch = cache.shape[1]
    whole = pl.BlockSpec(memory_space=pltpu.VMEM)
    operands = [lengths, qkv, cache, pages, *arrivals]
    return pl.pallas_call(
        functools.partial(attend_kernel, visit=visit, columns=columns,
                          packed=qkv.shape[2] != columns),
        out_shape=jax.ShapeDtypeStruct((1, batch, QUERY_HEADS * HEAD_SIZE), jnp.bfloat16),
        in_specs=[whole] * len(operands),
        out_specs=whole,
        compiler_params=params(),
        name="attend",
    )(*operands)


def output_kernel(*refs, slots, batch, arrivals):
    pieces, (w_ref, now_ref, out_ref) = refs[:-3], refs[-3:]
    features = w_ref.shape[0]
    depth = features // 4
    acc = jnp.zeros(out_ref.shape, jnp.float32)
    for k in range(0, features, depth):
        left = jnp.concatenate(
            [piece[i, :, k:k + depth].astype(jnp.float32)
             for piece in pieces for i in range(piece.shape[0])], axis=0)
        acc = acc + jnp.dot(left.astype(jnp.bfloat16), w_ref[k:k + depth],
                            preferred_element_type=jnp.float32)
    move = arrival_rows(lax.axis_index("slot"), slots, batch, arrivals)
    now = lax.dot_general(move, now_ref[...], (((0,), (0,)), ((), ())),
                          preferred_element_type=jnp.float32)
    updated = (now + acc).astype(jnp.bfloat16)
    out_ref[...] = jnp.dot(move, updated, preferred_element_type=jnp.float32).astype(jnp.bfloat16)


def output(groups, weight, now, slots):
    arrivals = [m for n, _ in groups for m in n]
    pieces = [b for _, b in groups]
    batch = pieces[0].shape[1]
    whole = pl.BlockSpec(memory_space=pltpu.VMEM)
    return pl.pallas_call(
        functools.partial(output_kernel, slots=slots, batch=batch, arrivals=arrivals),
        out_shape=jax.ShapeDtypeStruct(now.shape, jnp.bfloat16),
        in_specs=[whole] * (len(pieces) + 2),
        out_specs=whole,
        compiler_params=params(),
        name="output",
    )(*pieces, weight, now)


def shards(hidden_rows, norm_gain, qkv_weight, out_weight, cache_kv, cache_len, page_kv,
           page_dest, page_row, page_count):
    slots = lax.axis_size("slot")
    batch = hidden_rows.shape[1]
    rows = batch * slots
    width = hidden_rows.shape[3]
    kv_width = cache_kv.shape[5]
    masks = [slots >> (k + 1) for k in range(slots.bit_length() - 1)]
    across, over, core = masks[-3:]
    phases = [[mask] for mask in masks[:-3]] + [[across, over, across ^ over], [core]]
    offsets = [masks[0], 0]
    for mask in masks[1:]:
        offsets = offsets + [mask ^ o for o in offsets]
    cache = cache_kv[0, :, :, 0]
    lengths = cache_len[0, :, :, 0]
    weight_in = qkv_weight[0].T
    weight_out = out_weight[0]
    current = hidden_rows.reshape(rows, width)
    columns = weight_in.shape[0]
    arrivals = (page_dest[0], page_row[0], page_count[0])
    gains = [None] * 5
    for visit in range(CYCLE_STEPS):
        if visit == 0:
            block, gain = exchange(current, masks[0]), exchange(norm_gain, masks[0])
            outgoing, current, mine = pack(page_kv[0, 0], page_dest[0], current, norm_gain,
                                           room_for(columns))
            block, gain = jnp.concatenate([block, current]), jnp.concatenate([gain, mine])
        else:
            block = jnp.concatenate([beyond, current])
        for mask in masks[1:-3]:
            block = jnp.concatenate([block, exchange(block, mask)])
            if visit == 0:
                gain = jnp.concatenate([gain, exchange(gain, mask)])
        if visit == 0:
            spare = jnp.zeros((-gain.shape[0] % 16, width), gain.dtype)
            block = jnp.concatenate([block, gain, spare])
        size = slots // 8
        away = [offsets[g * size:(g + 1) * size] for g in range(8)]
        run = functools.partial(project, rows, batch, weight_in)
        second = exchange(block, across)
        third = exchange(block, over)
        pair = exchange(block, core)
        fourth = exchange(second, over)
        gains[0], state = run([(away[0], block), (away[4], pair)], gains[0], None)
        gains[1], state = run([(away[1], second), (away[2], third)], gains[1], state)
        second, third, state = lax.optimization_barrier((second, third, state))
        others = [exchange(x, core) for x in (second, third)]
        fourth, state = lax.optimization_barrier((fourth, state))
        corner = exchange(fourth, core)
        gains[3], state = run([(away[3], fourth), *zip(away[5:7], others)], gains[3], state)
        gains[4], qkv = run([(away[7], corner)], gains[4], state, last=True,
                             outgoing=None if visit else outgoing)
        qkv = lax.all_to_all(qkv, "slot", split_axis=0, concat_axis=0, tiled=True)
        if visit == 0:
            pages = qkv.reshape(-1, qkv.shape[2])
        context = attend(lengths, qkv, columns, cache, pages, arrivals, visit)
        groups = gather(context, phases)
        updated = output(groups, weight_out, current, slots)
        current = next_segment(updated)
        if visit < CYCLE_STEPS - 1:
            beyond = next_segment(updated, masks[0])
    return current.reshape(hidden_rows.shape)


def solution(mesh):
    return jax.shard_map(
        shards,
        mesh=mesh,
        in_specs=(
            P("segment", None, None, "slot"),
            P("segment", "slot"),
            P("segment", None, "slot"),
            P("segment", None, "slot"),
            P("segment", None, None, "slot", None, None),
            P("segment", None, None, "slot"),
            P("segment", "slot", None, None, None),
            P("segment", None, None),
            P("segment", None, None),
            P("segment", None, None),
        ),
        out_specs=P("segment", None, None, "slot"),
        check_vma=False,
    )
```

```python
import functools

import jax
import jax.numpy as jnp
from jax import lax
from jax.experimental import pallas as pl
from jax.experimental.pallas import tpu as pltpu
from jax.sharding import PartitionSpec as P

QUERY_HEADS = 32
KEY_VALUE_HEADS = 4
HEAD_SIZE = 128
CYCLE_STEPS = 2
GROUP = QUERY_HEADS // KEY_VALUE_HEADS
KEY_WIDTH = KEY_VALUE_HEADS * HEAD_SIZE
LANES = 128

norm_eps = 1e-06
VMEM_LIMIT = 12 * 1024 * 1024


def params(**kw):
    return pltpu.CompilerParams(vmem_limit_bytes=VMEM_LIMIT, **kw)


def iota(shape, dim):
    return lax.broadcasted_iota(jnp.int32, shape, dim)


def exchange(block, mask):
    n = lax.axis_size("slot")
    return lax.ppermute(block, "slot", [(i, i ^ mask) for i in range(n)])


def gather(block, phases):
    held = [([0], block)]
    for phase in phases:
        merged = block if len(held) == 1 else jnp.concatenate([b for _, b in held], axis=0)
        names = [m for n, _ in held for m in n]
        if phase == phases[-1]:
            core = phase[0]
            for some in [[0, 3], [2], [1]]:
                both = [held[k] for k in some]
                away = [core ^ m for n, _ in both for m in n]
                both = [b for _, b in both]
                both = both[0] if len(both) == 1 else jnp.concatenate(both, axis=0)
                held = held + [(away, exchange(both, core))]
            return held
        if len(held) > 1:
            held = [(names, merged)]
        held = held + [([m ^ n for n in names], exchange(merged, m)) for m in phase]


def next_segment(block, mask=0):
    n, slots = lax.axis_size("segment"), lax.axis_size("slot")
    route = [(s * slots + i, (s + 1) % n * slots + (i ^ mask)) for s in range(n)
             for i in range(slots)]
    return lax.ppermute(block, ("segment", "slot"), route)


def split_rows(index, slots, batch, slot_first):
    if slot_first:
        return index // batch, lax.rem(index, batch)
    return lax.rem(index, slots), index // slots


def slot_rows_first(slots, batch):
    rows = slots * batch
    to_slot, to_row = split_rows(iota((rows, rows), 0), slots, batch, True)
    from_slot, from_row = split_rows(iota((rows, rows), 1), slots, batch, False)
    return ((to_slot == from_slot) & (to_row == from_row)).astype(jnp.bfloat16)


def arrival_rows(own, slots, batch, arrivals):
    rows = slots * batch
    to_slot, to_row = split_rows(iota((rows, rows), 0), slots, batch, False)
    arrival, from_row = split_rows(iota((rows, rows), 1), slots, batch, True)
    from_slot = jnp.zeros_like(arrival)
    for place, mask in enumerate(arrivals):
        from_slot = jnp.where(arrival == place, mask, from_slot)
    return ((to_slot == (from_slot ^ own)) & (to_row == from_row)).astype(jnp.bfloat16)


def room_for(columns):
    return -(-(columns // 2) // LANES) * LANES


def pack_kernel(dest_ref, pages_ref, x_ref, gain_ref, send_ref, x_out, gain_out):
    x_out[...] = x_ref[...]
    gain_out[...] = gain_ref[...]
    own = lax.axis_index("slot")
    slots, page_tok, wide = send_ref.shape
    kv_width = pages_ref.shape[2]
    for p in range(pages_ref.shape[0]):
        send_ref[dest_ref[own, p], :, :kv_width] = pages_ref[p]
    for j in range(slots):
        send_ref[j, :, kv_width:] = jnp.zeros((page_tok, wide - kv_width), send_ref.dtype)


def pack(pages, dest, x, gain, room):
    _, page_tok, kv_width = pages.shape
    whole = pl.BlockSpec(memory_space=pltpu.VMEM)
    scalars = pl.BlockSpec(memory_space=pltpu.SMEM)
    return pl.pallas_call(
        pack_kernel,
        out_shape=[
            jax.ShapeDtypeStruct((dest.shape[0], page_tok, kv_width + room), pages.dtype),
            jax.ShapeDtypeStruct(x.shape, x.dtype),
            jax.ShapeDtypeStruct(gain.shape, gain.dtype),
        ],
        in_specs=[scalars] + [whole] * 3,
        out_specs=[whole] * 3,
        compiler_params=params(),
        name="pack",
    )(dest, pages, x, gain)


def project_kernel(w_ref, *refs, away, rows, carried, first, last, packed, batch):
    refs = list(refs)
    own = lax.axis_index("slot")
    x_refs = [refs.pop(0) for _ in away]
    kept = None if carried else refs.pop(0)
    acc_in, square_in = (None, None) if first else (refs.pop(0), refs.pop(0))
    pages_ref = refs.pop(0) if packed else None
    if carried:
        kept = refs.pop(0)
    blocks, width = len(away[0]), x_refs[0].shape[1]
    columns, model_width = w_ref.shape
    acc = jnp.zeros((rows, columns), jnp.float32) if first else acc_in[...]
    square = jnp.zeros((rows, LANES), jnp.float32) if first else square_in[...]
    for g, masks in enumerate(away):
        if carried:
            kept[g] = x_refs[g][blocks * rows:]
        gains = kept[g].astype(jnp.float32)
        for i in range(blocks):
            x = x_refs[g][i * rows:(i + 1) * rows]
            gain = gains[i:i + 1]
            parts = []
            for r in range(0, width, LANES):
                part = x[:, r:r + LANES].astype(jnp.float32)
                square = square + part * part
                parts.append((part * gain[:, r:r + LANES]).astype(jnp.bfloat16))
            x = parts[0] if len(parts) == 1 else jnp.concatenate(parts, axis=1)
            here = pl.ds(pl.multiple_of((own ^ masks[i]) * width, width), width)
            acc = acc + lax.dot_general(x, w_ref[:, here], (((1,), (1,)), ((), ())),
                                        preferred_element_type=jnp.float32)
    if not last:
        refs[0][...] = acc
        refs[1][...] = square
        return
    sums = jnp.sum(square, axis=1, keepdims=True)
    out = (acc * lax.rsqrt(sums / model_width + norm_eps)).astype(jnp.bfloat16)
    slots = rows // batch
    out = jnp.dot(slot_rows_first(slots, batch), out, preferred_element_type=jnp.float32)
    half = columns // 2
    for j in range(slots):
        mine = out[j * batch:(j + 1) * batch]
        if packed:
            at = refs[0].shape[2] - room_for(columns)
            mine = jnp.concatenate([mine[:, :half], mine[:, half:]], axis=0)
            refs[0][j] = pages_ref[j]
            refs[0][j, :, at:at + half] = mine.astype(jnp.bfloat16)
        else:
            refs[0][j] = mine.astype(jnp.bfloat16)


def project(rows, batch, weight, groups, gains, state, last=False, outgoing=None):
    blocks, (held, width) = len(groups[0][0]), groups[0][1].shape
    columns = weight.shape[0]
    carried, first, packed = gains is None, state is None, outgoing is not None
    operands = [weight] + [x for _, x in groups] + ([] if carried else [gains])
    operands += [] if first else list(state)
    out_shape = []
    if carried:
        out_shape.append(jax.ShapeDtypeStruct((len(groups), held - blocks * rows, width),
                                              jnp.bfloat16))
    if packed:
        operands.append(outgoing)
        out_shape.append(jax.ShapeDtypeStruct(outgoing.shape, outgoing.dtype))
    elif last:
        out_shape.append(jax.ShapeDtypeStruct((rows // batch, batch, columns), jnp.bfloat16))
    else:
        out_shape += [jax.ShapeDtypeStruct((rows, columns), jnp.float32),
                      jax.ShapeDtypeStruct((rows, LANES), jnp.float32)]
    whole = pl.BlockSpec(memory_space=pltpu.VMEM)
    work = rows * width * columns * blocks * len(groups)
    out = pl.pallas_call(
        functools.partial(project_kernel, away=[masks for masks, _ in groups], rows=rows,
                          carried=carried, first=first, last=last, packed=packed, batch=batch),
        out_shape=out_shape,
        in_specs=[whole] * len(operands),
        out_specs=[whole] * len(out_shape),
        compiler_params=params(),
        cost_estimate=pl.CostEstimate(flops=8 * work, bytes_accessed=2 * work // rows,
                                      transcendentals=0),
        name="project",
    )(*operands)
    if carried:
        gains, *out = out
    return gains, (out[0] if last else out)


def token_rows(own, dest_ref, row_ref, count_ref, page_tok):
    slots = dest_ref.shape[0]
    tokens = slots * page_tok
    mine = dest_ref[...] == own
    spread = (iota((slots, tokens), 1) // page_tok == iota((slots, tokens), 0)).astype(jnp.float32)

    def to_tokens(values):
        kept = jnp.where(mine, values, 0).astype(jnp.float32)
        by_token = lax.dot_general(kept, spread, (((0,), (0,)), ((), ())),
                                   preferred_element_type=jnp.float32)
        return jnp.sum(by_token, axis=0, keepdims=True)

    place = lax.rem(iota((1, tokens), 1), page_tok).astype(jnp.float32)
    live = place < to_tokens(count_ref[...])
    return jnp.where(live, to_tokens(row_ref[...]), -1.0).astype(jnp.int32)


def attend_kernel(len_ref, qkv_ref, cache_ref, pages_ref, dest_ref, page_row_ref, count_ref,
                  out_ref, *, visit, columns, packed):
    slots = qkv_ref.shape[0]
    batch, positions = cache_ref.shape[1:3]
    tokens = pages_ref.shape[0]
    pieces = []
    for j in range(slots):
        if packed:
            half = columns // 2
            piece = qkv_ref[j, :, qkv_ref.shape[2] - room_for(columns):].astype(jnp.float32)
            pieces += [piece[:batch, :half], piece[batch:2 * batch, :half]]
        else:
            pieces.append(qkv_ref[j].astype(jnp.float32))
    full = jnp.concatenate(pieces, axis=1)
    group_rows = GROUP * batch
    near = batch * positions
    near_pad = -(-(near + 16) // LANES) * LANES
    rows = KEY_VALUE_HEADS * group_rows
    nt = (((1,), (1,)), ((), ()))
    far_scores, near_scores, near_values = [], [], []
    key_at = QUERY_HEADS * HEAD_SIZE
    value_at = key_at + KEY_WIDTH
    for h in range(KEY_VALUE_HEADS):
        query = jnp.concatenate(
            [full[:, (h * GROUP + g) * HEAD_SIZE:(h * GROUP + g + 1) * HEAD_SIZE]
             for g in range(GROUP)], axis=0).astype(jnp.bfloat16)
        lo, hi = h * HEAD_SIZE, (h + 1) * HEAD_SIZE

        def nearby(cache_lo, fresh_lo):
            fresh = full[:, fresh_lo:fresh_lo + HEAD_SIZE]
            fresh = jnp.concatenate(
                [fresh, jnp.zeros((near_pad - near - batch, HEAD_SIZE), jnp.float32)], axis=0)
            old = [cache_ref[visit, b, :, cache_lo:cache_lo + HEAD_SIZE] for b in range(batch)]
            return jnp.concatenate(old + [fresh.astype(jnp.bfloat16)], axis=0)

        keys = nearby(lo, key_at + lo)
        near_values.append(nearby(KEY_WIDTH + lo, value_at + lo))
        far_scores.append(lax.dot_general(query, pages_ref[:, lo:hi], nt,
                                          preferred_element_type=jnp.float32))
        near_scores.append(lax.dot_general(query, keys, nt, preferred_element_type=jnp.float32))
    scale = HEAD_SIZE ** (-0.5)
    far = jnp.concatenate(far_scores, axis=0) * scale
    close = jnp.concatenate(near_scores, axis=0) * scale
    far_row = lax.rem(iota((rows, tokens), 0), batch)
    code = token_rows(lax.axis_index("slot"), dest_ref, page_row_ref, count_ref, tokens // slots)
    far = jnp.where(code == far_row + visit * batch, far, -1e30)
    row = lax.rem(iota((rows, near_pad), 0), batch)
    lane = iota((rows, near_pad), 1)
    lengths = jnp.zeros((rows, near_pad), jnp.int32)
    for b in range(batch):
        lengths = jnp.where(row == b, len_ref[visit:visit + 1, b:b + 1], lengths)
    position = lane - row * positions
    seen = (position >= 0) & (position < lengths) | (lane == near + row)
    close = jnp.where(seen, close, -1e30)
    top = jnp.maximum(jnp.max(far, axis=1, keepdims=True), jnp.max(close, axis=1, keepdims=True))
    far = jnp.exp(far - top)
    close = jnp.exp(close - top)
    denominator = jnp.sum(far, axis=1, keepdims=True) + jnp.sum(close, axis=1, keepdims=True)
    far = (far / denominator).astype(jnp.bfloat16)
    close = (close / denominator).astype(jnp.bfloat16)
    for h in range(KEY_VALUE_HEADS):
        mine = slice(h * group_rows, (h + 1) * group_rows)
        lo = KEY_WIDTH + h * HEAD_SIZE
        context = jnp.dot(far[mine], pages_ref[:, lo:lo + HEAD_SIZE],
                          preferred_element_type=jnp.float32)
        context = context + jnp.dot(close[mine], near_values[h],
                                    preferred_element_type=jnp.float32)
        for g in range(GROUP):
            at = (h * GROUP + g) * HEAD_SIZE
            out_ref[0, :, at:at + HEAD_SIZE] = context[g * batch:(g + 1) * batch].astype(
                jnp.bfloat16)


def attend(lengths, qkv, columns, cache, pages, arrivals, visit):
    batch = cache.shape[1]
    whole = pl.BlockSpec(memory_space=pltpu.VMEM)
    operands = [lengths, qkv, cache, pages, *arrivals]
    return pl.pallas_call(
        functools.partial(attend_kernel, visit=visit, columns=columns,
                          packed=qkv.shape[2] != columns),
        out_shape=jax.ShapeDtypeStruct((1, batch, QUERY_HEADS * HEAD_SIZE), jnp.bfloat16),
        in_specs=[whole] * len(operands),
        out_specs=whole,
        compiler_params=params(),
        name="attend",
    )(*operands)


def output_kernel(*refs, slots, batch, arrivals):
    pieces, (w_ref, now_ref, out_ref) = refs[:-3], refs[-3:]
    features = w_ref.shape[0]
    depth = features // 4
    acc = jnp.zeros(out_ref.shape, jnp.float32)
    for k in range(0, features, depth):
        left = jnp.concatenate(
            [piece[i, :, k:k + depth].astype(jnp.float32)
             for piece in pieces for i in range(piece.shape[0])], axis=0)
        acc = acc + jnp.dot(left.astype(jnp.bfloat16), w_ref[k:k + depth],
                            preferred_element_type=jnp.float32)
    move = arrival_rows(lax.axis_index("slot"), slots, batch, arrivals)
    now = lax.dot_general(move, now_ref[...], (((0,), (0,)), ((), ())),
                          preferred_element_type=jnp.float32)
    updated = (now + acc).astype(jnp.bfloat16)
    out_ref[...] = jnp.dot(move, updated, preferred_element_type=jnp.float32).astype(jnp.bfloat16)


def output(groups, weight, now, slots):
    arrivals = [m for n, _ in groups for m in n]
    pieces = [b for _, b in groups]
    batch = pieces[0].shape[1]
    whole = pl.BlockSpec(memory_space=pltpu.VMEM)
    return pl.pallas_call(
        functools.partial(output_kernel, slots=slots, batch=batch, arrivals=arrivals),
        out_shape=jax.ShapeDtypeStruct(now.shape, jnp.bfloat16),
        in_specs=[whole] * (len(pieces) + 2),
        out_specs=whole,
        compiler_params=params(),
        name="output",
    )(*pieces, weight, now)


def shards(hidden_rows, norm_gain, qkv_weight, out_weight, cache_kv, cache_len, page_kv,
           page_dest, page_row, page_count):
    slots = lax.axis_size("slot")
    batch = hidden_rows.shape[1]
    rows = batch * slots
    width = hidden_rows.shape[3]
    kv_width = cache_kv.shape[5]
    masks = [slots >> (k + 1) for k in range(slots.bit_length() - 1)]
    across, over, core = masks[-3:]
    phases = [[mask] for mask in masks[:-3]] + [[across, over, across ^ over], [core]]
    offsets = [masks[0], 0]
    for mask in masks[1:]:
        offsets = offsets + [mask ^ o for o in offsets]
    cache = cache_kv[0, :, :, 0]
    lengths = cache_len[0, :, :, 0]
    weight_in = qkv_weight[0].T
    weight_out = out_weight[0]
    current = hidden_rows.reshape(rows, width)
    columns = weight_in.shape[0]
    arrivals = (page_dest[0], page_row[0], page_count[0])
    gains = [None] * 5
    for visit in range(CYCLE_STEPS):
        if visit == 0:
            block, gain = exchange(current, masks[0]), exchange(norm_gain, masks[0])
            outgoing, current, mine = pack(page_kv[0, 0], page_dest[0], current, norm_gain,
                                           room_for(columns))
            block, gain = jnp.concatenate([block, current]), jnp.concatenate([gain, mine])
        else:
            block = jnp.concatenate([beyond, current])
        for mask in masks[1:-3]:
            block = jnp.concatenate([block, exchange(block, mask)])
            if visit == 0:
                gain = jnp.concatenate([gain, exchange(gain, mask)])
        if visit == 0:
            spare = jnp.zeros((-gain.shape[0] % 16, width), gain.dtype)
            block = jnp.concatenate([block, gain, spare])
        size = slots // 8
        away = [offsets[g * size:(g + 1) * size] for g in range(8)]
        run = functools.partial(project, rows, batch, weight_in)
        second = exchange(block, across)
        third = exchange(block, over)
        pair = exchange(block, core)
        fourth = exchange(second, over)
        gains[0], state = run([(away[0], block), (away[4], pair)], gains[0], None)
        gains[1], state = run([(away[1], second), (away[2], third)], gains[1], state)
        second, third, state = lax.optimization_barrier((second, third, state))
        others = [exchange(x, core) for x in (second, third)]
        gains[2], state = run(list(zip(away[5:7], others)), gains[2], state)
        corner = exchange(fourth, core)
        gains[3], state = run([(away[3], fourth)], gains[3], state)
        gains[4], qkv = run([(away[7], corner)], gains[4], state, last=True,
                             outgoing=None if visit else outgoing)
        qkv = lax.all_to_all(qkv, "slot", split_axis=0, concat_axis=0, tiled=True)
        if visit == 0:
            pages = qkv.reshape(-1, qkv.shape[2])
        context = attend(lengths, qkv, columns, cache, pages, arrivals, visit)
        groups = gather(context, phases)
        updated = output(groups, weight_out, current, slots)
        current = next_segment(updated)
        if visit < CYCLE_STEPS - 1:
            beyond = next_segment(updated, masks[0])
    return current.reshape(hidden_rows.shape)


def solution(mesh):
    return jax.shard_map(
        shards,
        mesh=mesh,
        in_specs=(
            P("segment", None, None, "slot"),
            P("segment", "slot"),
            P("segment", None, "slot"),
            P("segment", None, "slot"),
            P("segment", None, None, "slot", None, None),
            P("segment", None, None, "slot"),
            P("segment", "slot", None, None, None),
            P("segment", None, None),
            P("segment", None, None),
            P("segment", None, None),
        ),
        out_specs=P("segment", None, None, "slot"),
        check_vma=False,
    )
```
